32 devices in a mesh: expert: 8 (over z, x), tensor: 4 (over y, core).
Axes of the slice: x: 2, y: 2, z: 4, core: 2. Of those that a mesh axis runs over, the one named last changes fastest.
Arguments:
- tokens: bfloat16 [2048, 1024], P('expert'), may hold values from -6 to 6
- cotangent: bfloat16 [2048, 1024], P('expert'), may hold values from -6 to 6
- segments: int32 [8, 256], P('expert'), may hold values from 0 to 2, never falling along the last dimension, each value on 1 to 128 neighbouring positions
- routes: int32 [2048, 8], P('expert'), may hold values from 0 to 31, all different within a row; in each aligned block of 64 rows (0 to 63, 64 to 127, ...) at most 32 rows name the same one
- gates: float32 [2048, 8], P('expert'), may hold values from 0.06 to 0.19
- w_query: float32 [1024, 1024], P('expert', 'tensor'), may hold values from -0.1875 to 0.1875
- key_projection: float32 [1024, 512], P('expert', 'tensor'), may hold values from -0.1875 to 0.1875
- value_projection: float32 [1024, 512], P('expert', 'tensor'), may hold values from -0.1875 to 0.1875
- w_out: float32 [1024, 1024], P('tensor', 'expert'), may hold values from -0.75 to 0.75
- gain_attn: float32 [1024], P('expert'), may hold values from 0.1 to 1.9
- gain_moe: float32 [1024], P('expert'), may hold values from 0.1 to 1.9
- w_gate: float32 [32, 1024, 512], P(None, 'expert', 'tensor'), may hold values from -0.1875 to 0.1875
- w_up: float32 [32, 1024, 512], P(None, 'expert', 'tensor'), may hold values from -0.1875 to 0.1875
- w_down: float32 [32, 512, 1024], P(None, 'tensor', 'expert'), may hold values from -0.75 to 0.75
Outputs:
- output: bfloat16 [2048, 1024], P('expert')
- grad_tokens: float32 [2048, 1024], P('expert')
- grad_query: float32 [1024, 1024], P('expert', 'tensor')
- grad_key: float32 [1024, 512], P('expert', 'tensor')
- grad_value: float32 [1024, 512], P('expert', 'tensor')
- grad_out: float32 [1024, 1024], P('tensor', 'expert')
- grad_gain_attn: float32 [1024], P('expert')
- grad_gain_moe: float32 [1024], P('expert')
- grad_gate: float32 [32, 1024, 512], P(None, 'expert', 'tensor')
- grad_up: float32 [32, 1024, 512], P(None, 'expert', 'tensor')
- grad_down: float32 [32, 512, 1024], P(None, 'tensor', 'expert')
The draws below stay inside these ranges and needn't reach their ends.
Inputs may be any that keep to these rules, and one draw needn't show every extreme that they name: Within each row of segments the document numbers never fall; each document holds 1 to 128 tokens and one holds exactly 128. `routes`: each row names 8 different experts. In each aligned block of 64 rows no expert is named by more than 32 rows, and in at least one block some expert is named by exactly 32 rows.
All inputs are finite; a program needn't handle non-finite values.
Results may differ from the reference program's by a relative error of at most 0.012.
The reference program's roundings to bfloat16 on the way count: a program that leaves them out, or rounds other values in their place, can miss the bound.
Values may be sent and summed in bfloat16 or wider, within the bound.
No kernel may reach another device: no remote copies, remote signals or barrier semaphores. Data moves between devices by JAX's collectives and lax.ppermute only.
A program may use at most 256 MiB of HBM per device.

```python
import math
import jax
import jax.numpy as jnp
import numpy as np
from jax import lax

MODEL_WIDTH = 1024
QUERY_HEADS = 16
KEY_VALUE_HEADS = 8
HEAD_SIZE = 64
FF = 512
EXPERTS = 32
TOP = 8
TOK_DEV = 256
GROUPS = 4
GROUP_TOKENS = 64
MOST = 32
DOCS = 3
DOC_MOST = 128
TOKENS = 2048
N_EXPERT = 8
N_TENSOR = 4


def with_spikes(array, key, source, target, blocks, factor):
    def block_of(dim):
        return (jnp.arange(array.shape[dim]) // (array.shape[dim] // blocks)).reshape((-1,) + (1,) * (array.ndim - 1 - dim))

    one_side = jax.random.permutation(key, blocks)[block_of(target)]
    second = (block_of(target) + blocks // 2) % blocks
    return jnp.where((block_of(source) == one_side) | (block_of(source) == second), factor * array, array)


def shard_levels(rng, dims, pieces, low, top_value):
    def one(axis_at, parts):
        heights = jax.random.uniform(jax.random.fold_in(jax.random.fold_in(rng, 6), axis_at), (parts,), jnp.float32, low / len(pieces), top_value / len(pieces))
        return jnp.repeat(jnp.exp(heights), dims[axis_at] // parts).reshape((-1,) + (1,) * (len(dims) - axis_at - 1))

    level = one(*pieces[0])
    for cut in pieces[1:]:
        level = level * one(*cut)
    return level


def split_up(count, total, limit, slope):
    weights = [(1 << 20) // math.isqrt(rank ** slope) + 1 for rank in range(2, count + 1)]
    rest, given = total - limit - (count - 1), [1] * (count - 1)
    while rest > 0:
        movable = [i for i in range(count - 1) if given[i] < limit]
        mass, left = sum([weights[i] for i in movable]), rest
        for i in movable:
            more = min(limit - given[i], max(1, left * weights[i] // mass), rest)
            given[i] = given[i] + more
            rest = rest - more
    return np.array([limit] + given)


def uneven_parts(rng, count, total, bound, slope):
    if count == 2:
        one = jax.random.randint(rng, (), max(1, total - bound), min(bound, total - 1) + 1)
        return jnp.stack([one, total - one])
    sizes = jnp.asarray(split_up(count, total, bound, slope), jnp.int32)
    couples = (count - 1) // 2
    donor, taker = sizes[1:1 + 2 * couples:2], sizes[2:2 + 2 * couples:2]
    margin = jnp.minimum(donor - 1, bound - taker)
    passed = jax.random.randint(jax.random.fold_in(rng, 1), (couples,), 0, 1 << 20) % (margin + 1)
    sizes = sizes.at[1:1 + 2 * couples:2].set(donor - passed).at[2:2 + 2 * couples:2].set(taker + passed)
    return sizes[jax.random.permutation(jax.random.fold_in(rng, 2), count)]


def routed_block(own_key, own, number, rows, amount, top, bound, skew):
    sequence = jax.random.permutation(own_key, amount)
    crowded, usual = load_shares(amount, rows * top, bound, skew, True), load_shares(amount, rows * top, bound, skew, False)
    places = jnp.arange(amount)

    def named(tallies, offset_by):
        used = int((tallies > 0).sum())
        fixed = max(1, used // 4)
        shifted = fixed + (places - fixed + offset_by * (used - fixed)) % max(1, amount - fixed)
        return jnp.zeros((amount,), jnp.int32).at[sequence[jnp.where(places < fixed, places, shifted)]].set(jnp.asarray(tallies, jnp.int32))

    tallies = jnp.where(number % 4 == 0, named(crowded, number // 4), named(usual, number - number // 4 - 1))
    mixed = jax.random.permutation(jax.random.fold_in(own, 3), amount)
    source_of, sink = mixed[0:amount // 2 * 2:2], mixed[1:amount // 2 * 2:2]
    slack = jnp.minimum(tallies[source_of] - 1, bound - tallies[sink]) // 2
    slack = jnp.where((source_of == sequence[0]) | (sink == sequence[0]) | (tallies[sink] == 0), 0, jnp.maximum(slack, 0))
    shifted = jax.random.randint(jax.random.fold_in(own, 4), (amount // 2,), 0, 1 << 20) % (slack + 1)
    tallies = tallies.at[source_of].add(-shifted).at[sink].add(shifted)
    labels = jnp.searchsorted(jnp.cumsum(tallies), jnp.arange(rows * top), side="right").astype(jnp.int32)
    table = labels.reshape(top, rows).T
    table = table[jax.random.permutation(jax.random.fold_in(own, 1), rows)]
    offset_by = jax.random.randint(jax.random.fold_in(own, 2), (rows, 1), 0, top)
    return jnp.take_along_axis(table, (jnp.arange(top)[None, :] + offset_by) % top, axis=1)


def load_shares(amount, total, limit, slope, full):
    weights = [(1 << 20) // math.isqrt(grade ** slope) + 1 for grade in range(1, amount + 1)]
    largest = limit if full else min(limit, max(-(-total // amount), total * weights[0] // sum(weights)))
    least = 1 if total - largest >= amount - 1 else 0
    given, spare = [largest] + [least] * (amount - 1), total - largest - least * (amount - 1)
    while spare > 0:
        free = [i for i in range(1, amount) if given[i] < largest] or [i for i in range(1, amount) if given[i] < limit]
        whole, left = sum([weights[i] for i in free]), spare
        for i in free:
            extra = min(limit - given[i], max(1, left * weights[i] // whole), spare)
            given[i] = given[i] + extra
            spare = spare - extra
    return np.array(given)


def scatter_about(key, extent, deviation, limit, shards=(), held_as=jnp.bfloat16):
    array = deviation * jax.random.normal(key, extent, jnp.float32)
    if shards:
        array = array * shard_levels(key, extent, shards, -0.22, 0.18)
    return jnp.clip(array, -limit, limit).astype(held_as)


def gaussian_with(stream_key, shape, scale, reach, shards, heavy, kind=jnp.bfloat16):
    drawn = scale * jax.random.normal(stream_key, shape, jnp.float32)
    if shards:
        drawn = drawn * shard_levels(stream_key, shape, shards, -0.22, 0.18)
    return jnp.clip(with_spikes(drawn, jax.random.fold_in(stream_key, 3), *heavy), -reach, reach).astype(kind)


def setup_inputs(seed: int = 0) -> dict:
    streams_of = jax.random.split(jax.random.key(seed), 15)
    tokens = gaussian_with(streams_of[0], (TOKENS, MODEL_WIDTH), 1.0, 6.0, ((0, 8),), (0, 1, 8, 2.0))
    cotangent = gaussian_with(streams_of[1], (TOKENS, MODEL_WIDTH), 1.0, 6.0, ((0, 8),), (0, 1, 8, 2.0))
    segments = jax.vmap(lambda own: jnp.searchsorted(jnp.cumsum(uneven_parts(own, DOCS, TOK_DEV, DOC_MOST, 0)), jnp.arange(TOK_DEV), side="right"))(jax.random.split(streams_of[2], N_EXPERT)).reshape((N_EXPERT, TOK_DEV)).astype(jnp.int32)
    routes_keys = jax.random.split(jax.random.fold_in(streams_of[3], 1), TOKENS // GROUP_TOKENS)
    routes_turns = jax.random.permutation(jax.random.fold_in(streams_of[3], 3), TOKENS // GROUP_TOKENS)
    routes = jax.vmap(lambda own, number: routed_block(jax.random.fold_in(streams_of[3], 2), own, number, GROUP_TOKENS, EXPERTS, TOP, MOST, 1))(routes_keys, routes_turns).reshape((TOKENS, TOP))
    gates = jnp.clip(0.06 + 0.13 * jax.random.uniform(streams_of[4], (TOKENS, TOP), jnp.float32) ** shard_levels(streams_of[4], (TOKENS, TOP), ((0, 8),), -0.2, 0.2), 0.06, 0.19)
    w_query = scatter_about(streams_of[5], (MODEL_WIDTH, QUERY_HEADS * HEAD_SIZE), MODEL_WIDTH ** -0.5, 0.1875, ((0, 8), (1, 4)), jnp.float32)
    key_projection = scatter_about(streams_of[6], (MODEL_WIDTH, KEY_VALUE_HEADS * HEAD_SIZE), MODEL_WIDTH ** -0.5, 0.1875, ((0, 8), (1, 4)), jnp.float32)
    value_projection = scatter_about(streams_of[7], (MODEL_WIDTH, KEY_VALUE_HEADS * HEAD_SIZE), MODEL_WIDTH ** -0.5, 0.1875, ((0, 8), (1, 4)), jnp.float32)
    w_out = scatter_about(streams_of[8], (QUERY_HEADS * HEAD_SIZE, MODEL_WIDTH), (QUERY_HEADS * HEAD_SIZE // 16) ** -0.5, 0.75, ((0, 4), (1, 8)), jnp.float32)
    gain_attn = jnp.clip(1.0 + 0.18 * jax.random.normal(streams_of[9], (MODEL_WIDTH,), jnp.float32), 0.1, 1.9)
    gain_moe = jnp.clip(1.0 + 0.18 * jax.random.normal(streams_of[10], (MODEL_WIDTH,), jnp.float32), 0.1, 1.9)
    w_gate = scatter_about(streams_of[11], (EXPERTS, MODEL_WIDTH, FF), MODEL_WIDTH ** -0.5, 0.1875, ((1, 8), (2, 4)), jnp.float32)
    w_up = scatter_about(streams_of[12], (EXPERTS, MODEL_WIDTH, FF), MODEL_WIDTH ** -0.5, 0.1875, ((1, 8), (2, 4)), jnp.float32)
    w_down = scatter_about(streams_of[13], (EXPERTS, FF, MODEL_WIDTH), (FF // 8) ** -0.5, 0.75, ((1, 4), (2, 8)), jnp.float32)
    return dict(tokens=tokens, cotangent=cotangent, segments=segments, routes=routes, gates=gates, w_query=w_query, key_projection=key_projection, value_projection=value_projection, w_out=w_out, gain_attn=gain_attn, gain_moe=gain_moe, w_gate=w_gate, w_up=w_up, w_down=w_down)


@jax.custom_vjp
def lower_precision(v):
    return lax.optimization_barrier(v.astype(jnp.bfloat16)).astype(jnp.float32)

@jax.custom_vjp
def lower_backward(v):
    return v

def low_keep(v):
    return (lower_precision(v), None)

def low_pass(kept, grad):
    return (grad,)

def back_keep(v):
    return (v, None)

def back_low(kept, grad):
    return (lower_precision(grad),)
lower_precision.defvjp(low_keep, low_pass)
lower_backward.defvjp(back_keep, back_low)
EPS = 1e-06
THETA = 10000.0
MASKED = -1e+30
HIGH_PRECISION = lax.Precision.HIGHEST

def both_parts(v):
    return lower_precision(lower_backward(v))

def positions_of(documents):
    index = jnp.arange(documents.shape[0], dtype=jnp.int32)
    begins = jnp.concatenate([jnp.ones((1,), jnp.int32), (documents[1:] != documents[:-1]).astype(jnp.int32)])
    first = lax.cummax(index * begins, axis=0)
    return index - first

def rope_tables(position, width):
    half = width // 2
    freqs = THETA ** (-2.0 * jnp.arange(half, dtype=jnp.float32) / width)
    angle = position.astype(jnp.float32)[:, None] * freqs[None, :]
    return (jnp.cos(angle), jnp.sin(angle))

def rotary_apply(field, cosine_table, sine_table):
    half = field.shape[-1] // 2
    first = field[..., :half]
    second = field[..., half:]
    cosine_table = cosine_table[:, None, :]
    sine_table = sine_table[:, None, :]
    return jnp.concatenate([first * cosine_table - second * sine_table, second * cosine_table + first * sine_table], axis=-1)

def rms_norm(field, gain):
    return field * lax.rsqrt(lax.optimization_barrier(jnp.mean(field * field, axis=-1, keepdims=True)) + EPS) * gain

def attend(hidden_rows, documents, query_weight, key_matrix, value_matrix):
    sequence_length = hidden_rows.shape[0]
    cosine_table, sine_table = rope_tables(positions_of(documents), HEAD_SIZE)
    query_rows = lower_backward(jnp.dot(hidden_rows, query_weight, precision=HIGH_PRECISION)).reshape(sequence_length, QUERY_HEADS, HEAD_SIZE)
    key_rows = lower_backward(jnp.dot(hidden_rows, key_matrix, precision=HIGH_PRECISION)).reshape(sequence_length, KEY_VALUE_HEADS, HEAD_SIZE)
    value_rows = both_parts(jnp.dot(hidden_rows, value_matrix, precision=HIGH_PRECISION)).reshape(sequence_length, KEY_VALUE_HEADS, HEAD_SIZE)
    query_rows = lower_precision(rotary_apply(query_rows, cosine_table, sine_table)).reshape(sequence_length, KEY_VALUE_HEADS, QUERY_HEADS // KEY_VALUE_HEADS, HEAD_SIZE)
    key_rows = lower_precision(rotary_apply(key_rows, cosine_table, sine_table))
    scores = lower_backward(jnp.einsum('qhgd,khd->hgqk', query_rows, key_rows, precision=HIGH_PRECISION) * HEAD_SIZE ** (-0.5))
    index = jnp.arange(sequence_length)
    allowed = (index[None, :] <= index[:, None]) & (documents[None, :] == documents[:, None])
    scores = jnp.where(allowed[None, None], scores, MASKED)
    shares = lower_precision(jax.nn.softmax(scores, axis=-1))
    mixed = jnp.einsum('hgqk,khd->qhgd', shares, value_rows, precision=HIGH_PRECISION)
    return both_parts(mixed.reshape(sequence_length, QUERY_HEADS * HEAD_SIZE))

def slot_table(routes):
    flat = routes.reshape(-1)
    matches = (flat[:, None] == jnp.arange(EXPERTS, dtype=jnp.int32)[None, :]).astype(jnp.int32)
    rank = lax.optimization_barrier(jnp.sum((jnp.cumsum(matches, axis=0) - matches) * matches, axis=1))
    return (flat, rank)

def expert_layer(hidden_rows, routes, gates, gate_all, up_all, down_all):
    flat, rank = slot_table(routes)
    capacity = N_EXPERT * GROUPS * MOST
    place = flat * capacity + rank
    pairs = flat.shape[0]
    source = jnp.zeros((EXPERTS * capacity,), jnp.int32).at[place].set(jnp.arange(pairs, dtype=jnp.int32))
    filled = jnp.zeros((EXPERTS * capacity,), jnp.int32).at[place].set(1)
    source = source.reshape(EXPERTS, capacity)
    filled = filled.reshape(EXPERTS, capacity)
    quarter = FF // N_TENSOR

    def one_expert(items):
        picks, marks, gate_weight, up_weight, down_weight = items
        rows = jnp.where(marks[:, None] > 0, hidden_rows[picks // TOP], 0.0)
        total = jnp.zeros_like(rows)
        for part in range(N_TENSOR):
            window = slice(part * quarter, (part + 1) * quarter)
            part_rows = lower_backward(rows)
            gate_pre = lower_backward(jnp.dot(part_rows, gate_weight[:, window], precision=HIGH_PRECISION))
            up_pre = lower_backward(jnp.dot(part_rows, up_weight[:, window], precision=HIGH_PRECISION))
            active = lower_precision(jax.nn.silu(gate_pre) * up_pre)
            total = total + lower_precision(jnp.dot(active, down_weight[window, :], precision=HIGH_PRECISION))
        return total
    outs = lax.map(jax.checkpoint(one_expert), (source, filled, gate_all, up_all, down_all))
    pair_out = lower_backward(outs.reshape(EXPERTS * capacity, MODEL_WIDTH)[place]).reshape(-1, TOP, MODEL_WIDTH)
    return lax.optimization_barrier(jnp.sum(gates[:, :, None] * pair_out, axis=1))

def layer(inputs, w_query, key_projection, value_projection, w_out, gain_attn, gain_moe, w_gate, w_up, w_down, segments, routes, gates):
    query_weight = lower_precision(w_query)
    key_matrix = lower_precision(key_projection)
    value_matrix = lower_precision(value_projection)
    out_weight = lower_precision(w_out)
    attn_gain = lower_precision(gain_attn)
    moe_gain = lower_precision(gain_moe)
    gate_all = lower_precision(w_gate)
    up_all = lower_precision(w_up)
    down_all = lower_precision(w_down)
    hidden_rows = lower_precision(rms_norm(inputs, attn_gain))
    sequences = hidden_rows.reshape(N_EXPERT, TOK_DEV, MODEL_WIDTH)

    def one_sequence(item):
        return attend(item[0], item[1], query_weight, key_matrix, value_matrix)
    mixed = lax.map(jax.checkpoint(one_sequence), (sequences, segments))
    attention = lower_backward(jnp.dot(mixed.reshape(-1, QUERY_HEADS * HEAD_SIZE), out_weight, precision=HIGH_PRECISION))
    middle = inputs + attention
    second = lower_precision(rms_norm(middle, moe_gain))
    return middle + expert_layer(second, routes, gates, gate_all, up_all, down_all)

def reference(tokens, cotangent, segments, routes, gates, w_query, key_projection, value_projection, w_out, gain_attn, gain_moe, w_gate, w_up, w_down):

    def forward(inputs, wq_master, wk_master, wv_master, wo_master, first_gain, second_gain, gate_master, up_master, down_master):
        return layer(inputs, wq_master, wk_master, wv_master, wo_master, first_gain, second_gain, gate_master, up_master, down_master, segments, routes, gates)
    output, pullback = jax.vjp(forward, tokens.astype(jnp.float32), w_query, key_projection, value_projection, w_out, gain_attn, gain_moe, w_gate, w_up, w_down)
    grads = pullback(cotangent.astype(jnp.float32))
    return (output.astype(jnp.bfloat16), grads[0], grads[1], grads[2], grads[3], grads[4], grads[5], grads[6], grads[7], grads[8], grads[9])
```

```python
import jax
import jax.numpy as jnp
from jax import lax
from jax.sharding import PartitionSpec as P

HEAD_SIZE = 64
EXPERTS = 32
TOP = 8
EPS = 1e-06
THETA = 10000.0
MASKED = -1e30

LOW = jnp.bfloat16
FULL = jnp.float32
ROWS_ON_ROWS = (((0,), (0,)), ((), ()))
COLS_ON_ROWS = (((1,), (0,)), ((), ()))
COLS_ON_COLS = (((1,), (1,)), ((), ()))


def mul(left, right, dims=COLS_ON_ROWS):
    return lax.dot_general(left, right, dims, preferred_element_type=FULL)


def swap(field, axis, mask):
    count = lax.axis_size(axis)
    return lax.ppermute(field, axis, [(i, i ^ mask) for i in range(count)])


def stages_of(count, first_bit):
    bits = [1 << b for b in range(first_bit, count.bit_length() - 1)]
    bits.reverse()
    stages = []
    if len(bits) >= 2:
        stages.append([bits[0], bits[1], bits[0] | bits[1]])
        bits = bits[2:]
    return stages + [[b] for b in bits]


def gather_stage(field, axis, masks):
    return jnp.concatenate([field] + [swap(field, axis, m) for m in masks], axis=0)


def scatter_stage(low_parts, kept, axis, masks):
    total = kept
    for part, m in zip(low_parts, masks):
        total = total + swap(part, axis, m).astype(FULL)
    return total


def reorder(field, mine, count, dim):
    size = field.shape[dim] // count
    return jnp.concatenate(
        [lax.dynamic_slice_in_dim(field, (mine ^ m) * size, size, dim) for m in range(count)],
        axis=dim,
    )


def rms_scale(field):
    return lax.rsqrt(jnp.mean(field * field, axis=-1, keepdims=True) + EPS)


def norm_back(grad, field, scale, gain):
    weighted = grad * gain
    inner = jnp.mean(weighted * field, axis=-1, keepdims=True)
    return scale * weighted - field * (scale * scale * scale) * inner


def turn(field, cosine, sine):
    half = field.shape[-1] // 2
    first, second = field[..., :half], field[..., half:]
    cosine, sine = cosine[:, None, :], sine[:, None, :]
    return jnp.concatenate(
        [first * cosine - second * sine, second * cosine + first * sine], axis=-1
    )


def local(
    tokens,
    cotangent,
    segments,
    routes,
    gates,
    w_query,
    key_projection,
    value_projection,
    w_out,
    gain_attn,
    gain_moe,
    w_gate,
    w_up,
    w_down,
):
    n_e, n_t = lax.axis_size("expert"), lax.axis_size("tensor")
    e, t = lax.axis_index("expert"), lax.axis_index("tensor")
    replicas = max(1, n_e // EXPERTS)
    own_experts = EXPERTS * replicas // n_e
    first_bit = replicas.bit_length() - 1
    length, width = tokens.shape
    part = width // n_e
    rows = length // n_t
    q_cols, k_cols = w_query.shape[1], key_projection.shape[1]
    hidden = w_gate.shape[2]
    group_masks = [m for s in stages_of(n_e, 0) for m in s]

    qkv_shard = jnp.concatenate([w_query, key_projection, value_projection], axis=1).astype(LOW)
    out_shard = w_out.astype(LOW)
    gain_shard = jnp.stack([gain_attn, gain_moe]).astype(LOW)

    def every(shard):
        held = {0: shard}
        for masks in stages_of(n_e, 0):
            fresh = {}
            for m in masks:
                for k, piece in held.items():
                    fresh[k ^ m] = swap(piece, "expert", m)
            held.update(fresh)
        return [held[m] for m in range(n_e)]

    qkv_rows = jnp.concatenate(every(qkv_shard), axis=0)
    out_cols = jnp.concatenate(every(out_shard), axis=1)
    gains = lax.all_gather(gain_shard, "expert", axis=1, tiled=True).astype(FULL)
    first_gain, second_gain = gains[0:1], gains[1:2]

    packed = jnp.concatenate(
        [
            w.astype(LOW).reshape(EXPERTS // own_experts, own_experts, w.shape[1] * w.shape[2] // 128, 128)
            for w in (w_gate, w_up, w_down)
        ],
        axis=1,
    )

    def to_owner(m):
        return lax.dynamic_index_in_dim(packed, (e ^ m) // replicas, 0, keepdims=False)

    arrived = [to_owner(0)] + [swap(to_owner(m), "expert", m) for m in range(1, n_e)]
    gate_up = jnp.zeros((n_e, part, 2 * own_experts * hidden), LOW)
    down = jnp.zeros((own_experts * hidden, width), LOW)
    for m, piece in enumerate(arrived):
        block = piece[: 2 * own_experts].reshape(2 * own_experts, part, hidden)
        block = block.transpose(1, 0, 2).reshape(1, part, 2 * own_experts * hidden)
        gate_up = lax.dynamic_update_slice(gate_up, block, (e ^ m, 0, 0))
        block = piece[2 * own_experts :].reshape(own_experts * hidden, part)
        down = lax.dynamic_update_slice(down, block, (0, (e ^ m) * part))
    gate_up = gate_up.reshape(width, 2 * own_experts * hidden)

    e_stages = [("expert", s) for s in stages_of(n_e, first_bit)]
    t_stages = [("tensor", [1 << b]) for b in reversed(range(n_t.bit_length() - 1))]
    t_last = t_stages[-1:]
    t_stages = t_stages[:-1]
    paths = [e_stages + t_stages, e_stages[:1] + t_stages + e_stages[1:]]

    def gather_tokens(block):
        half = block.shape[0] // 2
        chunks = []
        for field, path in zip((block[:half], block[half:]), paths):
            for axis, masks in path:
                field = gather_stage(field, axis, masks)
            chunks.append(field)
        field = jnp.concatenate(chunks, axis=0)
        for axis, masks in t_last:
            field = gather_stage(field, axis, masks)
        return field

    def scatter_tokens(field):
        for axis, masks in t_last:
            size = field.shape[0] // 2
            field = scatter_stage([field[size:].astype(LOW)], field[:size], axis, masks)
        half = field.shape[0] // 2
        done = []
        for chunk, path in zip((field[:half], field[half:]), paths):
            for axis, masks in reversed(path):
                size = chunk.shape[0] // (len(masks) + 1)
                sent = [
                    chunk[(i + 1) * size : (i + 2) * size].astype(LOW) for i in range(len(masks))
                ]
                chunk = scatter_stage(sent, chunk[:size], axis, masks)
            done.append(chunk)
        return jnp.concatenate(done, axis=0)

    own = t * rows
    grad_rows = lax.dynamic_slice_in_dim(cotangent, own, rows, 0)
    gate_rows = lax.dynamic_slice_in_dim(gates, own, rows, 0)
    route_rows = lax.dynamic_slice_in_dim(routes, own, rows, 0)
    gate_high = gate_rows.astype(LOW)
    gate_rest = (gate_rows - gate_high.astype(FULL)).astype(LOW)
    extra = jnp.concatenate(
        [
            route_rows.astype(LOW),
            gate_high,
            gate_rest,
            jnp.zeros((rows, 128 - 3 * TOP), LOW),
        ],
        axis=1,
    )
    grad_all = gather_tokens(jnp.concatenate([grad_rows, extra], axis=1))
    extra_all = grad_all[:, width : width + 3 * TOP].astype(FULL)
    grad_all = grad_all[:, :width]
    route_all = extra_all[:, :TOP].astype(jnp.int32)
    gate_all = extra_all[:, TOP : 2 * TOP] + extra_all[:, 2 * TOP :]
    first_expert = e // replicas * own_experts
    gate_of = jnp.concatenate(
        [
            jnp.broadcast_to(
                jnp.sum(
                    jnp.where(route_all == first_expert + j, gate_all, 0.0), axis=1, keepdims=True
                ),
                (route_all.shape[0], hidden),
            )
            for j in range(own_experts)
        ],
        axis=1,
    )

    inputs = tokens.astype(FULL)
    first_scale = rms_scale(inputs)
    first_hidden = (inputs * first_scale * first_gain).astype(LOW)
    hidden_rel = reorder(first_hidden, e, n_e, 1)
    documents = segments[0]
    index = jnp.arange(length)
    allowed = (index[None, :] <= index[:, None]) & (documents[None, :] == documents[:, None])
    position = jnp.sum(allowed.astype(FULL), axis=1) - 1.0
    freqs = THETA ** (-2.0 * jnp.arange(HEAD_SIZE // 2, dtype=FULL) / HEAD_SIZE)
    angle = position[:, None] * freqs[None, :]
    cosine, sine = jnp.cos(angle), jnp.sin(angle)
    heads, groups = q_cols // HEAD_SIZE, k_cols // HEAD_SIZE
    per_group = heads // groups
    qkv = mul(hidden_rel, qkv_rows)
    turned = turn(
        qkv[:, : q_cols + k_cols].reshape(length, heads + groups, HEAD_SIZE), cosine, sine
    ).astype(LOW)
    query = turned[:, :heads].reshape(length, groups, per_group, HEAD_SIZE)
    key = turned[:, heads:]
    value = qkv[:, q_cols + k_cols :].astype(LOW).reshape(length, groups, HEAD_SIZE)
    scores = jnp.einsum("qhgd,khd->hgqk", query, key, preferred_element_type=FULL)
    scores = jnp.where(allowed[None, None], scores * HEAD_SIZE**-0.5, MASKED)
    peak = jnp.max(scores, axis=-1, keepdims=True)
    raised = jnp.exp(scores - peak)
    shares = raised / jnp.sum(raised, axis=-1, keepdims=True)
    shares_low = shares.astype(LOW)
    mixed = jnp.einsum("hgqk,khd->qhgd", shares_low, value, preferred_element_type=FULL)
    mixed = mixed.astype(LOW).reshape(length, q_cols)
    order = [0]
    for axis, masks in reversed(t_stages + t_last):
        order = [k ^ b for b in [0] + masks for k in order] if False else order
    order = list(range(n_t))
    for_stage = [masks[0] for axis, masks in t_last + t_stages]
    order = [0]
    for b in reversed(for_stage):
        order = order + [k ^ b for k in order]
    mixed_rel = jnp.concatenate(
        [lax.dynamic_slice_in_dim(mixed, (t ^ m) * rows, rows, 0) for m in order], axis=0
    )

    def scatter_rows(field):
        for b in for_stage:
            size = field.shape[0] // 2
            field = scatter_stage([field[size:].astype(LOW)], field[:size], "tensor", [b])
        return field

    def gather_rows(field):
        for b in reversed(for_stage):
            field = gather_stage(field, "tensor", [b])
        return field

    own_inputs = lax.dynamic_slice_in_dim(tokens, own, rows, 0).astype(FULL)
    attention = reorder(scatter_rows(mul(mixed_rel, out_cols)), e, n_e, 1)
    middle = own_inputs + attention
    second_scale = rms_scale(middle)
    second_hidden = (middle * second_scale * second_gain).astype(LOW)

    hidden_all = gather_tokens(second_hidden)
    both = mul(hidden_all, gate_up)
    wide = own_experts * hidden
    gate_pre, up_pre = both[:, :wide], both[:, wide:]
    back = mul(grad_all, down, COLS_ON_COLS) * gate_of
    squash = jax.nn.sigmoid(gate_pre)
    silu = gate_pre * squash
    active = (silu * up_pre).astype(LOW).astype(FULL)
    active = (active * gate_of).astype(LOW)
    grad_gate = (back * up_pre * squash * (1.0 + gate_pre * (1.0 - squash))).astype(LOW)
    grad_up = (back * silu).astype(LOW)
    grad_both = jnp.concatenate([grad_gate, grad_up], axis=1)
    grad_second = scatter_tokens(mul(grad_both, gate_up, COLS_ON_COLS))
    expert_out = scatter_tokens(mul(active, down))
    output_rows = (middle + expert_out).astype(LOW)
    output = lax.all_gather(output_rows, "tensor", axis=0, tiled=True)

    grad_gate_up_w = mul(hidden_all, grad_both, ROWS_ON_ROWS)
    grad_down_w = mul(active, grad_all, ROWS_ON_ROWS)

    def to_holder(m):
        block = lax.dynamic_slice_in_dim(grad_gate_up_w, (e ^ m) * part, part, 0)
        block = block.reshape(part, 2 * own_experts, hidden).transpose(1, 0, 2)
        block = block.reshape(2 * own_experts, part * hidden // 128, 128)
        other = lax.dynamic_slice_in_dim(grad_down_w, (e ^ m) * part, part, 1)
        other = other.reshape(own_experts, hidden * part // 128, 128)
        return jnp.concatenate([block, other], axis=0)

    returned = [to_holder(0)] + [
        swap(to_holder(m).astype(LOW), "expert", m).astype(FULL) for m in range(1, n_e)
    ]
    shards = [jnp.zeros((EXPERTS,) + w.shape[1:], FULL) for w in (w_gate, w_up, w_down)]
    totals = {}
    for m, piece in enumerate(returned):
        root = m // replicas
        totals[root] = totals[root] + piece if root in totals else piece
    for root, piece in totals.items():
        at = (e // replicas ^ root) * own_experts
        for i, shard in enumerate(shards):
            block = piece[i * own_experts : (i + 1) * own_experts]
            shards[i] = lax.dynamic_update_slice(
                shard, block.reshape((own_experts,) + shard.shape[1:]), (at, 0, 0)
            )

    own_grad = grad_rows.astype(FULL)
    moe_gain_part = jnp.sum(grad_second * middle * second_scale, axis=0, keepdims=True)
    grad_middle = own_grad + norm_back(grad_second, middle, second_scale, second_gain)
    branch_rel = gather_rows(reorder(grad_middle.astype(LOW), e, n_e, 1))
    grad_out_w = mul(mixed_rel, branch_rel, ROWS_ON_ROWS)
    grad_mixed_rel = mul(branch_rel, out_cols, COLS_ON_COLS).astype(LOW)
    place = {m: k for k, m in enumerate(order)}

    def natural_rows(field):
        table = jnp.array([place[m] for m in range(n_t)], jnp.int32)
        return jnp.concatenate(
            [lax.dynamic_slice_in_dim(field, table[t ^ k] * rows, rows, 0) for k in range(n_t)],
            axis=0,
        )

    grad_mixed = natural_rows(grad_mixed_rel).reshape(length, groups, per_group, HEAD_SIZE)
    grad_shares = jnp.einsum("qhgd,khd->hgqk", grad_mixed, value, preferred_element_type=FULL)
    inner = jnp.sum(shares * grad_shares, axis=-1, keepdims=True)
    grad_scores = (shares * (grad_shares - inner)).astype(LOW)
    grad_query = jnp.einsum("hgqk,khd->qhgd", grad_scores, key, preferred_element_type=FULL)
    grad_key = jnp.einsum("hgqk,qhgd->khd", grad_scores, query, preferred_element_type=FULL)
    grad_value = jnp.einsum("hgqk,qhgd->khd", shares_low, grad_mixed, preferred_element_type=FULL)
    grad_turned = jnp.concatenate(
        [grad_query.reshape(length, heads, HEAD_SIZE), grad_key], axis=1
    ) * HEAD_SIZE**-0.5
    grad_qkv = jnp.concatenate(
        [
            turn(grad_turned, cosine, -sine).astype(LOW).reshape(length, q_cols + k_cols),
            grad_value.astype(LOW).reshape(length, k_cols),
        ],
        axis=1,
    )
    grad_qkv_w = mul(hidden_rel, grad_qkv, ROWS_ON_ROWS)
    grad_qkv_rel = jnp.concatenate(
        [lax.dynamic_slice_in_dim(grad_qkv, (t ^ m) * rows, rows, 0) for m in order], axis=0
    )
    grad_first = reorder(
        scatter_rows(mul(grad_qkv_rel, qkv_rows, COLS_ON_COLS)), e, n_e, 1
    )
    own_scale = lax.dynamic_slice_in_dim(first_scale, own, rows, 0)
    attn_gain_part = jnp.sum(grad_first * own_inputs * own_scale, axis=0, keepdims=True)
    grad_input = grad_middle + norm_back(grad_first, own_inputs, own_scale, first_gain)
    grad_input = lax.all_gather(grad_input.astype(LOW), "tensor", axis=0, tiled=True).astype(FULL)

    def shared(blocks):
        held = blocks
        for masks in reversed(stages_of(n_e, 0)):
            span = {0, *masks}
            bits = 0
            for m in masks:
                bits |= m
            kept = {}
            for k in held:
                if k & bits == 0:
                    total = held[k]
                    for m in masks:
                        total = total + swap(held[k ^ m].astype(LOW), "expert", m).astype(FULL)
                    kept[k] = total
            held = kept
        return held[0]

    qkv_grad = shared({m: grad_qkv_w[m * part : (m + 1) * part] for m in range(n_e)})
    out_grad = shared({m: grad_out_w[:, m * part : (m + 1) * part] for m in range(n_e)})
    gain_parts = jnp.concatenate([attn_gain_part, moe_gain_part], axis=0)
    gain_grads = lax.psum(gain_parts, ("expert", "tensor"))
    gain_grads = lax.dynamic_slice_in_dim(gain_grads, e * part, part, 1)
    return (
        output,
        grad_input,
        qkv_grad[:, :q_cols],
        qkv_grad[:, q_cols : q_cols + k_cols],
        qkv_grad[:, q_cols + k_cols :],
        out_grad,
        gain_grads[0],
        gain_grads[1],
        shards[0],
        shards[1],
        shards[2],
    )


def solution(mesh):
    by_rows = P("expert", None)
    by_both = P("expert", "tensor")
    in_experts = P(None, "expert", "tensor")
    down_specs = P(None, "tensor", "expert")
    return jax.shard_map(
        local,
        mesh=mesh,
        in_specs=(by_rows,) * 5
        + (by_both,) * 3
        + (P("tensor", "expert"), P("expert"), P("expert"), in_experts, in_experts, down_specs),
        out_specs=(by_rows, by_rows)
        + (by_both,) * 3
        + (P("tensor", "expert"), P("expert"), P("expert"), in_experts, in_experts, down_specs),
        check_vma=False,
    )
```

```python
import functools

import jax
import jax.numpy as jnp
from jax import lax
from jax.experimental import pallas as pl
from jax.experimental.pallas import tpu as pltpu
from jax.sharding import PartitionSpec as P

HEAD_SIZE = 64
EXPERTS = 32
TOP = 8
EPS = 1e-06
THETA = 10000.0
MASKED = -1e30
LANES = 128
LIMIT = 56 * 1024 * 1024

LOW = jnp.bfloat16
FULL = jnp.float32
ROWS_ON_ROWS = (((0,), (0,)), ((), ()))
COLS_ON_ROWS = (((1,), (0,)), ((), ()))
COLS_ON_COLS = (((1,), (1,)), ((), ()))


def mul(left, right, dims=COLS_ON_ROWS):
    return lax.dot_general(left, right, dims, preferred_element_type=FULL)


def shape(dims, dtype):
    return jax.ShapeDtypeStruct(dims, dtype)


def call(body, outs, *args, grid=None, in_specs=None, out_specs=None, scratch=(), flops=0):
    size = sum(a.size * a.dtype.itemsize for a in args)
    size += sum(o.size * jnp.dtype(o.dtype).itemsize for o in outs)
    whole = pl.BlockSpec(memory_space=pltpu.VMEM)
    if in_specs is None:
        in_specs = [whole] * (len(args) - 1)
    if out_specs is None:
        out_specs = [whole] * len(outs)
    extra = {} if grid is None else {"grid": grid}
    return pl.pallas_call(
        body,
        out_shape=list(outs),
        in_specs=[pl.BlockSpec(memory_space=pltpu.SMEM)] + list(in_specs),
        out_specs=list(out_specs),
        scratch_shapes=list(scratch),
        compiler_params=pltpu.CompilerParams(vmem_limit_bytes=LIMIT),
        cost_estimate=pl.CostEstimate(flops=flops, bytes_accessed=size, transcendentals=0),
        **extra,
    )(*args)


def swap(field, axis, mask):
    count = lax.axis_size(axis)
    return lax.ppermute(field, axis, [(i, i ^ mask) for i in range(count)])


def swap_by_parity(field, even, odd):
    n_e, n_t = lax.axis_size("expert"), lax.axis_size("tensor")
    pairs = []
    for e in range(n_e):
        for t in range(n_t):
            axis, mask = odd if t & 1 else even
            to = ((e ^ mask) * n_t + t) if axis == "expert" else (e * n_t + (t ^ mask))
            pairs.append((e * n_t + t, to))
    return lax.ppermute(field, ("expert", "tensor"), pairs)


def first_and_rest(count, first_bit):
    bits = [1 << b for b in range(first_bit, count.bit_length() - 1)]
    bits.reverse()
    if len(bits) < 2:
        return bits, []
    return [bits[0], bits[1], bits[0] | bits[1]], bits[2:]


def rotate(field, cosine, sine):
    lane = lax.broadcasted_iota(jnp.int32, (field.shape[0], LANES), 1)
    low_half = lane % HEAD_SIZE < HEAD_SIZE // 2
    turned = []
    for at in range(0, field.shape[1], LANES):
        block = field[:, at : at + LANES]
        ahead = pltpu.roll(block, LANES - HEAD_SIZE // 2, 1)
        behind = pltpu.roll(block, HEAD_SIZE // 2, 1)
        turned.append(block * cosine + jnp.where(low_half, ahead, behind) * sine)
    return jnp.concatenate(turned, axis=1)


def admitted(doc_row, doc_col):
    length = doc_row.shape[1]
    row = lax.broadcasted_iota(jnp.int32, (length, length), 0)
    col = lax.broadcasted_iota(jnp.int32, (length, length), 1)
    return (col <= row) & (doc_row == doc_col)


def softmax_of(query, key, allowed):
    scores = mul(query, key, COLS_ON_COLS) * HEAD_SIZE**-0.5
    scores = jnp.where(allowed, scores, MASKED)
    raised = jnp.exp(scores - jnp.max(scores, axis=1, keepdims=True))
    return raised / jnp.sum(raised, axis=1, keepdims=True)


def place_rows(target, sources, masks, me, part, pitch):
    for source, names in zip(sources, masks):
        for k, m in enumerate(names):
            at = pl.multiple_of((me ^ m) * part, part)
            target[pl.ds(at, part), :] = source[k * pitch : k * pitch + part, :]


def attend_body(masks, part, pitch, q_cols, k_cols, rows, order, where, *refs):
    n = len(masks)
    sources = refs[:n]
    tokens, gain, doc_row, doc_col, cosine, sine = refs[n : n + 6]
    weights, hidden, qkv_out, mixed_out = refs[n + 6 : n + 10]
    mixed = refs[n + 10]
    place_rows(weights, sources, masks, where[0], part, pitch)
    x = tokens[...].astype(FULL)
    scale = lax.rsqrt(jnp.mean(x * x, axis=1, keepdims=True) + EPS)
    first = (x * scale * gain[0:1, :]).astype(LOW)
    hidden[...] = first
    qkv = mul(first, weights[...])
    turned = rotate(qkv[:, : q_cols + k_cols], cosine[...], sine[...]).astype(LOW)
    values = qkv[:, q_cols + k_cols :].astype(LOW)
    qkv_out[:, : q_cols + k_cols] = turned
    qkv_out[:, q_cols + k_cols :] = values
    allowed = admitted(doc_row[...], doc_col[...])
    per_group = q_cols // k_cols
    for h in range(q_cols // HEAD_SIZE):
        at, g = h * HEAD_SIZE, h // per_group * HEAD_SIZE
        shares = softmax_of(
            turned[:, at : at + HEAD_SIZE],
            turned[:, q_cols + g : q_cols + g + HEAD_SIZE],
            allowed,
        ).astype(LOW)
        mixed[:, at : at + HEAD_SIZE] = mul(shares, values[:, g : g + HEAD_SIZE]).astype(LOW)
    for k, m in enumerate(order):
        at = pl.multiple_of((where[1] ^ m) * rows, rows)
        mixed_out[k * rows : (k + 1) * rows, :] = mixed[pl.ds(at, rows), :]


def branch_body(masks, part, where, *refs):
    n = len(masks)
    sources = refs[:n]
    mixed, weights, kept, sent = refs[n:]
    place_rows(weights, sources, masks, where[0], part, part)
    half = kept.shape[0]
    product = mul(mixed[...], weights[...], COLS_ON_COLS)
    kept[...] = product[:half]
    sent[...] = product[half:].astype(LOW)


def middle_body(rows, where, tokens, kept, got, gain, middle, hidden):
    at = pl.multiple_of(where[1] * rows, rows)
    m = tokens[pl.ds(at, rows), :].astype(FULL) + (kept[...] + got[...].astype(FULL))
    middle[...] = m
    scale = lax.rsqrt(jnp.mean(m * m, axis=1, keepdims=True) + EPS)
    hidden[...] = (m * scale * gain[1:2, :]).astype(LOW)


def owner_body(n_piece, n_e, part, own, hid, replicas, where, *refs):
    pieces = refs[:n_e]
    grads = refs[n_e : n_e + n_piece]
    weights, gate_out, back_out, buffer = refs[n_e + n_piece :]
    width = n_e * part
    step = pl.program_id(0)

    @pl.when(step == 0)
    def _():
        place_rows(weights, pieces, [[m] for m in range(n_e)], where[0], part, part)

    for k in range(n_piece):

        @pl.when(step == k)
        def _():
            buffer[...] = grads[k][...]

    extra = buffer[:, width:].astype(FULL)
    lane = lax.broadcasted_iota(jnp.int32, extra.shape, 1)
    gate = pltpu.roll(extra, LANES - TOP, 1) + pltpu.roll(extra, LANES - 2 * TOP, 1)
    first = where[0] // replicas * own
    back = mul(buffer[:, :width], weights[:, 2 * own * hid :])
    table = jnp.zeros(extra.shape, FULL)
    for j in range(own):
        hit = (lane < TOP) & (extra == (first + j).astype(FULL))
        column = jnp.sum(jnp.where(hit, gate, 0.0), axis=1, keepdims=True)
        table = jnp.where(lane == j, column, table)
        back_out[:, j * hid : (j + 1) * hid] = back[:, j * hid : (j + 1) * hid] * column
    gate_out[...] = table


def expert_body(n_piece, own, hid, where, *refs):
    rows = refs[:n_piece]
    weights, gate, back, grad_hidden, active_out, grad_both, buffer = refs[n_piece:]
    step = pl.program_id(0)
    for k in range(n_piece):

        @pl.when(step == k)
        def _():
            buffer[...] = rows[k][...]

    wide = own * hid
    both = mul(buffer[...], weights[:, : 2 * wide])
    for j in range(own):
        at = slice(j * hid, (j + 1) * hid)
        up_at = slice(wide + j * hid, wide + (j + 1) * hid)
        pre, up = both[:, at], both[:, up_at]
        squash = 1.0 / (1.0 + jnp.exp(-pre))
        silu = pre * squash
        active = (silu * up).astype(LOW).astype(FULL)
        active_out[:, at] = (active * gate[:, j : j + 1]).astype(LOW)
        d = back[:, at]
        grad_both[:, at] = (d * up * squash * (1.0 + pre * (1.0 - squash))).astype(LOW)
        grad_both[:, up_at] = (d * silu).astype(LOW)
    product = mul(grad_both[...], weights[:, : 2 * wide], COLS_ON_COLS)
    grad_hidden[...] = product.astype(grad_hidden.dtype)


def out_body(where, active, weights, out):
    out[...] = mul(active[...], weights[...], COLS_ON_COLS).astype(out.dtype)


def weight_grad_body(n_piece, where, *refs):
    hidden = refs[:n_piece]
    grads = refs[n_piece : 2 * n_piece]
    both = refs[2 * n_piece : 2 * n_piece + 2]
    active = refs[2 * n_piece + 2 : 2 * n_piece + 4]
    out, column = refs[2 * n_piece + 4 :]
    size = hidden[0].shape[0]
    half = n_piece // 2 * size
    wide = both[0].shape[1]
    for sources, right, cols in ((hidden, both, slice(0, wide)), (grads, active, slice(wide, None))):
        for k in range(n_piece):
            column[k * size : (k + 1) * size, :] = sources[k][...]
        total = mul(column[:half], right[0][...], ROWS_ON_ROWS)
        total = total + mul(column[half:], right[1][...], ROWS_ON_ROWS)
        out[:, cols] = total.astype(LOW)


def middle_back_body(n_got, where, *refs):
    kept, got = refs[0], refs[1 : 1 + n_got]
    middle, grad, gain, grad_middle, low, gain_part = refs[1 + n_got :]
    total = kept[...]
    for piece in got:
        total = total + piece[...].astype(FULL)
    m = middle[...]
    scale = lax.rsqrt(jnp.mean(m * m, axis=1, keepdims=True) + EPS)
    gain_part[...] = jnp.broadcast_to(
        jnp.sum(total * m * scale, axis=0, keepdims=True), gain_part.shape
    )
    weighted = total * gain[1:2, :]
    inner = jnp.mean(weighted * m, axis=1, keepdims=True)
    back = grad[...].astype(FULL) + (scale * weighted - m * (scale * scale * scale) * inner)
    grad_middle[...] = back
    low[...] = back.astype(LOW)


def attend_back_body(n_piece, q_cols, k_cols, rows, part, order, even, odd, where, *refs):
    pieces = refs[:n_piece]
    mixed, out_weights, qkv_in, doc_row, doc_col, cosine, sine, hidden, weights = refs[
        n_piece : n_piece + 9
    ]
    kept, sent, first_kept, first_sent, branch, natural, grad_qkv, grads = refs[n_piece + 9 :]
    for k in range(n_piece):
        branch[k * rows : (k + 1) * rows, :] = pieces[k][...]
    grad_mixed = mul(branch[...], out_weights[...]).astype(LOW)
    for k, m in enumerate(order):
        at = pl.multiple_of((where[1] ^ m) * rows, rows)
        natural[pl.ds(at, rows), :q_cols] = grad_mixed[k * rows : (k + 1) * rows]
    qk = q_cols + k_cols
    total = qk + k_cols
    grads[:, total:] = mul(branch[...], mixed[...], ROWS_ON_ROWS)
    allowed = admitted(doc_row[...], doc_col[...])
    per_group = q_cols // k_cols
    query_grads, key_grads, value_grads = [], [], []
    for g in range(k_cols // HEAD_SIZE):
        key = qkv_in[:, q_cols + g * HEAD_SIZE : q_cols + (g + 1) * HEAD_SIZE]
        value = qkv_in[:, qk + g * HEAD_SIZE : qk + (g + 1) * HEAD_SIZE]
        key_grad = value_grad = None
        for h in range(g * per_group, (g + 1) * per_group):
            at = slice(h * HEAD_SIZE, (h + 1) * HEAD_SIZE)
            query = qkv_in[:, at]
            shares = softmax_of(query, key, allowed)
            grad = natural[:, at]
            grad_shares = mul(grad, value, COLS_ON_COLS)
            inner = jnp.sum(shares * grad_shares, axis=1, keepdims=True)
            grad_scores = (shares * (grad_shares - inner)).astype(LOW)
            query_grads.append(mul(grad_scores, key))
            dk = mul(grad_scores, query, ROWS_ON_ROWS)
            dv = mul(shares.astype(LOW), grad, ROWS_ON_ROWS)
            key_grad = dk if key_grad is None else key_grad + dk
            value_grad = dv if value_grad is None else value_grad + dv
        key_grads.append(key_grad)
        value_grads.append(value_grad)
    turned = jnp.concatenate(query_grads + key_grads, axis=1) * HEAD_SIZE**-0.5
    grad_qkv[:, :qk] = rotate(turned, cosine[...], -sine[...]).astype(LOW)
    grad_qkv[:, qk:] = jnp.concatenate(value_grads, axis=1).astype(LOW)
    grads[:, :total] = mul(hidden[...], grad_qkv[...], ROWS_ON_ROWS)
    for names, target in ((even, kept), (odd, sent)):
        for k, m in enumerate(names):
            at = pl.multiple_of((where[0] ^ m) * part, part)
            target[k * part : (k + 1) * part, :] = grads[pl.ds(at, part), :].astype(target.dtype)
    for k, m in enumerate(order):
        at = pl.multiple_of((where[1] ^ m) * rows, rows)
        natural[k * rows : (k + 1) * rows, :total] = grad_qkv[pl.ds(at, rows), :]
    product = mul(natural[:, :total], weights[...], COLS_ON_COLS)
    half = first_kept.shape[0]
    first_kept[...] = product[:half]
    first_sent[...] = product[half:].astype(LOW)


def tokens_back_body(rows, where, tokens, kept, got, gain, grad_middle, moe_part, out):
    at = pl.multiple_of(where[1] * rows, rows)
    x = tokens[pl.ds(at, rows), :].astype(FULL)
    scale = lax.rsqrt(jnp.mean(x * x, axis=1, keepdims=True) + EPS)
    first = kept[...] + got[...].astype(FULL)
    attn_part = jnp.sum(first * x * scale, axis=0, keepdims=True)
    weighted = first * gain[0:1, :]
    inner = jnp.mean(weighted * x, axis=1, keepdims=True)
    out[:rows] = grad_middle[...] + (scale * weighted - x * (scale * scale * scale) * inner)
    line = lax.broadcasted_iota(jnp.int32, moe_part.shape, 0)
    out[rows:] = jnp.where(line == 0, attn_part, jnp.where(line == 1, moe_part[...], 0.0))


def unpack_body(n_e, own, hid, replicas, turn, where, *refs):
    pieces = refs[:n_e]
    outs = refs[n_e:]
    step = pl.program_id(0)
    for root in range(n_e // replicas):

        @pl.when(step == root)
        def _():
            total = pieces[root * replicas][...].astype(FULL)
            for r in range(1, replicas):
                total = total + pieces[root * replicas + r][...].astype(FULL)
            for i, out in enumerate(outs):
                for j in range(own):
                    at = (i * own + j) * hid
                    block = total[:, at : at + hid]
                    out[j] = block.T if turn and i == 2 else block


def local(
    tokens,
    cotangent,
    segments,
    routes,
    gates,
    w_query,
    key_projection,
    value_projection,
    w_out,
    gain_attn,
    gain_moe,
    w_gate,
    w_up,
    w_down,
):
    n_e, n_t = lax.axis_size("expert"), lax.axis_size("tensor")
    e, t = lax.axis_index("expert"), lax.axis_index("tensor")
    where = jnp.stack([e, t]).astype(jnp.int32)
    replicas = max(1, n_e // EXPERTS)
    own_experts = EXPERTS * replicas // n_e
    first_bit = replicas.bit_length() - 1
    length, width = tokens.shape
    part = width // n_e
    rows = length // n_t
    q_cols, k_cols = w_query.shape[1], key_projection.shape[1]
    qkv_cols = q_cols + 2 * k_cols
    hidden = w_gate.shape[2]
    wide = own_experts * hidden

    pad = 16
    gain_rows = jnp.stack([gain_attn, gain_moe])
    gain_rows = jnp.pad(gain_rows, ((0, pad - 2), (0, qkv_cols - part)))
    qkv_shard = jnp.concatenate(
        [
            jnp.concatenate([w_query, key_projection, value_projection], axis=1),
            gain_rows,
        ],
        axis=0,
    ).astype(LOW)
    out_shard = w_out.T.astype(LOW)

    masks_first, bits_rest = first_and_rest(n_e, 0)

    def every(shard):
        arrays = [jnp.concatenate([shard] + [swap(shard, "expert", m) for m in masks_first])]
        names = [[0] + masks_first]
        for b in bits_rest:
            arrays = arrays + [swap(a, "expert", b) for a in arrays]
            names = names + [[m ^ b for m in line] for line in names]
        return arrays, names

    qkv_arrays, names = every(qkv_shard)
    out_arrays, _ = every(out_shard)
    pitch = part + pad
    held = {}
    for array, line in zip(qkv_arrays, names):
        for k, m in enumerate(line):
            held[m] = array[k * pitch + part : k * pitch + part + 2, :part]
    gains = jnp.stack([held[m] for m in range(n_e)]).astype(FULL)
    gains = jnp.concatenate(
        [lax.dynamic_index_in_dim(gains, e ^ k, 0, keepdims=False) for k in range(n_e)], axis=1
    )

    def blocks(w):
        w = w.reshape(EXPERTS // own_experts, own_experts, part, hidden)
        return w.transpose(0, 2, 1, 3).reshape(EXPERTS // own_experts, part, wide)

    packed = jnp.concatenate(
        [blocks(w.astype(LOW)) for w in (w_gate, w_up, w_down.transpose(0, 2, 1))], axis=2
    )

    def to_owner(m):
        return lax.dynamic_index_in_dim(packed, (e ^ m) // replicas, 0, keepdims=False)

    arrived = [to_owner(0)] + [swap(to_owner(m), "expert", m) for m in range(1, n_e)]

    masks_tok, bits_tok = first_and_rest(n_e, first_bit)
    e_rest = [("expert", b) for b in bits_tok]
    t_bits = [("tensor", 1 << b) for b in reversed(range(n_t.bit_length() - 1))]
    even_path, odd_path = e_rest + t_bits[:-1], t_bits[:-1] + e_rest
    last = t_bits[-1]

    def gather_tokens(block):
        pieces = [jnp.concatenate([block] + [swap(block, "expert", m) for m in masks_tok])]
        for even, odd in zip(even_path, odd_path):
            pieces = pieces + [swap_by_parity(p, even, odd) for p in pieces]
        return pieces + [swap(p, *last) for p in pieces]

    def scatter_tokens(kept, sent):
        pieces = [a + swap(s, *last).astype(FULL) for a, s in zip(kept, sent)]
        for even, odd in zip(reversed(even_path), reversed(odd_path)):
            half = len(pieces) // 2
            pieces = [
                a + swap_by_parity(b.astype(LOW), even, odd).astype(FULL)
                for a, b in zip(pieces[:half], pieces[half:])
            ]
        (piece,) = pieces
        size = piece.shape[0] // (len(masks_tok) + 1)
        got = [
            swap(piece[(i + 1) * size : (i + 2) * size].astype(LOW), "expert", m)
            for i, m in enumerate(masks_tok)
        ]
        return piece[:size], got

    own = t * rows
    grad_rows = lax.dynamic_slice_in_dim(cotangent, own, rows, 0)
    gate_rows = lax.dynamic_slice_in_dim(gates, own, rows, 0)
    route_rows = lax.dynamic_slice_in_dim(routes, own, rows, 0)
    gate_high = gate_rows.astype(LOW)
    gate_rest = (gate_rows - gate_high.astype(FULL)).astype(LOW)
    extra = jnp.concatenate([route_rows.astype(LOW), gate_high, gate_rest], axis=1)
    extra = jnp.pad(extra, ((0, 0), (0, LANES - 3 * TOP)))
    grad_pieces = gather_tokens(jnp.concatenate([grad_rows, extra], axis=1))

    documents = segments[0]
    doc_row, doc_col = documents[None, :], documents[:, None]
    index = jnp.arange(length)
    same = (index[None, :] < index[:, None]) & (doc_row == doc_col)
    position = jnp.sum(same.astype(FULL), axis=1, keepdims=True)
    lane = jnp.arange(LANES)
    freqs = THETA ** (-2.0 * (lane % (HEAD_SIZE // 2)).astype(FULL) / HEAD_SIZE)
    angle = position * freqs[None, :]
    cosine = jnp.cos(angle)
    sine = jnp.sin(angle) * jnp.where(lane % HEAD_SIZE < HEAD_SIZE // 2, -1.0, 1.0)[None, :]
    t_masks = [b for _, b in reversed(t_bits)]
    order = [0]
    for b in reversed(t_masks):
        order = order + [k ^ b for k in order]
    weights, first_hidden, qkv, mixed = call(
        functools.partial(attend_body, names, part, pitch, q_cols, k_cols, rows, order),
        [
            shape((width, qkv_cols), LOW),
            shape((length, width), LOW),
            shape((length, qkv_cols), LOW),
            shape((length, q_cols), LOW),
        ],
        where, *qkv_arrays, tokens, gains, doc_row, doc_col, cosine, sine,
        scratch=[pltpu.VMEM((length, q_cols), LOW)],
        flops=2 * length * (width * qkv_cols + 2 * length * q_cols),
    )
    out_weights, kept, sent = call(
        functools.partial(branch_body, names, part),
        [
            shape((width, q_cols), LOW),
            shape((length // 2, width), FULL),
            shape((length // 2, width), LOW),
        ],
        where, *out_arrays, mixed,
        flops=2 * length * width * q_cols,
    )

    def scatter_rows(kept, sent):
        for b in t_masks[:-1]:
            total = kept + swap(sent, "tensor", b).astype(FULL)
            half = total.shape[0] // 2
            kept, sent = total[:half], total[half:].astype(LOW)
        return kept, swap(sent, "tensor", t_masks[-1])

    kept, got = scatter_rows(kept, sent)
    middle, second_hidden = call(
        functools.partial(middle_body, rows),
        [shape((rows, width), FULL), shape((rows, width), LOW)],
        where, tokens, kept, got, gains,
    )

    n_piece = len(grad_pieces)
    size = grad_pieces[0].shape[0]
    total_rows = n_piece * size
    whole = lambda a: pl.BlockSpec(a.shape, lambda i: (0,) * a.ndim)
    tile = lambda cols: pl.BlockSpec((size, cols), lambda i: (i, 0))
    expert_weights, gate_table, back = call(
        functools.partial(owner_body, n_piece, n_e, part, own_experts, hidden, replicas),
        [
            shape((width, 3 * wide), LOW),
            shape((total_rows, LANES), FULL),
            shape((total_rows, wide), FULL),
        ],
        where, *arrived, *grad_pieces,
        grid=(n_piece,),
        in_specs=[whole(a) for a in arrived] + [whole(a) for a in grad_pieces],
        out_specs=[
            pl.BlockSpec((width, 3 * wide), lambda i: (0, 0)),
            tile(LANES),
            tile(wide),
        ],
        scratch=[pltpu.VMEM((size, width + LANES), LOW)],
        flops=2 * total_rows * width * wide,
    )
    hidden_pieces = gather_tokens(second_hidden)
    half = n_piece // 2

    def experts(first, out_type):
        chosen = hidden_pieces[first : first + half]
        later = lambda cols: pl.BlockSpec((size, cols), lambda i: (i + first, 0))
        return call(
            functools.partial(expert_body, half, own_experts, hidden),
            [
                shape((half * size, width), out_type),
                shape((half * size, wide), LOW),
                shape((half * size, 2 * wide), LOW),
            ],
            where, *chosen, expert_weights, gate_table, back,
            grid=(half,),
            in_specs=[whole(a) for a in chosen]
            + [whole(expert_weights), later(LANES), later(wide)],
            out_specs=[tile(width), tile(wide), tile(2 * wide)],
            scratch=[pltpu.VMEM((size, width), LOW)],
            flops=2 * half * size * width * 4 * wide,
        )

    def pieces_of(field):
        return [field[k * size : (k + 1) * size] for k in range(half)]

    sent_hidden, sent_active, sent_both = experts(half, LOW)
    kept_hidden, kept_active, kept_both = experts(0, FULL)
    grad_kept, grad_got = scatter_tokens(pieces_of(kept_hidden), pieces_of(sent_hidden))

    def down(active, out_type):
        return call(
            out_body,
            [shape((half * size, width), out_type)],
            where, active, expert_weights,
            grid=(half,),
            in_specs=[tile(wide), pl.BlockSpec((width, wide), lambda i: (0, 2))],
            out_specs=[tile(width)],
            flops=2 * half * size * width * wide,
        )[0]

    sent_out, kept_out = down(sent_active, LOW), down(kept_active, FULL)
    out_kept, out_got = scatter_tokens(pieces_of(kept_out), pieces_of(sent_out))
    expert_out = out_kept
    for piece in out_got:
        expert_out = expert_out + piece.astype(FULL)
    output_rows = (middle + expert_out).astype(LOW)
    output = lax.all_gather(output_rows, "tensor", axis=0, tiled=True)

    block = 256
    column = pl.BlockSpec((size, block), lambda i: (0, i))
    (weight_grads,) = call(
        functools.partial(weight_grad_body, n_piece),
        [shape((width, 3 * wide), LOW)],
        where, *hidden_pieces, *grad_pieces, kept_both, sent_both, kept_active, sent_active,
        grid=(width // block,),
        in_specs=[column] * (2 * n_piece)
        + [whole(kept_both), whole(sent_both), whole(kept_active), whole(sent_active)],
        out_specs=[pl.BlockSpec((block, 3 * wide), lambda i: (i, 0))],
        scratch=[pltpu.VMEM((total_rows, block), LOW)],
        flops=2 * total_rows * width * 3 * wide,
    )

    def to_holder(m):
        return lax.dynamic_slice_in_dim(weight_grads, (e ^ m) * part, part, 0)

    returned = [to_holder(0)] + [swap(to_holder(m), "expert", m) for m in range(1, n_e)]
    turn = part % LANES == 0
    at_root = lambda dims: pl.BlockSpec(
        (own_experts,) + dims, lambda i, where: ((where[0] // replicas) ^ i, 0, 0)
    )
    out_dims = [(part, hidden), (part, hidden), (hidden, part) if turn else (part, hidden)]
    shards = pl.pallas_call(
        functools.partial(unpack_body, n_e, own_experts, hidden, replicas, turn),
        out_shape=[shape((EXPERTS,) + d, FULL) for d in out_dims],
        grid_spec=pltpu.PrefetchScalarGridSpec(
            num_scalar_prefetch=1,
            grid=(n_e // replicas,),
            in_specs=[pl.BlockSpec(a.shape, lambda i, where: (0, 0)) for a in returned],
            out_specs=[at_root(d) for d in out_dims],
        ),
        compiler_params=pltpu.CompilerParams(vmem_limit_bytes=LIMIT),
        cost_estimate=pl.CostEstimate(
            flops=0, bytes_accessed=6 * EXPERTS * part * hidden * 3, transcendentals=0
        ),
    )(where, *returned)
    gate_shard, up_shard, down_shard = shards
    if not turn:
        down_shard = down_shard.transpose(0, 2, 1)

    grad_middle, branch_grad, moe_part = call(
        functools.partial(middle_back_body, len(grad_got)),
        [shape((rows, width), FULL), shape((rows, width), LOW), shape((16, width), FULL)],
        where, grad_kept, *grad_got, middle, grad_rows, gains,
    )
    branch_pieces = [branch_grad]
    for b in reversed(t_masks):
        branch_pieces = branch_pieces + [swap(p, "tensor", b) for p in branch_pieces]
    low_bit = bits_rest[-1:] or [0]
    odd = [m for m in range(n_e) if low_bit[0] and m & low_bit[0]]
    even = [m for m in range(n_e) if m not in odd]
    all_cols = qkv_cols + q_cols
    kept_w, sent_w, first_kept, first_sent = call(
        functools.partial(
            attend_back_body, len(branch_pieces), q_cols, k_cols, rows, part, order, even,
            [m ^ low_bit[0] for m in even],
        ),
        [
            shape((len(even) * part, all_cols), FULL),
            shape((len(even) * part, all_cols), LOW),
            shape((length // 2, width), FULL),
            shape((length // 2, width), LOW),
        ],
        where, *branch_pieces, mixed, out_weights, qkv, doc_row, doc_col, cosine, sine,
        first_hidden, weights,
        scratch=[
            pltpu.VMEM((length, width), LOW),
            pltpu.VMEM((length, max(q_cols, qkv_cols)), LOW),
            pltpu.VMEM((length, qkv_cols), LOW),
            pltpu.VMEM((width, all_cols), FULL),
        ],
        flops=2 * length * width * (2 * q_cols + 2 * qkv_cols),
    )
    total = kept_w + swap(sent_w, "expert", low_bit[0]).astype(FULL)
    names_left = even
    for b in reversed(bits_rest[:-1]):
        keep = [k for k, m in enumerate(names_left) if not m & b]
        give = [names_left.index(names_left[k] ^ b) for k in keep]
        pick = lambda ks: jnp.concatenate([total[k * part : (k + 1) * part] for k in ks])
        total = pick(keep) + swap(pick(give).astype(LOW), "expert", b).astype(FULL)
        names_left = [names_left[k] for k in keep]
    attn_grad = total[:part]
    for m in masks_first:
        k = names_left.index(m)
        attn_grad = attn_grad + swap(
            total[k * part : (k + 1) * part].astype(LOW), "expert", m
        ).astype(FULL)

    kept, got = scatter_rows(first_kept, first_sent)
    (token_rows,) = call(
        functools.partial(tokens_back_body, rows),
        [shape((rows + 16, width), FULL)],
        where, tokens, kept, got, gains, grad_middle, moe_part,
    )
    gathered = lax.all_gather(token_rows.astype(LOW), "tensor", axis=0, tiled=True)
    gathered = gathered.reshape(n_t, rows + 16, width).astype(FULL)
    grad_input = gathered[:, :rows].reshape(length, width)
    gain_sum = jnp.sum(gathered[:, rows : rows + 2], axis=0)

    def gain_block(m):
        return lax.dynamic_slice_in_dim(gain_sum, (e ^ m) * part, part, 1)

    held = {m: gain_block(m) for m in range(n_e)}
    for b in reversed(bits_rest):
        keep = [m for m in held if not m & b]
        sent = jnp.concatenate([held[m ^ b] for m in keep], axis=0)
        got = swap(sent, "expert", b)
        held = {m: held[m] + got[2 * k : 2 * k + 2] for k, m in enumerate(keep)}
    gain_grads = held[0]
    for m in masks_first:
        gain_grads = gain_grads + swap(held[m], "expert", m)
    return (
        output,
        grad_input,
        attn_grad[:, :q_cols],
        attn_grad[:, q_cols : q_cols + k_cols],
        attn_grad[:, q_cols + k_cols : qkv_cols],
        attn_grad[:, qkv_cols:].T,
        gain_grads[0],
        gain_grads[1],
        gate_shard,
        up_shard,
        down_shard,
    )


def solution(mesh):
    by_rows = P("expert", None)
    by_both = P("expert", "tensor")
    in_experts = P(None, "expert", "tensor")
    down_specs = P(None, "tensor", "expert")
    return jax.shard_map(
        local,
        mesh=mesh,
        in_specs=(by_rows,) * 5
        + (by_both,) * 3
        + (P("tensor", "expert"), P("expert"), P("expert"), in_experts, in_experts, down_specs),
        out_specs=(by_rows, by_rows)
        + (by_both,) * 3
        + (P("tensor", "expert"), P("expert"), P("expert"), in_experts, in_experts, down_specs),
        check_vma=False,
    )
```

```python
import functools

import jax
import jax.numpy as jnp
from jax import lax
from jax.experimental import pallas as pl
from jax.experimental.pallas import tpu as pltpu
from jax.sharding import PartitionSpec as P

HEAD_SIZE = 64
EXPERTS = 32
TOP = 8
EPS = 1e-06
THETA = 10000.0
MASKED = -1e30
LANES = 128
LIMIT = 56 * 1024 * 1024

LOW = jnp.bfloat16
FULL = jnp.float32
ROWS_ON_ROWS = (((0,), (0,)), ((), ()))
COLS_ON_ROWS = (((1,), (0,)), ((), ()))
COLS_ON_COLS = (((1,), (1,)), ((), ()))


def mul(left, right, dims=COLS_ON_ROWS):
    return lax.dot_general(left, right, dims, preferred_element_type=FULL)


def shape(dims, dtype):
    return jax.ShapeDtypeStruct(dims, dtype)


def call(body, outs, *args, grid=None, in_specs=None, out_specs=None, scratch=(), flops=0):
    size = sum(a.size * a.dtype.itemsize for a in args)
    size += sum(o.size * jnp.dtype(o.dtype).itemsize for o in outs)
    whole = pl.BlockSpec(memory_space=pltpu.VMEM)
    if in_specs is None:
        in_specs = [whole] * (len(args) - 1)
    if out_specs is None:
        out_specs = [whole] * len(outs)
    extra = {} if grid is None else {"grid": grid}
    return pl.pallas_call(
        body,
        out_shape=list(outs),
        in_specs=[pl.BlockSpec(memory_space=pltpu.SMEM)] + list(in_specs),
        out_specs=list(out_specs),
        scratch_shapes=list(scratch),
        compiler_params=pltpu.CompilerParams(vmem_limit_bytes=LIMIT),
        cost_estimate=pl.CostEstimate(flops=flops, bytes_accessed=size, transcendentals=0),
        **extra,
    )(*args)


def swap(field, axis, mask):
    count = lax.axis_size(axis)
    return lax.ppermute(field, axis, [(i, i ^ mask) for i in range(count)])


def after(field, *earlier):
    return lax.optimization_barrier((field, *earlier))[0]


def swap_by_parity(field, even, odd):
    n_e, n_t = lax.axis_size("expert"), lax.axis_size("tensor")
    pairs = []
    for e in range(n_e):
        for t in range(n_t):
            axis, mask = odd if t & 1 else even
            to = ((e ^ mask) * n_t + t) if axis == "expert" else (e * n_t + (t ^ mask))
            pairs.append((e * n_t + t, to))
    return lax.ppermute(field, ("expert", "tensor"), pairs)


def bits_of(count, first_bit=0):
    return [1 << b for b in reversed(range(first_bit, count.bit_length() - 1))]


def position_in(mask, bits):
    return sum(jnp.where(mask & b != 0, 1 << i, 0) for i, b in enumerate(bits))


def order_of(bits):
    order = [0]
    for b in bits:
        order = order + [k ^ b for k in order]
    return order


def rotate(field, cosine, sine):
    lane = lax.broadcasted_iota(jnp.int32, (field.shape[0], LANES), 1)
    low_half = lane % HEAD_SIZE < HEAD_SIZE // 2
    turned = []
    for at in range(0, field.shape[1], LANES):
        block = field[:, at : at + LANES]
        ahead = pltpu.roll(block, LANES - HEAD_SIZE // 2, 1)
        behind = pltpu.roll(block, HEAD_SIZE // 2, 1)
        turned.append(block * cosine + jnp.where(low_half, ahead, behind) * sine)
    return jnp.concatenate(turned, axis=1)


def admitted(doc_row, doc_col):
    length = doc_row.shape[1]
    row = lax.broadcasted_iota(jnp.int32, (length, length), 0)
    col = lax.broadcasted_iota(jnp.int32, (length, length), 1)
    return (col <= row) & (doc_row == doc_col)


def softmax_of(query, key, allowed):
    scores = mul(query, key, COLS_ON_COLS) * HEAD_SIZE**-0.5
    scores = jnp.where(allowed, scores, MASKED)
    raised = jnp.exp(scores - jnp.max(scores, axis=1, keepdims=True))
    return raised / jnp.sum(raised, axis=1, keepdims=True)


def place_rows(target, sources, orders, where, part, pitch):
    count = len(orders[0]) // len(sources)
    for p, (even, odd) in enumerate(zip(*orders)):
        at = pl.multiple_of((where[0] ^ jnp.where(where[1] & 1 == 0, even, odd)) * part, part)
        k = p % count * pitch
        target[pl.ds(at, part), :] = sources[p // count][k : k + part, :]


def pack_body(own, hid, replicas, turn, where, gate, up, down, down_out, *sided):
    side = where[0] & 1
    for j in range(own):
        at = slice(j * hid, (j + 1) * hid)
        for k in range(2):
            block = down[(k * own if replicas == 1 else 0) + j]
            down_out[0, k, :, at] = (block.T if turn else block).astype(LOW)
            place = ((side ^ k) * own if replicas == 1 else 0) + j
            for source, out in ((gate, sided[k]), (up, sided[2 + k])):
                out[0, :, at] = source[place].astype(LOW)


def attend_body(orders, n, part, pitch, q_cols, k_cols, rows, order, where, *refs):
    sources = refs[:n]
    tokens, gain_in, doc_row, doc_col, cosine, sine = refs[n : n + 6]
    weights, hidden, qkv_out, mixed_out, gain = refs[n + 6 : n + 11]
    mixed = refs[n + 11]
    place_rows(weights, sources, orders, where, part, pitch)
    if part % LANES == 0:
        count = len(orders[0]) // n
        for p, (even, odd) in enumerate(zip(*orders)):
            at = pl.multiple_of((where[0] ^ jnp.where(where[1] & 1 == 0, even, odd)) * part, part)
            k = p % count * pitch + part
            gain[:, pl.ds(at, part)] = sources[p // count][k : k + gain.shape[0], :part].astype(FULL)
    else:
        gain[...] = gain_in[...]
    x = tokens[...].astype(FULL)
    scale = lax.rsqrt(jnp.mean(x * x, axis=1, keepdims=True) + EPS)
    first = (x * scale * gain[0:1, :]).astype(LOW)
    hidden[...] = first
    qkv = mul(first, weights[...])
    turned = rotate(qkv[:, : q_cols + k_cols], cosine[...], sine[...]).astype(LOW)
    values = qkv[:, q_cols + k_cols :].astype(LOW)
    qkv_out[:, : q_cols + k_cols] = turned
    qkv_out[:, q_cols + k_cols :] = values
    allowed = admitted(doc_row[...], doc_col[...])
    per_group = q_cols // k_cols
    for h in range(q_cols // HEAD_SIZE):
        at, g = h * HEAD_SIZE, h // per_group * HEAD_SIZE
        shares = softmax_of(
            turned[:, at : at + HEAD_SIZE],
            turned[:, q_cols + g : q_cols + g + HEAD_SIZE],
            allowed,
        ).astype(LOW)
        mixed[:, at : at + HEAD_SIZE] = mul(shares, values[:, g : g + HEAD_SIZE]).astype(LOW)
    for k, m in enumerate(order):
        at = pl.multiple_of((where[1] ^ m) * rows, rows)
        mixed_out[k * rows : (k + 1) * rows, :] = mixed[pl.ds(at, rows), :]


def branch_body(orders, n, part, where, *refs):
    sources = refs[:n]
    mixed, weights, kept, sent = refs[n:]
    place_rows(weights, sources, orders, where, part, part)
    half = kept.shape[0]
    product = mul(mixed[...], weights[...], COLS_ON_COLS)
    kept[...] = product[:half]
    sent[...] = product[half:].astype(LOW)


def middle_body(rows, where, tokens, kept, got, gain, middle, hidden):
    at = pl.multiple_of(where[1] * rows, rows)
    m = tokens[pl.ds(at, rows), :].astype(FULL) + (kept[...] + got[...].astype(FULL))
    middle[...] = m
    scale = lax.rsqrt(jnp.mean(m * m, axis=1, keepdims=True) + EPS)
    hidden[...] = (m * scale * gain[1:2, :]).astype(LOW)


def pick_tile(buffer, sources, tiles, step):
    for k, source in enumerate(sources):

        @pl.when(step // tiles == k)
        def _():
            buffer[...] = source[...]


def owner_body(n_piece, tiles, part, own, hid, replicas, where, *refs):
    grads = refs[:n_piece]
    this, other, gate_out, back_out, weights, buffer = refs[n_piece:]
    width = weights.shape[0]
    step = pl.program_id(0)

    @pl.when(step == 0)
    def _():
        for z in range(this.shape[0]):
            for k, source in enumerate((this, other)):
                at = pl.multiple_of((2 * z + ((where[0] & 1) ^ k)) * part, part)
                weights[pl.ds(at, part), :] = source[z]

    pick_tile(buffer, grads, tiles, step)
    extra = buffer[:, width:].astype(FULL)
    lane = lax.broadcasted_iota(jnp.int32, extra.shape, 1)
    gate = pltpu.roll(extra, LANES - TOP, 1) + pltpu.roll(extra, LANES - 2 * TOP, 1)
    first = where[0] // replicas * own
    back = mul(buffer[:, :width], weights[...])
    table = jnp.zeros(extra.shape, FULL)
    for j in range(own):
        hit = (lane < TOP) & (extra == (first + j).astype(FULL))
        column = jnp.sum(jnp.where(hit, gate, 0.0), axis=1, keepdims=True)
        table = jnp.where(lane == j, column, table)
        back_out[:, j * hid : (j + 1) * hid] = back[:, j * hid : (j + 1) * hid] * column
    gate_out[...] = table


def expert_body(n_piece, tiles, own, hid, where, *refs):
    rows = refs[:n_piece]
    gate_rows, up_rows, gate, back, grad_hidden, active_out, grad_gate, grad_up, buffer = refs[
        n_piece:
    ]
    pick_tile(buffer, rows, tiles, pl.program_id(0))
    gate_pre = mul(buffer[...], gate_rows[...])
    up_pre = mul(buffer[...], up_rows[...])
    for j in range(own):
        at = slice(j * hid, (j + 1) * hid)
        pre, up = gate_pre[:, at], up_pre[:, at]
        squash = 1.0 / (1.0 + jnp.exp(-pre))
        silu = pre * squash
        active = (silu * up).astype(LOW).astype(FULL)
        active_out[:, at] = (active * gate[:, j : j + 1]).astype(LOW)
        d = back[:, at]
        grad_gate[:, at] = (d * up * squash * (1.0 + pre * (1.0 - squash))).astype(LOW)
        grad_up[:, at] = (d * silu).astype(LOW)
    product = mul(grad_gate[...], gate_rows[...], COLS_ON_COLS)
    product = product + mul(grad_up[...], up_rows[...], COLS_ON_COLS)
    grad_hidden[...] = product.astype(grad_hidden.dtype)


def out_body(where, active, weights, out):
    out[...] = mul(active[...], weights[...], COLS_ON_COLS).astype(out.dtype)


def weight_grad_body(n_source, where, *refs):
    sources = refs[:n_source]
    column = refs[-1]
    count = (len(refs) - 1 - n_source) // 3
    rights, outs = refs[n_source : n_source + 2 * count], refs[n_source + 2 * count : -1]
    size = sources[0].shape[0]
    for k, source in enumerate(sources):
        column[k * size : (k + 1) * size, :] = source[...]
    half = column.shape[0] // 2
    for k, out in enumerate(outs):
        total = mul(column[:half], rights[2 * k][...], ROWS_ON_ROWS)
        out[...] = (total + mul(column[half:], rights[2 * k + 1][...], ROWS_ON_ROWS)).astype(LOW)


def middle_back_body(where, *refs):
    kept, got, middle, grad, gain, grad_middle, low, gain_part = refs
    total = kept[...] + got[...].astype(FULL)
    m = middle[...]
    scale = lax.rsqrt(jnp.mean(m * m, axis=1, keepdims=True) + EPS)
    gain_part[...] = jnp.broadcast_to(
        jnp.sum(total * m * scale, axis=0, keepdims=True), gain_part.shape
    )
    weighted = total * gain[1:2, :]
    inner = jnp.mean(weighted * m, axis=1, keepdims=True)
    back = grad[...].astype(FULL) + (scale * weighted - m * (scale * scale * scale) * inner)
    grad_middle[...] = back
    low[...] = back.astype(LOW)


def attend_back_body(n_piece, q_cols, k_cols, rows, part, order, orders, where, *refs):
    pieces = refs[:n_piece]
    mixed, out_weights, qkv_in, doc_row, doc_col, cosine, sine, hidden, weights = refs[
        n_piece : n_piece + 9
    ]
    kept, sent, first_kept, first_sent, branch, natural, grad_qkv, grads = refs[n_piece + 9 :]
    for k in range(n_piece):
        branch[k * rows : (k + 1) * rows, :] = pieces[k][...]
    grad_mixed = mul(branch[...], out_weights[...]).astype(LOW)
    for k, m in enumerate(order):
        at = pl.multiple_of((where[1] ^ m) * rows, rows)
        natural[pl.ds(at, rows), :q_cols] = grad_mixed[k * rows : (k + 1) * rows]
    qk = q_cols + k_cols
    total = qk + k_cols
    grads[:, total:] = mul(branch[...], mixed[...], ROWS_ON_ROWS)
    allowed = admitted(doc_row[...], doc_col[...])
    per_group = q_cols // k_cols
    query_grads, key_grads, value_grads = [], [], []
    for g in range(k_cols // HEAD_SIZE):
        key = qkv_in[:, q_cols + g * HEAD_SIZE : q_cols + (g + 1) * HEAD_SIZE]
        value = qkv_in[:, qk + g * HEAD_SIZE : qk + (g + 1) * HEAD_SIZE]
        key_grad = value_grad = None
        for h in range(g * per_group, (g + 1) * per_group):
            at = slice(h * HEAD_SIZE, (h + 1) * HEAD_SIZE)
            query = qkv_in[:, at]
            shares = softmax_of(query, key, allowed)
            grad = natural[:, at]
            grad_shares = mul(grad, value, COLS_ON_COLS)
            inner = jnp.sum(shares * grad_shares, axis=1, keepdims=True)
            grad_scores = (shares * (grad_shares - inner)).astype(LOW)
            query_grads.append(mul(grad_scores, key))
            dk = mul(grad_scores, query, ROWS_ON_ROWS)
            dv = mul(shares.astype(LOW), grad, ROWS_ON_ROWS)
            key_grad = dk if key_grad is None else key_grad + dk
            value_grad = dv if value_grad is None else value_grad + dv
        key_grads.append(key_grad)
        value_grads.append(value_grad)
    turned = jnp.concatenate(query_grads + key_grads, axis=1) * HEAD_SIZE**-0.5
    grad_qkv[:, :qk] = rotate(turned, cosine[...], -sine[...]).astype(LOW)
    grad_qkv[:, qk:] = jnp.concatenate(value_grads, axis=1).astype(LOW)
    grads[:, :total] = mul(hidden[...], grad_qkv[...], ROWS_ON_ROWS)
    for p, (even, odd) in enumerate(zip(*orders)):
        at = pl.multiple_of((where[0] ^ jnp.where(where[1] & 1 == 0, even, odd)) * part, part)
        target = kept if p < len(orders[0]) // 2 else sent
        k = p % (len(orders[0]) // 2)
        target[k * part : (k + 1) * part, :] = grads[pl.ds(at, part), :].astype(target.dtype)
    for k, m in enumerate(order):
        at = pl.multiple_of((where[1] ^ m) * rows, rows)
        natural[k * rows : (k + 1) * rows, :total] = grad_qkv[pl.ds(at, rows), :]
    product = mul(natural[:, :total], weights[...], COLS_ON_COLS)
    half = first_kept.shape[0]
    first_kept[...] = product[:half]
    first_sent[...] = product[half:].astype(LOW)


def tokens_back_body(rows, where, tokens, kept, got, gain, grad_middle, moe_part, out):
    at = pl.multiple_of(where[1] * rows, rows)
    x = tokens[pl.ds(at, rows), :].astype(FULL)
    scale = lax.rsqrt(jnp.mean(x * x, axis=1, keepdims=True) + EPS)
    first = kept[...] + got[...].astype(FULL)
    attn_part = jnp.sum(first * x * scale, axis=0, keepdims=True)
    weighted = first * gain[0:1, :]
    inner = jnp.mean(weighted * x, axis=1, keepdims=True)
    out[:rows] = grad_middle[...] + (scale * weighted - x * (scale * scale * scale) * inner)
    line = lax.broadcasted_iota(jnp.int32, moe_part.shape, 0)
    out[rows:] = jnp.where(line == 0, attn_part, jnp.where(line == 1, moe_part[...], 0.0))


def unpack_body(own, hid, replicas, turn, where, this, other, out):
    side = where[0] & 1
    for j in range(own):
        pieces = [source[0, :, j * hid : (j + 1) * hid].astype(FULL) for source in (this, other)]
        pieces = [piece.T for piece in pieces] if turn else pieces
        if replicas == 1:
            out[side * own + j] = pieces[0]
            out[(1 - side) * own + j] = pieces[1]
        else:
            first = 2 * pl.program_id(0) % replicas == 0
            out[j] = pieces[0] + pieces[1] + jnp.where(first, 0.0, out[j])


def local(
    tokens,
    cotangent,
    segments,
    routes,
    gates,
    w_query,
    key_projection,
    value_projection,
    w_out,
    gain_attn,
    gain_moe,
    w_gate,
    w_up,
    w_down,
):
    n_e, n_t = lax.axis_size("expert"), lax.axis_size("tensor")
    e, t = lax.axis_index("expert"), lax.axis_index("tensor")
    where = jnp.stack([e, t]).astype(jnp.int32)
    replicas = max(1, n_e // EXPERTS)
    own_experts = EXPERTS * replicas // n_e
    first_bit = replicas.bit_length() - 1
    length, width = tokens.shape
    part = width // n_e
    rows = length // n_t
    q_cols, k_cols = w_query.shape[1], key_projection.shape[1]
    qkv_cols = q_cols + 2 * k_cols
    hidden = w_gate.shape[2]
    wide = own_experts * hidden

    pad = 16
    gain_rows = jnp.stack([gain_attn, gain_moe])
    gain_rows = jnp.pad(gain_rows, ((0, pad - 2), (0, qkv_cols - part)))
    qkv_shard = jnp.concatenate(
        [
            jnp.concatenate([w_query, key_projection, value_projection], axis=1),
            gain_rows,
        ],
        axis=0,
    ).astype(LOW)
    out_shard = w_out.T.astype(LOW)

    e_bits, t_bits = bits_of(n_e), bits_of(n_t)
    even_bits, odd_bits = e_bits, e_bits[-1:] + e_bits[:-1]
    orders = order_of(even_bits), order_of(odd_bits)
    by_parity = [(("expert", a), ("expert", b)) for a, b in zip(even_bits, odd_bits)]

    def every(shard, before_last):
        came = []
        for even, odd in by_parity[:-1]:
            came.append(swap_by_parity(shard, even, odd))
            shard = jnp.concatenate([shard, came[-1]])
        shard, *before_last = lax.optimization_barrier((shard, *before_last))
        came.append(swap_by_parity(shard, *by_parity[-1]))
        return [shard, came[-1]], came, before_last

    pairs = n_e // 2
    turn = part % LANES == 0
    pair_experts = 2 * own_experts // replicas or 1
    at_pair = lambda dims: pl.BlockSpec(
        (pair_experts,) + dims, lambda z: (2 * z // max(2, replicas), 0, 0)
    )
    sources = [w_gate, w_up, w_down if turn else w_down.transpose(0, 2, 1)]
    sided = pl.BlockSpec((1, part, wide), lambda z: (z, 0, 0))
    packed = call(
        functools.partial(pack_body, own_experts, hidden, replicas, turn),
        [shape((pairs, 2, part, wide), LOW)] + [shape((pairs, part, wide), LOW)] * 4,
        where, *sources,
        grid=(pairs,),
        in_specs=[at_pair(w.shape[1:]) for w in sources],
        out_specs=[pl.BlockSpec((1, 2, part, wide), lambda z: (z, 0, 0, 0))] + [sided] * 4,
    )
    side = e & 1
    lines = [[z * 2 + k for z in range(n_e // 2)] for k in range(2)]

    def along(blocks):
        return lax.all_to_all(
            blocks, "expert", 0, 0, tiled=True, axis_index_groups=lines
        )

    def sides(blocks):
        this = lax.dynamic_index_in_dim(blocks, side, 1, keepdims=False)
        return this, lax.dynamic_index_in_dim(blocks, 1 - side, 1, keepdims=False)

    def to_neighbour(this, other, *earlier):
        got = swap(after(other, *earlier), "expert", 1)
        return jnp.where(
            side == 0, jnp.concatenate([this, got], axis=1), jnp.concatenate([got, this], axis=1)
        )

    def from_neighbour(blocks, *earlier):
        blocks = along(after(blocks.reshape(n_e // 2, 2 * part, wide), *earlier))
        this, other = sides(blocks.reshape(n_e // 2, 2, part, wide))
        return this, swap(other, "expert", 1)

    qkv_arrays, qkv_came, packed = every(qkv_shard, packed)
    out_arrays, _, _ = every(after(out_shard, qkv_came[0]), ())
    down_this, down_other = from_neighbour(packed[0], qkv_came[-1])
    near = [to_neighbour(*packed[k : k + 2], qkv_came[-1]) for k in (1, 3)]
    pitch = part + pad
    gains = jnp.zeros((pad, LANES), FULL)
    if part % LANES:
        held = jnp.concatenate(
            [a.reshape(-1, pitch, qkv_cols)[:, part:, :part] for a in qkv_arrays]
        ).astype(FULL)
        on_even = [position_in(e ^ k, even_bits) for k in range(n_e)]
        on_odd = [position_in(e ^ k, odd_bits) for k in range(n_e)]
        gains = jnp.concatenate(
            [
                lax.dynamic_index_in_dim(held, jnp.where(t & 1 == 0, a, b), 0, keepdims=False)
                for a, b in zip(on_even, on_odd)
            ],
            axis=1,
        )

    e_path = [("expert", b) for b in bits_of(n_e, first_bit)]
    t_path = [("tensor", b) for b in t_bits]
    even_path, odd_path = e_path + t_path[:-1], e_path[:-1] + t_path[:-1] + e_path[-1:]
    path = list(zip(even_path, odd_path))
    last = t_path[-1]

    def gather_tokens(field, ties=()):
        came = []
        for even, odd in path:
            if len(came) == 2 and ties:
                field = after(field, *ties)
            came.append(swap_by_parity(field, even, odd))
            pieces = [field, came[-1]]
            field = jnp.concatenate(pieces)
        return pieces + [swap(p, *last) for p in pieces], came

    def scatter_tokens(kept, sent, ties):
        total = kept + swap(sent, *last).astype(FULL)
        came = []
        for even, odd in reversed(path):
            half = total.shape[0] // 2
            kept, sent = total[:half], total[half:].astype(LOW)
            if len(came) < len(ties) and ties[len(came)]:
                sent = after(sent, *ties[len(came)])
            came.append(swap_by_parity(sent, even, odd))
            total = kept + came[-1].astype(FULL)
        return kept, came

    own = t * rows
    grad_rows = lax.dynamic_slice_in_dim(cotangent, own, rows, 0)
    gate_rows = lax.dynamic_slice_in_dim(gates, own, rows, 0)
    route_rows = lax.dynamic_slice_in_dim(routes, own, rows, 0)
    gate_high = gate_rows.astype(LOW)
    gate_rest = (gate_rows - gate_high.astype(FULL)).astype(LOW)
    extra = jnp.concatenate([route_rows.astype(LOW), gate_high, gate_rest], axis=1)
    extra = jnp.pad(extra, ((0, 0), (0, LANES - 3 * TOP)))
    grad_pieces, _ = gather_tokens(after(jnp.concatenate([grad_rows, extra], axis=1), out_arrays[-1]))

    documents = segments[0]
    doc_row, doc_col = documents[None, :], documents[:, None]
    index = jnp.arange(length)
    same = (index[None, :] < index[:, None]) & (doc_row == doc_col)
    position = jnp.sum(same.astype(FULL), axis=1, keepdims=True)
    lane = jnp.arange(LANES)
    freqs = THETA ** (-2.0 * (lane % (HEAD_SIZE // 2)).astype(FULL) / HEAD_SIZE)
    angle = position * freqs[None, :]
    cosine = jnp.cos(angle)
    sine = jnp.sin(angle) * jnp.where(lane % HEAD_SIZE < HEAD_SIZE // 2, -1.0, 1.0)[None, :]
    t_masks = t_bits[::-1]
    order = order_of(t_bits)
    weights, first_hidden, qkv, mixed, gains = call(
        functools.partial(attend_body, orders, 2, part, pitch, q_cols, k_cols, rows, order),
        [
            shape((width, qkv_cols), LOW),
            shape((length, width), LOW),
            shape((length, qkv_cols), LOW),
            shape((length, q_cols), LOW),
            shape((pad, width), FULL),
        ],
        where, *qkv_arrays, tokens, gains, doc_row, doc_col, cosine, sine,
        scratch=[pltpu.VMEM((length, q_cols), LOW)],
        flops=2 * length * (width * qkv_cols + 2 * length * q_cols),
    )
    out_weights, kept, sent = call(
        functools.partial(branch_body, orders, 2, part),
        [
            shape((width, q_cols), LOW),
            shape((length // 2, width), FULL),
            shape((length // 2, width), LOW),
        ],
        where, *out_arrays, mixed,
        flops=2 * length * width * q_cols,
    )

    def all_rows(field):
        size = field.shape[0]
        for b in t_bits:
            field = jnp.concatenate([field, swap(field, "tensor", b)])
        at = [position_in(t ^ k, t_bits) * size for k in range(n_t)]
        return jnp.concatenate([lax.dynamic_slice_in_dim(field, a, size, 0) for a in at])

    def scatter_rows(kept, sent):
        for b in t_masks[:-1]:
            total = kept + swap(sent, "tensor", b).astype(FULL)
            half = total.shape[0] // 2
            kept, sent = total[:half], total[half:].astype(LOW)
        return kept, swap(sent, "tensor", t_masks[-1])

    kept, got = scatter_rows(kept, sent)
    middle, second_hidden = call(
        functools.partial(middle_body, rows),
        [shape((rows, width), FULL), shape((rows, width), LOW)],
        where, tokens, kept, got, gains,
    )

    size = 256
    total_rows = sum(p.shape[0] for p in grad_pieces)
    steps = total_rows // size
    whole = lambda a: pl.BlockSpec(a.shape, lambda i: (0,) * a.ndim)
    tile = lambda cols: pl.BlockSpec((size, cols), lambda i: (i, 0))

    def tiles_of(pieces):
        count = pieces[0].shape[0] // size
        return count, [
            pl.BlockSpec((size, p.shape[1]), lambda i, k=k: (jnp.clip(i - k * count, 0, count - 1), 0))
            for k, p in enumerate(pieces)
        ]

    tiles, specs = tiles_of(grad_pieces)
    gate_table, back, down_rows = call(
        functools.partial(owner_body, len(grad_pieces), tiles, part, own_experts, hidden, replicas),
        [
            shape((total_rows, LANES), FULL),
            shape((total_rows, wide), FULL),
            shape((width, wide), LOW),
        ],
        where, *grad_pieces, down_this, down_other,
        grid=(steps,),
        in_specs=specs + [whole(down_this), whole(down_other)],
        out_specs=[tile(LANES), tile(wide), pl.BlockSpec((width, wide), lambda i: (0, 0))],
        scratch=[pltpu.VMEM((size, width + LANES), LOW)],
        flops=2 * total_rows * width * wide,
    )
    hidden_pieces, hidden_came = gather_tokens(second_hidden, [down_other, *near])
    gate_rows, up_rows = (
        along(after(p, hidden_came[1])).reshape(width, wide) for p in near
    )
    half = steps // 2

    def experts(chosen, first, out_type):
        later = lambda cols: pl.BlockSpec((size, cols), lambda i: (i + first, 0))
        tiles, specs = tiles_of(chosen)
        return call(
            functools.partial(expert_body, len(chosen), tiles, own_experts, hidden),
            [
                shape((half * size, width), out_type),
                shape((half * size, wide), LOW),
                shape((half * size, wide), LOW),
                shape((half * size, wide), LOW),
            ],
            where, *chosen, gate_rows, up_rows, gate_table, back,
            grid=(half,),
            in_specs=specs
            + [whole(gate_rows), whole(up_rows), later(LANES), later(wide)],
            out_specs=[tile(width), tile(wide), tile(wide), tile(wide)],
            scratch=[pltpu.VMEM((size, width), LOW)],
            flops=2 * half * size * width * 4 * wide,
        )

    sent_hidden, *sent_right = experts(hidden_pieces[2:], half, LOW)
    kept_hidden, *kept_right = experts(hidden_pieces[:2], 0, FULL)

    block = 256
    column = lambda a: pl.BlockSpec((a.shape[0], block), lambda i: (0, i))

    def weight_grad(sources, chosen):
        rights = [side[k] for k in chosen for side in (kept_right, sent_right)]
        return call(
            functools.partial(weight_grad_body, len(sources)),
            [shape((width, wide), LOW)] * len(chosen),
            where, *sources, *rights,
            grid=(width // block,),
            in_specs=[column(a) for a in sources] + [whole(a) for a in rights],
            out_specs=[pl.BlockSpec((block, wide), lambda i: (i, 0))] * len(chosen),
            scratch=[pltpu.VMEM((total_rows, block), LOW)],
            flops=2 * total_rows * width * wide * len(chosen),
        )

    (down_grad,) = weight_grad(grad_pieces, [0])
    gate_grad, up_grad = weight_grad(hidden_pieces, [1, 2])
    down_back = from_neighbour(down_grad)
    def down(active, out_type):
        return call(
            out_body,
            [shape((half * size, width), out_type)],
            where, active, down_rows,
            grid=(half,),
            in_specs=[tile(wide), whole(down_rows)],
            out_specs=[tile(width)],
            flops=2 * half * size * width * wide,
        )[0]

    sent_out = down(after(sent_right[0], up_grad), LOW)
    kept_out = down(after(kept_right[0], up_grad), FULL)
    grad_kept, grad_came = scatter_tokens(
        kept_hidden, sent_hidden, [(), (down_grad,), (down_back[0], gate_grad, kept_out, sent_out)]
    )
    grad_got = grad_came[-1]
    out_kept, out_came = scatter_tokens(kept_out, sent_out, [(grad_came[1],)])
    out_got = out_came[-1]
    output_rows = (middle + (out_kept + out_got.astype(FULL))).astype(LOW)
    output = all_rows(output_rows)

    grad_middle, branch_grad, moe_part = call(
        middle_back_body,
        [shape((rows, width), FULL), shape((rows, width), LOW), shape((16, width), FULL)],
        where, after(grad_kept, out_came[0]), grad_got, middle, grad_rows, gains,
    )
    branch_pieces = [branch_grad]
    for b in reversed(t_masks):
        branch_pieces = branch_pieces + [swap(p, "tensor", b) for p in branch_pieces]
    all_cols = qkv_cols + q_cols
    kept_w, sent_w, first_kept, first_sent = call(
        functools.partial(
            attend_back_body, len(branch_pieces), q_cols, k_cols, rows, part, order, orders
        ),
        [
            shape((width // 2, all_cols), FULL),
            shape((width // 2, all_cols), LOW),
            shape((length // 2, width), FULL),
            shape((length // 2, width), LOW),
        ],
        where, *branch_pieces[:-1], after(branch_pieces[-1], out_came[1]), mixed, out_weights, qkv, doc_row, doc_col, cosine, sine,
        first_hidden, weights,
        scratch=[
            pltpu.VMEM((length, width), LOW),
            pltpu.VMEM((length, max(q_cols, qkv_cols)), LOW),
            pltpu.VMEM((length, qkv_cols), LOW),
            pltpu.VMEM((width, all_cols), FULL),
        ],
        flops=2 * length * width * (2 * q_cols + 2 * qkv_cols),
    )
    attn_came = []
    for even, odd in reversed(by_parity):
        attn_came.append(swap_by_parity(sent_w, even, odd))
        attn_grad = kept_w + attn_came[-1].astype(FULL)
        half_rows = attn_grad.shape[0] // 2
        kept_w, sent_w = attn_grad[:half_rows], attn_grad[half_rows:].astype(LOW)

    gate_back = from_neighbour(gate_grad, grad_got)
    returned = [
        gate_back,
        from_neighbour(up_grad, gate_back[0]),
        down_back,
    ]

    out_dims = [(part, hidden), (part, hidden), (hidden, part) if turn else (part, hidden)]

    def unpack(pair, dims, turned):
        source = pl.BlockSpec((1, part, wide), lambda z: (z, 0, 0))
        return call(
            functools.partial(unpack_body, own_experts, hidden, replicas, turned),
            [shape((EXPERTS,) + dims, FULL)],
            where, *pair,
            grid=(n_e // 2,),
            in_specs=[source, source],
            out_specs=[at_pair(dims)],
        )[0]

    shards = [unpack(p, d, turn and i == 2) for i, (p, d) in enumerate(zip(returned, out_dims))]
    gate_shard, up_shard, down_shard = shards
    if not turn:
        down_shard = down_shard.transpose(0, 2, 1)

    kept, got = scatter_rows(first_kept, first_sent)
    (token_rows,) = call(
        functools.partial(tokens_back_body, rows),
        [shape((rows + 16, width), FULL)],
        where, tokens, kept, after(got, attn_came[0], gate_back[0]), gains, grad_middle, moe_part,
    )
    gathered = all_rows(token_rows.astype(LOW))
    gathered = gathered.reshape(n_t, rows + 16, width).astype(FULL)
    grad_input = gathered[:, :rows].reshape(length, width)
    gain_sum = jnp.sum(gathered[:, rows : rows + 2], axis=0)

    def gain_block(m):
        return lax.dynamic_slice_in_dim(gain_sum, (e ^ m) * part, part, 1)

    lines = jnp.stack([gain_block(m) for m in order_of(e_bits)])
    for b in reversed(e_bits):
        half_rows = lines.shape[0] // 2
        lines = lines[:half_rows] + swap(lines[half_rows:], "expert", b)
    gain_grads = lines[0]
    return (
        output,
        grad_input,
        attn_grad[:, :q_cols],
        attn_grad[:, q_cols : q_cols + k_cols],
        attn_grad[:, q_cols + k_cols : qkv_cols],
        attn_grad[:, qkv_cols:].T,
        gain_grads[0],
        gain_grads[1],
        gate_shard,
        up_shard,
        down_shard,
    )


def solution(mesh):
    by_rows = P("expert", None)
    by_both = P("expert", "tensor")
    in_experts = P(None, "expert", "tensor")
    down_specs = P(None, "tensor", "expert")
    return jax.shard_map(
        local,
        mesh=mesh,
        in_specs=(by_rows,) * 5
        + (by_both,) * 3
        + (P("tensor", "expert"), P("expert"), P("expert"), in_experts, in_experts, down_specs),
        out_specs=(by_rows, by_rows)
        + (by_both,) * 3
        + (P("tensor", "expert"), P("expert"), P("expert"), in_experts, in_experts, down_specs),
        check_vma=False,
    )
```

```python
import functools

import jax
import jax.numpy as jnp
from jax import lax
from jax.experimental import pallas as pl
from jax.experimental.pallas import tpu as pltpu
from jax.sharding import PartitionSpec as P

HEAD_SIZE = 64
EXPERTS = 32
TOP = 8
EPS = 1e-06
THETA = 10000.0
MASKED = -1e30
LANES = 128
LIMIT = 24 * 1024 * 1024
LARGE = 56 * 1024 * 1024

LOW = jnp.bfloat16
FULL = jnp.float32
ROWS_ON_ROWS = (((0,), (0,)), ((), ()))
COLS_ON_ROWS = (((1,), (0,)), ((), ()))
COLS_ON_COLS = (((1,), (1,)), ((), ()))


def mul(left, right, dims=COLS_ON_ROWS):
    return lax.dot_general(left, right, dims, preferred_element_type=FULL)


def shape(dims, dtype):
    return jax.ShapeDtypeStruct(dims, dtype)


def call(body, outs, *args, grid=None, in_specs=None, out_specs=None, scratch=(), flops=0, limit=LIMIT):
    size = sum(a.size * a.dtype.itemsize for a in args)
    size += sum(o.size * jnp.dtype(o.dtype).itemsize for o in outs)
    whole = pl.BlockSpec(memory_space=pltpu.VMEM)
    if in_specs is None:
        in_specs = [whole] * (len(args) - 1)
    if out_specs is None:
        out_specs = [whole] * len(outs)
    extra = {} if grid is None else {"grid": grid}
    return pl.pallas_call(
        body,
        out_shape=list(outs),
        in_specs=[pl.BlockSpec(memory_space=pltpu.SMEM)] + list(in_specs),
        out_specs=list(out_specs),
        scratch_shapes=list(scratch),
        compiler_params=pltpu.CompilerParams(vmem_limit_bytes=limit),
        cost_estimate=pl.CostEstimate(flops=flops, bytes_accessed=size, transcendentals=0),
        **extra,
    )(*args)


def swap(field, axis, mask):
    count = lax.axis_size(axis)
    return lax.ppermute(field, axis, [(i, i ^ mask) for i in range(count)])


def after(field, *earlier):
    return lax.optimization_barrier((field, *earlier))[0]


def swap_by_parity(field, even, odd):
    n_e, n_t = lax.axis_size("expert"), lax.axis_size("tensor")
    pairs = []
    for e in range(n_e):
        for t in range(n_t):
            axis, mask = odd if t & 1 else even
            to = ((e ^ mask) * n_t + t) if axis == "expert" else (e * n_t + (t ^ mask))
            pairs.append((e * n_t + t, to))
    return lax.ppermute(field, ("expert", "tensor"), pairs)


def bits_of(count, first_bit=0):
    return [1 << b for b in reversed(range(first_bit, count.bit_length() - 1))]


def position_in(mask, bits):
    return sum(jnp.where(mask & b != 0, 1 << i, 0) for i, b in enumerate(bits))


def order_of(bits):
    order = [0]
    for b in bits:
        order = order + [k ^ b for k in order]
    return order


def rotate(field, cosine, sine):
    lane = lax.broadcasted_iota(jnp.int32, (field.shape[0], LANES), 1)
    low_half = lane % HEAD_SIZE < HEAD_SIZE // 2
    turned = []
    for at in range(0, field.shape[1], LANES):
        block = field[:, at : at + LANES]
        ahead = pltpu.roll(block, LANES - HEAD_SIZE // 2, 1)
        behind = pltpu.roll(block, HEAD_SIZE // 2, 1)
        turned.append(block * cosine + jnp.where(low_half, ahead, behind) * sine)
    return jnp.concatenate(turned, axis=1)


def admitted(doc_row, doc_col):
    length = doc_row.shape[1]
    row = lax.broadcasted_iota(jnp.int32, (length, length), 0)
    col = lax.broadcasted_iota(jnp.int32, (length, length), 1)
    return (col <= row) & (doc_row == doc_col)


def softmax_of(query, key, allowed):
    scores = mul(query, key, COLS_ON_COLS) * HEAD_SIZE**-0.5
    scores = jnp.where(allowed, scores, MASKED)
    raised = jnp.exp(scores - jnp.max(scores, axis=1, keepdims=True))
    return raised / jnp.sum(raised, axis=1, keepdims=True)


def place_rows(target, sources, orders, where, part, pitch):
    count = len(orders[0]) // len(sources)
    for p, (even, odd) in enumerate(zip(*orders)):
        at = pl.multiple_of((where[0] ^ jnp.where(where[1] & 1 == 0, even, odd)) * part, part)
        k = p % count * pitch
        target[pl.ds(at, part), :] = sources[p // count][k : k + part, :]


def pack_body(own, hid, replicas, turn, where, gate, up, down, down_out, *sided):
    side = where[0] & 1
    for j in range(own):
        at = slice(j * hid, (j + 1) * hid)
        for k in range(2):
            block = down[(k * own if replicas == 1 else 0) + j]
            down_out[0, k, :, at] = (block.T if turn else block).astype(LOW)
            place = ((side ^ k) * own if replicas == 1 else 0) + j
            sided[k][0, :, at] = gate[place].astype(LOW)
            up_at = slice((own + j) * hid, (own + j + 1) * hid)
            sided[k][0, :, up_at] = up[place].astype(LOW)


def attend_body(orders, n, part, pitch, q_cols, k_cols, rows, order, where, *refs):
    sources = refs[:n]
    tokens, gain_in, doc_row, doc_col, cosine, sine = refs[n : n + 6]
    weights, hidden, qkv_out, mixed_out, gain, kept, sent, mixed = refs[n + 6 :]
    place_rows(weights, sources, orders, where, part, pitch)
    if part % LANES == 0:
        count = len(orders[0]) // n
        for p, (even, odd) in enumerate(zip(*orders)):
            at = pl.multiple_of((where[0] ^ jnp.where(where[1] & 1 == 0, even, odd)) * part, part)
            k = p % count * pitch + part
            gain[:, pl.ds(at, part)] = sources[p // count][k : k + gain.shape[0], :part].astype(FULL)
    else:
        gain[...] = gain_in[...]
    x = tokens[...].astype(FULL)
    scale = lax.rsqrt(jnp.mean(x * x, axis=1, keepdims=True) + EPS)
    first = (x * scale * gain[0:1, :]).astype(LOW)
    hidden[...] = first
    qkv = mul(first, weights[:, : q_cols + 2 * k_cols])
    turned = rotate(qkv[:, : q_cols + k_cols], cosine[...], sine[...]).astype(LOW)
    values = qkv[:, q_cols + k_cols :].astype(LOW)
    qkv_out[:, : q_cols + k_cols] = turned
    qkv_out[:, q_cols + k_cols :] = values
    allowed = admitted(doc_row[...], doc_col[...])
    per_group = q_cols // k_cols
    for h in range(q_cols // HEAD_SIZE):
        at, g = h * HEAD_SIZE, h // per_group * HEAD_SIZE
        shares = softmax_of(
            turned[:, at : at + HEAD_SIZE],
            turned[:, q_cols + g : q_cols + g + HEAD_SIZE],
            allowed,
        ).astype(LOW)
        mixed[:, at : at + HEAD_SIZE] = mul(shares, values[:, g : g + HEAD_SIZE]).astype(LOW)
    for k, m in enumerate(order):
        at = pl.multiple_of((where[1] ^ m) * rows, rows)
        mixed_out[k * rows : (k + 1) * rows, :] = mixed[pl.ds(at, rows), :]
    product = mul(mixed_out[...], weights[:, q_cols + 2 * k_cols :], COLS_ON_COLS)
    half = kept.shape[0]
    kept[...] = product[:half]
    sent[...] = product[half:].astype(LOW)


def middle_body(rows, where, tokens, kept, got, gain, middle, hidden):
    at = pl.multiple_of(where[1] * rows, rows)
    m = tokens[pl.ds(at, rows), :].astype(FULL) + (kept[...] + got[...].astype(FULL))
    middle[...] = m
    scale = lax.rsqrt(jnp.mean(m * m, axis=1, keepdims=True) + EPS)
    hidden[...] = (m * scale * gain[1:2, :]).astype(LOW)


def pick_tile(buffer, sources, tiles, step):
    for k, source in enumerate(sources):

        @pl.when(step // tiles == k)
        def _():
            buffer[...] = source[...]


def owner_body(n_piece, tiles, part, own, hid, replicas, where, *refs):
    grads = refs[:n_piece]
    this, other, gate_out, back_out, weights, buffer = refs[n_piece:]
    width = weights.shape[0]
    step = pl.program_id(0)

    @pl.when(step == 0)
    def _():
        for z in range(this.shape[0]):
            for k, source in enumerate((this, other)):
                at = pl.multiple_of((2 * z + ((where[0] & 1) ^ k)) * part, part)
                weights[pl.ds(at, part), :] = source[z]

    pick_tile(buffer, grads, tiles, step)
    extra = buffer[:, width:].astype(FULL)
    lane = lax.broadcasted_iota(jnp.int32, extra.shape, 1)
    gate = pltpu.roll(extra, LANES - TOP, 1) + pltpu.roll(extra, LANES - 2 * TOP, 1)
    first = where[0] // replicas * own
    back = mul(buffer[:, :width], weights[...])
    table = jnp.zeros(extra.shape, FULL)
    for j in range(own):
        hit = (lane < TOP) & (extra == (first + j).astype(FULL))
        column = jnp.sum(jnp.where(hit, gate, 0.0), axis=1, keepdims=True)
        table = jnp.where(lane == j, column, table)
        back_out[:, j * hid : (j + 1) * hid] = back[:, j * hid : (j + 1) * hid] * column
    gate_out[...] = table


def expert_body(n_piece, tiles, own, hid, where, *refs):
    rows = refs[:n_piece]
    weights, gate, back, grad_hidden, active_out, grad_both, buffer = refs[n_piece:]
    pick_tile(buffer, rows, tiles, pl.program_id(0))
    wide = own * hid
    both = mul(buffer[...], weights[...])
    for j in range(own):
        at = slice(j * hid, (j + 1) * hid)
        up_at = slice(wide + j * hid, wide + (j + 1) * hid)
        pre, up = both[:, at], both[:, up_at]
        squash = 1.0 / (1.0 + jnp.exp(-pre))
        silu = pre * squash
        active = (silu * up).astype(LOW).astype(FULL)
        active_out[:, at] = (active * gate[:, j : j + 1]).astype(LOW)
        d = back[:, at]
        grad_both[:, at] = (d * up * squash * (1.0 + pre * (1.0 - squash))).astype(LOW)
        grad_both[:, up_at] = (d * silu).astype(LOW)
    product = mul(grad_both[...], weights[...], COLS_ON_COLS)
    grad_hidden[...] = product.astype(grad_hidden.dtype)


def out_body(where, active, weights, out):
    out[...] = mul(active[...], weights[...], COLS_ON_COLS).astype(out.dtype)


def weight_grad_body(n_source, part, where, *refs):
    sources = refs[:n_source]
    kept, sent, *outs, column, total = refs[n_source:]
    half, size = kept.shape[0], sources[0].shape[0]
    for k, source in enumerate(sources):
        column[k * size : (k + 1) * size, :] = source[...]
    product = mul(column[:half], kept[...], ROWS_ON_ROWS)
    total[...] = (product + mul(column[half:], sent[...], ROWS_ON_ROWS)).astype(LOW)
    for z in range(total.shape[0] // (2 * part)):
        for k in range(2):
            if len(outs) == 2:
                at = pl.multiple_of((2 * z + ((where[0] & 1) ^ k)) * part, part)
                outs[k][z] = total[pl.ds(at, part), :]
            else:
                at = (2 * z + k) * part
                outs[0][z, k] = total[at : at + part, :]


def middle_back_body(where, *refs):
    kept, got, middle, grad, gain, grad_middle, low, gain_part = refs
    total = kept[...] + got[...].astype(FULL)
    m = middle[...]
    scale = lax.rsqrt(jnp.mean(m * m, axis=1, keepdims=True) + EPS)
    gain_part[...] = jnp.broadcast_to(
        jnp.sum(total * m * scale, axis=0, keepdims=True), gain_part.shape
    )
    weighted = total * gain[1:2, :]
    inner = jnp.mean(weighted * m, axis=1, keepdims=True)
    back = grad[...].astype(FULL) + (scale * weighted - m * (scale * scale * scale) * inner)
    grad_middle[...] = back
    low[...] = back.astype(LOW)


def attend_back_body(n_piece, q_cols, k_cols, rows, part, order, orders, where, *refs):
    pieces = refs[:n_piece]
    mixed, qkv_in, doc_row, doc_col, cosine, sine, hidden, weights = refs[n_piece : n_piece + 8]
    kept, sent, first_kept, first_sent, branch, natural, grad_qkv, grads = refs[n_piece + 8 :]
    for k in range(n_piece):
        branch[k * rows : (k + 1) * rows, :] = pieces[k][...]
    grad_mixed = mul(branch[...], weights[:, q_cols + 2 * k_cols :]).astype(LOW)
    for k, m in enumerate(order):
        at = pl.multiple_of((where[1] ^ m) * rows, rows)
        natural[pl.ds(at, rows), :q_cols] = grad_mixed[k * rows : (k + 1) * rows]
    qk = q_cols + k_cols
    total = qk + k_cols
    grads[:, total:] = mul(branch[...], mixed[...], ROWS_ON_ROWS)
    allowed = admitted(doc_row[...], doc_col[...])
    per_group = q_cols // k_cols
    query_grads, key_grads, value_grads = [], [], []
    for g in range(k_cols // HEAD_SIZE):
        key = qkv_in[:, q_cols + g * HEAD_SIZE : q_cols + (g + 1) * HEAD_SIZE]
        value = qkv_in[:, qk + g * HEAD_SIZE : qk + (g + 1) * HEAD_SIZE]
        key_grad = value_grad = None
        for h in range(g * per_group, (g + 1) * per_group):
            at = slice(h * HEAD_SIZE, (h + 1) * HEAD_SIZE)
            query = qkv_in[:, at]
            shares = softmax_of(query, key, allowed)
            grad = natural[:, at]
            grad_shares = mul(grad, value, COLS_ON_COLS)
            inner = jnp.sum(shares * grad_shares, axis=1, keepdims=True)
            grad_scores = (shares * (grad_shares - inner)).astype(LOW)
            query_grads.append(mul(grad_scores, key))
            dk = mul(grad_scores, query, ROWS_ON_ROWS)
            dv = mul(shares.astype(LOW), grad, ROWS_ON_ROWS)
            key_grad = dk if key_grad is None else key_grad + dk
            value_grad = dv if value_grad is None else value_grad + dv
        key_grads.append(key_grad)
        value_grads.append(value_grad)
    turned = jnp.concatenate(query_grads + key_grads, axis=1) * HEAD_SIZE**-0.5
    grad_qkv[:, :qk] = rotate(turned, cosine[...], -sine[...]).astype(LOW)
    grad_qkv[:, qk:] = jnp.concatenate(value_grads, axis=1).astype(LOW)
    grads[:, :total] = mul(hidden[...], grad_qkv[...], ROWS_ON_ROWS)
    for p, (even, odd) in enumerate(zip(*orders)):
        at = pl.multiple_of((where[0] ^ jnp.where(where[1] & 1 == 0, even, odd)) * part, part)
        target = kept if p < len(orders[0]) // 2 else sent
        k = p % (len(orders[0]) // 2)
        target[k * part : (k + 1) * part, :] = grads[pl.ds(at, part), :].astype(target.dtype)
    for k, m in enumerate(order):
        at = pl.multiple_of((where[1] ^ m) * rows, rows)
        natural[k * rows : (k + 1) * rows, :total] = grad_qkv[pl.ds(at, rows), :]
    product = mul(natural[:, :total], weights[:, :total], COLS_ON_COLS)
    half = first_kept.shape[0]
    first_kept[...] = product[:half]
    first_sent[...] = product[half:].astype(LOW)


def tokens_back_body(rows, where, tokens, kept, got, gain, grad_middle, moe_part, out):
    at = pl.multiple_of(where[1] * rows, rows)
    x = tokens[pl.ds(at, rows), :].astype(FULL)
    scale = lax.rsqrt(jnp.mean(x * x, axis=1, keepdims=True) + EPS)
    first = kept[...] + got[...].astype(FULL)
    attn_part = jnp.sum(first * x * scale, axis=0, keepdims=True)
    weighted = first * gain[0:1, :]
    inner = jnp.mean(weighted * x, axis=1, keepdims=True)
    out[:rows] = grad_middle[...] + (scale * weighted - x * (scale * scale * scale) * inner)
    line = lax.broadcasted_iota(jnp.int32, moe_part.shape, 0)
    out[rows:] = jnp.where(line == 0, attn_part, jnp.where(line == 1, moe_part[...], 0.0))


def unpack_body(own, hid, replicas, turn, where, source, *outs):
    part = source.shape[0] // 2
    for k in range(own * len(outs)):
        out, j = outs[k // own], k % own
        cols = slice(k * hid, (k + 1) * hid)
        pieces = [source[i * part : (i + 1) * part, cols].astype(FULL) for i in range(2)]
        pieces = [piece.T for piece in pieces] if turn else pieces
        if replicas == 1:
            out[j] = pieces[0]
            out[own + j] = pieces[1]
        else:
            first = 2 * pl.program_id(0) % replicas == 0
            out[j] = pieces[0] + pieces[1] + jnp.where(first, 0.0, out[j])


def local(
    tokens,
    cotangent,
    segments,
    routes,
    gates,
    w_query,
    key_projection,
    value_projection,
    w_out,
    gain_attn,
    gain_moe,
    w_gate,
    w_up,
    w_down,
):
    n_e, n_t = lax.axis_size("expert"), lax.axis_size("tensor")
    e, t = lax.axis_index("expert"), lax.axis_index("tensor")
    where = jnp.stack([e, t]).astype(jnp.int32)
    replicas = max(1, n_e // EXPERTS)
    own_experts = EXPERTS * replicas // n_e
    first_bit = replicas.bit_length() - 1
    length, width = tokens.shape
    part = width // n_e
    rows = length // n_t
    q_cols, k_cols = w_query.shape[1], key_projection.shape[1]
    qkv_cols = q_cols + 2 * k_cols
    hidden = w_gate.shape[2]
    wide = own_experts * hidden

    pad = 16
    all_cols = qkv_cols + q_cols
    gain_rows = jnp.pad(jnp.stack([gain_attn, gain_moe]), ((0, pad - 2), (0, all_cols - part)))
    shard = jnp.concatenate([w_query, key_projection, value_projection, w_out.T], axis=1)
    shard = jnp.concatenate([shard, gain_rows]).astype(LOW)

    e_bits, t_bits = bits_of(n_e), bits_of(n_t)
    even_bits, odd_bits = e_bits, e_bits[-1:] + e_bits[:-1]
    orders = order_of(even_bits), order_of(odd_bits)
    by_parity = [(("expert", a), ("expert", b)) for a, b in zip(even_bits, odd_bits)]

    def every(shard, ready, later):
        came, sends = [], []
        for k, (even, odd) in enumerate(by_parity):
            if k == 1:
                shard, *ready = lax.optimization_barrier((shard, *ready))
            if k == 2:
                shard = after(shard, later)
            sends.append(shard)
            came.append(swap_by_parity(shard, even, odd))
            shard = jnp.concatenate([shard, came[-1]])
        return [sends[-1], came[-1]], came, sends, ready

    pairs = n_e // 2
    turn = part % LANES == 0
    pair_experts = 2 * own_experts // replicas or 1
    at_pair = lambda dims: pl.BlockSpec(
        (pair_experts,) + dims, lambda z: (2 * z // max(2, replicas), 0, 0)
    )
    sources = [w_gate, w_up, w_down if turn else w_down.transpose(0, 2, 1)]
    sided = pl.BlockSpec((1, part, 2 * wide), lambda z: (z, 0, 0))
    packed = call(
        functools.partial(pack_body, own_experts, hidden, replicas, turn),
        [shape((pairs, 2, part, wide), LOW)] + [shape((pairs, part, 2 * wide), LOW)] * 2,
        where, *sources,
        grid=(pairs,),
        in_specs=[at_pair(w.shape[1:]) for w in sources],
        out_specs=[pl.BlockSpec((1, 2, part, wide), lambda z: (z, 0, 0, 0))] + [sided] * 2,
    )
    side = e & 1
    lines = [[z * 2 + k for z in range(n_e // 2)] for k in range(2)]

    def along(blocks):
        return lax.all_to_all(
            blocks, "expert", 0, 0, tiled=True, axis_index_groups=lines
        )

    def from_neighbour(blocks, *earlier):
        cols = blocks.shape[-1]
        blocks = along(after(blocks.reshape(pairs, 2 * part, cols), *earlier))
        blocks = blocks.reshape(pairs, 2, part, cols)
        this = lax.dynamic_index_in_dim(blocks, side, 1, keepdims=False)
        other = lax.dynamic_index_in_dim(blocks, 1 - side, 1, keepdims=False)
        return this, swap(other, "expert", 1)

    def to_neighbour(this, other, *earlier):
        got = swap(after(other, *earlier), "expert", 1)
        return jnp.where(
            side == 0, jnp.concatenate([this, got], axis=1), jnp.concatenate([got, this], axis=1)
        )

    e_path = [("expert", b) for b in bits_of(n_e, first_bit)]
    t_path = [("tensor", b) for b in t_bits]
    even_path, odd_path = e_path + t_path[:-1], e_path[:-1] + t_path[:-1] + e_path[-1:]
    path = list(zip(even_path, odd_path))
    last = t_path[-1]

    own = t * rows
    grad_rows = lax.dynamic_slice_in_dim(cotangent, own, rows, 0)
    gate_rows = lax.dynamic_slice_in_dim(gates, own, rows, 0)
    route_rows = lax.dynamic_slice_in_dim(routes, own, rows, 0)
    gate_high = gate_rows.astype(LOW)
    gate_rest = (gate_rows - gate_high.astype(FULL)).astype(LOW)
    extra = jnp.concatenate([route_rows.astype(LOW), gate_high, gate_rest], axis=1)
    extra = jnp.pad(extra, ((0, 0), (0, LANES - 3 * TOP)))
    grad_steps = [jnp.concatenate([grad_rows, extra], axis=1)]
    grad_first = swap_by_parity(grad_steps[0], *path[0])
    attn_arrays, attn_came, attn_sends, packed = every(shard, packed, grad_first)
    grad_steps.append(jnp.concatenate([grad_steps[0], grad_first]))
    grad_second = swap_by_parity(after(grad_steps[1], attn_sends[-1]), *path[1])
    grad_steps.append(jnp.concatenate([grad_steps[1], grad_second]))
    down_this, down_other = from_neighbour(packed[0], attn_came[-1])
    near = to_neighbour(*packed[1:], attn_came[-1])
    pitch = part + pad
    gains = jnp.zeros((pad, LANES), FULL)
    if part % LANES:
        held = jnp.concatenate(
            [a.reshape(-1, pitch, all_cols)[:, part:, :part] for a in attn_arrays]
        ).astype(FULL)
        on_even = [position_in(e ^ k, even_bits) for k in range(n_e)]
        on_odd = [position_in(e ^ k, odd_bits) for k in range(n_e)]
        gains = jnp.concatenate(
            [
                lax.dynamic_index_in_dim(held, jnp.where(t & 1 == 0, a, b), 0, keepdims=False)
                for a, b in zip(on_even, on_odd)
            ],
            axis=1,
        )

    def add_halves(kept, got):
        half = got.shape[0] // 2
        return kept[:half] + got[:half].astype(FULL), (
            kept[half:] + got[half:].astype(FULL)
        ).astype(LOW)

    def scatter_stage(kept, sent, k):
        got = swap_by_parity(sent, *path[-1 - k])
        return (kept, got) if k == len(path) - 1 else add_halves(kept, got)

    documents = segments[0]
    doc_row, doc_col = documents[None, :], documents[:, None]
    index = jnp.arange(length)
    same = (index[None, :] < index[:, None]) & (doc_row == doc_col)
    position = jnp.sum(same.astype(FULL), axis=1, keepdims=True)
    lane = jnp.arange(LANES)
    freqs = THETA ** (-2.0 * (lane % (HEAD_SIZE // 2)).astype(FULL) / HEAD_SIZE)
    angle = position * freqs[None, :]
    cosine = jnp.cos(angle)
    sine = jnp.sin(angle) * jnp.where(lane % HEAD_SIZE < HEAD_SIZE // 2, -1.0, 1.0)[None, :]
    t_masks = t_bits[::-1]
    order = order_of(t_bits)
    weights, first_hidden, qkv, mixed, gains, kept, sent = call(
        functools.partial(attend_body, orders, 2, part, pitch, q_cols, k_cols, rows, order),
        [
            shape((width, all_cols), LOW),
            shape((length, width), LOW),
            shape((length, qkv_cols), LOW),
            shape((length, q_cols), LOW),
            shape((pad, width), FULL),
            shape((length // 2, width), FULL),
            shape((length // 2, width), LOW),
        ],
        where, *attn_arrays[:-1], after(attn_arrays[-1], grad_second), tokens, gains, doc_row, doc_col, cosine, sine,
        scratch=[pltpu.VMEM((length, q_cols), LOW)],
        flops=2 * length * (width * qkv_cols + 2 * length * q_cols),
    )
    def all_rows(field):
        size = field.shape[0]
        for b in t_bits:
            field = jnp.concatenate([field, swap(field, "tensor", b)])
        at = [position_in(t ^ k, t_bits) * size for k in range(n_t)]
        return jnp.concatenate([lax.dynamic_slice_in_dim(field, a, size, 0) for a in at])

    def scatter_rows(kept, sent):
        for b in t_masks[:-1]:
            total = kept + swap(sent, "tensor", b).astype(FULL)
            half = total.shape[0] // 2
            kept, sent = total[:half], total[half:].astype(LOW)
        return kept, swap(sent, "tensor", t_masks[-1])

    grad_third = swap_by_parity(after(grad_steps[-1], attn_arrays[-1]), *path[2])
    kept, got = scatter_rows(kept, sent)
    middle, second_hidden = call(
        functools.partial(middle_body, rows),
        [shape((rows, width), FULL), shape((rows, width), LOW)],
        where, tokens, kept, after(got, grad_third, down_this), gains,
    )

    hidden_field = second_hidden
    for k, (even, odd) in enumerate(path):
        if k == 1:
            hidden_field = after(hidden_field, near, *([grad_got] if len(path) > 3 else []))
        if k == 2:
            hidden_field = after(hidden_field, down_other)
        hidden_got = swap_by_parity(hidden_field, even, odd)
        if k == 1:
            gate_up_rows = along(after(near, hidden_got)).reshape(width, 2 * wide)
        hidden_pieces = [hidden_field, hidden_got]
        hidden_field = jnp.concatenate(hidden_pieces)
        if k == 0:
            grad_field, grad_got = grad_steps[-1], grad_third
            for k in range(3, len(path)):
                grad_field = jnp.concatenate([grad_field, grad_got])
                grad_got = swap_by_parity(after(grad_field, second_hidden), *path[k])
            grad_pieces = [grad_field, grad_got]
    hidden_pieces = hidden_pieces + [swap(p, *last) for p in hidden_pieces]
    grad_pieces = grad_pieces + [swap(p, *last) for p in grad_pieces]
    size = 256
    total_rows = sum(p.shape[0] for p in grad_pieces)
    steps = total_rows // size
    whole = lambda a: pl.BlockSpec(a.shape, lambda i: (0,) * a.ndim)
    tile = lambda cols: pl.BlockSpec((size, cols), lambda i: (i, 0))

    def tiles_of(pieces):
        count = pieces[0].shape[0] // size
        return count, [
            pl.BlockSpec((size, p.shape[1]), lambda i, k=k: (jnp.clip(i - k * count, 0, count - 1), 0))
            for k, p in enumerate(pieces)
        ]

    tiles, specs = tiles_of(grad_pieces)
    gate_table, back, down_rows = call(
        functools.partial(owner_body, len(grad_pieces), tiles, part, own_experts, hidden, replicas),
        [
            shape((total_rows, LANES), FULL),
            shape((total_rows, wide), FULL),
            shape((width, wide), LOW),
        ],
        where, *grad_pieces, down_this, down_other,
        grid=(steps,),
        in_specs=specs + [whole(down_this), whole(down_other)],
        out_specs=[tile(LANES), tile(wide), pl.BlockSpec((width, wide), lambda i: (0, 0))],
        scratch=[pltpu.VMEM((size, width + LANES), LOW)],
        flops=2 * total_rows * width * wide,
        limit=LARGE,
    )
    half = steps // 2

    def experts(chosen, first, out_type):
        later = lambda cols: pl.BlockSpec((size, cols), lambda i: (i + first, 0))
        tiles, specs = tiles_of(chosen)
        return call(
            functools.partial(expert_body, len(chosen), tiles, own_experts, hidden),
            [
                shape((half * size, width), out_type),
                shape((half * size, wide), LOW),
                shape((half * size, 2 * wide), LOW),
            ],
            where, *chosen, gate_up_rows, gate_table, back,
            grid=(half,),
            in_specs=specs
            + [whole(gate_up_rows), later(LANES), later(wide)],
            out_specs=[tile(width), tile(wide), tile(2 * wide)],
            scratch=[pltpu.VMEM((size, width), LOW)],
            flops=2 * half * size * width * 4 * wide,
            limit=LARGE,
        )

    sent_hidden, sent_active, sent_both = experts(hidden_pieces[2:], half, LOW)
    kept_hidden, kept_active, kept_both = experts(hidden_pieces[:2], 0, FULL)

    block = 256
    column = lambda a: pl.BlockSpec((a.shape[0], block), lambda i: (0, i))

    def weight_grad(sources, kept, sent, sided):
        cols = kept.shape[1]
        dims = [(part, cols)] * 2 if sided else [(2, part, cols)]
        count = block // (2 * part)
        return call(
            functools.partial(weight_grad_body, len(sources), part),
            [shape((pairs,) + d, LOW) for d in dims],
            where, *sources, kept, sent,
            grid=(width // block,),
            in_specs=[column(a) for a in sources] + [whole(kept), whole(sent)],
            out_specs=[pl.BlockSpec((count,) + d, lambda i, n=len(d): (i,) + (0,) * n) for d in dims],
            scratch=[pltpu.VMEM((total_rows, block), LOW), pltpu.VMEM((block, cols), LOW)],
            flops=2 * total_rows * width * cols,
            limit=LARGE,
        )

    hidden_kept, hidden_sent = add_halves(kept_hidden, swap(sent_hidden, *last))
    def down(active, out_type):
        return call(
            out_body,
            [shape((half * size, width), out_type)],
            where, active, down_rows,
            grid=(half,),
            in_specs=[tile(wide), whole(down_rows)],
            out_specs=[tile(width)],
            flops=2 * half * size * width * wide,
            limit=LARGE,
        )[0]

    steps_back = len(path)
    kept, sent = scatter_stage(hidden_kept, hidden_sent, 0)
    (down_grad,) = weight_grad(grad_pieces, kept_active, after(sent_active, hidden_sent), False)
    sent_out = down(after(sent_active, down_grad), LOW)
    kept_out = down(after(kept_active, down_grad), FULL)
    kept, sent = scatter_stage(kept, after(sent, down_grad), 1)
    out_kept, out_sent = add_halves(kept_out, swap(sent_out, *last))
    both_this, both_other = weight_grad(hidden_pieces, kept_both, after(sent_both, sent_out), True)
    grad_near = to_neighbour(both_this, both_other)
    down_back = from_neighbour(down_grad)
    sent = after(sent, down_back[0], both_other, kept_out)
    for k in range(2, steps_back - 1):
        kept, sent = scatter_stage(kept, sent, k)
    grad_kept, grad_got = scatter_stage(kept, after(sent, out_sent), steps_back - 1)
    out_kept, out_sent = scatter_stage(out_kept, out_sent, 0)
    out_first = out_sent
    out_kept, out_sent = scatter_stage(out_kept, out_sent, 1)
    out_second = out_sent
    both_back = along(after(grad_near, grad_got)).reshape(width, 2 * wide)

    grad_middle, branch_grad, moe_part = call(
        middle_back_body,
        [shape((rows, width), FULL), shape((rows, width), LOW), shape((16, width), FULL)],
        where, grad_kept, grad_got, middle, grad_rows, gains,
    )
    branch_pieces = [branch_grad]
    for b in reversed(t_masks):
        branch_pieces = branch_pieces + [swap(p, "tensor", b) for p in branch_pieces]
    sum_orders = orders[0], orders[0]
    kept_w, sent_w, first_kept, first_sent = call(
        functools.partial(
            attend_back_body, len(branch_pieces), q_cols, k_cols, rows, part, order, sum_orders
        ),
        [
            shape((width // 2, all_cols), FULL),
            shape((width // 2, all_cols), LOW),
            shape((length // 2, width), FULL),
            shape((length // 2, width), LOW),
        ],
        where, *branch_pieces[:-1], after(branch_pieces[-1], out_first), mixed, qkv, doc_row, doc_col, cosine, sine,
        first_hidden, weights,
        scratch=[
            pltpu.VMEM((length, width), LOW),
            pltpu.VMEM((length, max(q_cols, qkv_cols)), LOW),
            pltpu.VMEM((length, qkv_cols), LOW),
            pltpu.VMEM((width, all_cols), FULL),
        ],
        flops=2 * length * width * (2 * q_cols + 2 * qkv_cols),
    )
    got_w = swap(sent_w, "expert", e_bits[-1])
    attn_grad = kept_w + got_w.astype(FULL)
    kept, got = scatter_rows(first_kept, first_sent)
    (token_rows,) = call(
        functools.partial(tokens_back_body, rows),
        [shape((rows + 16, width), FULL)],
        where, tokens, kept, after(got, got_w, out_second), gains, grad_middle, moe_part,
    )
    gathered = all_rows(token_rows.astype(LOW))
    gathered = gathered.reshape(n_t, rows + 16, width).astype(FULL)
    grad_input = gathered[:, :rows].reshape(length, width)
    gain_sum = jnp.sum(gathered[:, rows : rows + 2], axis=0)

    blocks = gain_sum.reshape(2, n_e, part).transpose(1, 0, 2)

    half_rows = attn_grad.shape[0] // 2
    kept_w, sent_w = attn_grad[:half_rows], attn_grad[half_rows:].astype(LOW)
    blocks = after(blocks, sent_w)
    gain_grads = jnp.sum(lax.all_to_all(blocks, "expert", 0, 0, tiled=True), axis=0)
    out_sent = after(out_sent, both_back)
    for k, b in enumerate(reversed(e_bits[:-1])):
        attn_grad = kept_w + swap(sent_w, "expert", b).astype(FULL)
        half_rows = attn_grad.shape[0] // 2
        kept_w, sent_w = attn_grad[:half_rows], attn_grad[half_rows:].astype(LOW)
        if k == 0:
            out_kept, out_sent = scatter_stage(out_kept, out_sent, 2)
            out_sent = after(out_sent, sent_w)
    for k in range(3, steps_back):
        out_kept, out_sent = scatter_stage(out_kept, out_sent, k)
    output_rows = (middle + (out_kept + out_sent.astype(FULL))).astype(LOW)
    output = all_rows(output_rows)

    out_dims = [(part, hidden), (part, hidden), (hidden, part) if turn else (part, hidden)]

    def unpack(source, dims, turned):
        cols = source.shape[1]
        return call(
            functools.partial(unpack_body, own_experts, hidden, replicas, turned),
            [shape((EXPERTS,) + dims, FULL)] * (cols // wide),
            where, source,
            grid=(pairs,),
            in_specs=[pl.BlockSpec((2 * part, cols), lambda z: (z, 0))],
            out_specs=[at_pair(dims)] * (cols // wide),
        )

    sides_of = lambda this, other: jnp.where(
        side == 0, jnp.stack([this, other], axis=1), jnp.stack([other, this], axis=1)
    )
    down_back = sides_of(*down_back).reshape(width, wide)
    shards = unpack(both_back, out_dims[0], False) + unpack(down_back, out_dims[2], turn)
    gate_shard, up_shard, down_shard = shards
    if not turn:
        down_shard = down_shard.transpose(0, 2, 1)

    return (
        output,
        grad_input,
        attn_grad[:, :q_cols],
        attn_grad[:, q_cols : q_cols + k_cols],
        attn_grad[:, q_cols + k_cols : qkv_cols],
        attn_grad[:, qkv_cols:].T,
        gain_grads[0],
        gain_grads[1],
        gate_shard,
        up_shard,
        down_shard,
    )


def solution(mesh):
    by_rows = P("expert", None)
    by_both = P("expert", "tensor")
    in_experts = P(None, "expert", "tensor")
    down_specs = P(None, "tensor", "expert")
    return jax.shard_map(
        local,
        mesh=mesh,
        in_specs=(by_rows,) * 5
        + (by_both,) * 3
        + (P("tensor", "expert"), P("expert"), P("expert"), in_experts, in_experts, down_specs),
        out_specs=(by_rows, by_rows)
        + (by_both,) * 3
        + (P("tensor", "expert"), P("expert"), P("expert"), in_experts, in_experts, down_specs),
        check_vma=False,
    )
```

```python
import functools

import jax
import jax.numpy as jnp
from jax import lax
from jax.experimental import pallas as pl
from jax.experimental.pallas import tpu as pltpu
from jax.sharding import PartitionSpec as P

HEAD_SIZE = 64
EXPERTS = 32
TOP = 8
EPS = 1e-06
THETA = 10000.0
MASKED = -1e30
LANES = 128
LIMIT = 24 * 1024 * 1024
LARGE = 56 * 1024 * 1024

LOW = jnp.bfloat16
FULL = jnp.float32
ROWS_ON_ROWS = (((0,), (0,)), ((), ()))
COLS_ON_ROWS = (((1,), (0,)), ((), ()))
COLS_ON_COLS = (((1,), (1,)), ((), ()))


def mul(left, right, dims=COLS_ON_ROWS):
    return lax.dot_general(left, right, dims, preferred_element_type=FULL)


def shape(dims, dtype):
    return jax.ShapeDtypeStruct(dims, dtype)


def call(body, outs, *args, grid=None, in_specs=None, out_specs=None, scratch=(), flops=0, limit=LIMIT):
    size = sum(a.size * a.dtype.itemsize for a in args)
    size += sum(o.size * jnp.dtype(o.dtype).itemsize for o in outs)
    whole = pl.BlockSpec(memory_space=pltpu.VMEM)
    if in_specs is None:
        in_specs = [whole] * (len(args) - 1)
    if out_specs is None:
        out_specs = [whole] * len(outs)
    extra = {} if grid is None else {"grid": grid}
    return pl.pallas_call(
        body,
        out_shape=list(outs),
        in_specs=[pl.BlockSpec(memory_space=pltpu.SMEM)] + list(in_specs),
        out_specs=list(out_specs),
        scratch_shapes=list(scratch),
        compiler_params=pltpu.CompilerParams(vmem_limit_bytes=limit),
        cost_estimate=pl.CostEstimate(flops=flops, bytes_accessed=size, transcendentals=0),
        **extra,
    )(*args)


def swap(field, axis, mask):
    count = lax.axis_size(axis)
    return lax.ppermute(field, axis, [(i, i ^ mask) for i in range(count)])


def after(field, *earlier):
    return lax.optimization_barrier((field, *earlier))[0]


def swap_by_parity(field, even, odd):
    n_e, n_t = lax.axis_size("expert"), lax.axis_size("tensor")
    pairs = []
    for e in range(n_e):
        for t in range(n_t):
            axis, mask = odd if t & 1 else even
            to = ((e ^ mask) * n_t + t) if axis == "expert" else (e * n_t + (t ^ mask))
            pairs.append((e * n_t + t, to))
    return lax.ppermute(field, ("expert", "tensor"), pairs)


def bits_of(count, first_bit=0):
    return [1 << b for b in reversed(range(first_bit, count.bit_length() - 1))]


def position_in(mask, bits):
    return sum(jnp.where(mask & b != 0, 1 << i, 0) for i, b in enumerate(bits))


def order_of(bits):
    order = [0]
    for b in bits:
        order = order + [k ^ b for k in order]
    return order


def rotate(field, cosine, sine):
    lane = lax.broadcasted_iota(jnp.int32, (field.shape[0], LANES), 1)
    low_half = lane % HEAD_SIZE < HEAD_SIZE // 2
    turned = []
    for at in range(0, field.shape[1], LANES):
        block = field[:, at : at + LANES]
        ahead = pltpu.roll(block, LANES - HEAD_SIZE // 2, 1)
        behind = pltpu.roll(block, HEAD_SIZE // 2, 1)
        turned.append(block * cosine + jnp.where(low_half, ahead, behind) * sine)
    return jnp.concatenate(turned, axis=1)


def admitted(doc_row, doc_col):
    length = doc_row.shape[1]
    row = lax.broadcasted_iota(jnp.int32, (length, length), 0)
    col = lax.broadcasted_iota(jnp.int32, (length, length), 1)
    return (col <= row) & (doc_row == doc_col)


def softmax_of(query, key, allowed):
    scores = mul(query, key, COLS_ON_COLS) * HEAD_SIZE**-0.5
    scores = jnp.where(allowed, scores, MASKED)
    raised = jnp.exp(scores - jnp.max(scores, axis=1, keepdims=True))
    return raised / jnp.sum(raised, axis=1, keepdims=True)


def place_rows(target, sources, orders, where, part, pitch):
    count = len(orders[0]) // len(sources)
    for p, (even, odd) in enumerate(zip(*orders)):
        at = pl.multiple_of((where[0] ^ jnp.where(where[1] & 1 == 0, even, odd)) * part, part)
        k = p % count * pitch
        target[pl.ds(at, part), :] = sources[p // count][k : k + part, :]


def pack_body(own, hid, replicas, turn, where, gate, up, down, down_out, *sided):
    side = where[0] & 1
    for j in range(own):
        at = slice(j * hid, (j + 1) * hid)
        for k in range(2):
            block = down[(k * own if replicas == 1 else 0) + j]
            down_out[0, k, :, at] = (block.T if turn else block).astype(LOW)
            place = ((side ^ k) * own if replicas == 1 else 0) + j
            sided[k][0, :, at] = gate[place].astype(LOW)
            up_at = slice((own + j) * hid, (own + j + 1) * hid)
            sided[k][0, :, up_at] = up[place].astype(LOW)


def interleave_body(part, where, this, other, out):
    for k, source in enumerate((this, other)):
        at = pl.multiple_of(((where[0] & 1) ^ k) * part, part)
        out[0, pl.ds(at, part), :] = source[0]


def attend_body(orders, n, part, pitch, q_cols, k_cols, rows, order, where, *refs):
    sources = refs[:n]
    tokens, gain_in, doc_row, doc_col, cosine, sine = refs[n : n + 6]
    weights, hidden, qkv_out, mixed_out, gain, kept, sent, mixed = refs[n + 6 :]
    place_rows(weights, sources, orders, where, part, pitch)
    if part % LANES == 0:
        count = len(orders[0]) // n
        for p, (even, odd) in enumerate(zip(*orders)):
            at = pl.multiple_of((where[0] ^ jnp.where(where[1] & 1 == 0, even, odd)) * part, part)
            k = p % count * pitch + part
            gain[:, pl.ds(at, part)] = sources[p // count][k : k + gain.shape[0], :part].astype(FULL)
    else:
        gain[...] = gain_in[...]
    x = tokens[...].astype(FULL)
    scale = lax.rsqrt(jnp.mean(x * x, axis=1, keepdims=True) + EPS)
    first = (x * scale * gain[0:1, :]).astype(LOW)
    hidden[...] = first
    qkv = mul(first, weights[:, : q_cols + 2 * k_cols])
    turned = rotate(qkv[:, : q_cols + k_cols], cosine[...], sine[...]).astype(LOW)
    values = qkv[:, q_cols + k_cols :].astype(LOW)
    qkv_out[:, : q_cols + k_cols] = turned
    qkv_out[:, q_cols + k_cols :] = values
    allowed = admitted(doc_row[...], doc_col[...])
    per_group = q_cols // k_cols
    for h in range(q_cols // HEAD_SIZE):
        at, g = h * HEAD_SIZE, h // per_group * HEAD_SIZE
        shares = softmax_of(
            turned[:, at : at + HEAD_SIZE],
            turned[:, q_cols + g : q_cols + g + HEAD_SIZE],
            allowed,
        ).astype(LOW)
        mixed[:, at : at + HEAD_SIZE] = mul(shares, values[:, g : g + HEAD_SIZE]).astype(LOW)
    for k, m in enumerate(order):
        at = pl.multiple_of((where[1] ^ m) * rows, rows)
        mixed_out[k * rows : (k + 1) * rows, :] = mixed[pl.ds(at, rows), :]
    product = mul(mixed_out[...], weights[:, q_cols + 2 * k_cols :], COLS_ON_COLS)
    half = kept.shape[0]
    kept[...] = product[:half]
    sent[...] = product[half:].astype(LOW)


def middle_body(rows, where, tokens, kept, got, gain, middle, hidden):
    at = pl.multiple_of(where[1] * rows, rows)
    m = tokens[pl.ds(at, rows), :].astype(FULL) + (kept[...] + got[...].astype(FULL))
    middle[...] = m
    scale = lax.rsqrt(jnp.mean(m * m, axis=1, keepdims=True) + EPS)
    hidden[...] = (m * scale * gain[1:2, :]).astype(LOW)


def pick_tile(buffer, sources, tiles, step):
    for k, source in enumerate(sources):

        @pl.when(step // tiles == k)
        def _():
            buffer[...] = source[...]


def owner_body(n_piece, tiles, part, own, hid, replicas, where, *refs):
    grads = refs[:n_piece]
    this, other, gate_out, back_out, weights, buffer = refs[n_piece:]
    width = weights.shape[0]
    step = pl.program_id(0)

    @pl.when(step == 0)
    def _():
        for z in range(this.shape[0]):
            for k, source in enumerate((this, other)):
                at = pl.multiple_of((2 * z + ((where[0] & 1) ^ k)) * part, part)
                weights[pl.ds(at, part), :] = source[z]

    pick_tile(buffer, grads, tiles, step)
    extra = buffer[:, width:].astype(FULL)
    lane = lax.broadcasted_iota(jnp.int32, extra.shape, 1)
    gate = pltpu.roll(extra, LANES - TOP, 1) + pltpu.roll(extra, LANES - 2 * TOP, 1)
    first = where[0] // replicas * own
    back = mul(buffer[:, :width], weights[...])
    table = jnp.zeros(extra.shape, FULL)
    for j in range(own):
        hit = (lane < TOP) & (extra == (first + j).astype(FULL))
        column = jnp.sum(jnp.where(hit, gate, 0.0), axis=1, keepdims=True)
        table = jnp.where(lane == j, column, table)
        back_out[:, j * hid : (j + 1) * hid] = back[:, j * hid : (j + 1) * hid] * column
    gate_out[...] = table


def expert_body(n_piece, tiles, own, hid, where, *refs):
    rows = refs[:n_piece]
    weights, gate, back, grad_hidden, active_out, grad_both, buffer = refs[n_piece:]
    pick_tile(buffer, rows, tiles, pl.program_id(0))
    wide = own * hid
    both = mul(buffer[...], weights[...])
    for j in range(own):
        at = slice(j * hid, (j + 1) * hid)
        up_at = slice(wide + j * hid, wide + (j + 1) * hid)
        pre, up = both[:, at], both[:, up_at]
        squash = 1.0 / (1.0 + jnp.exp(-pre))
        silu = pre * squash
        active = (silu * up).astype(LOW).astype(FULL)
        active_out[:, at] = (active * gate[:, j : j + 1]).astype(LOW)
        d = back[:, at]
        grad_both[:, at] = (d * up * squash * (1.0 + pre * (1.0 - squash))).astype(LOW)
        grad_both[:, up_at] = (d * silu).astype(LOW)
    product = mul(grad_both[...], weights[...], COLS_ON_COLS)
    grad_hidden[...] = product.astype(grad_hidden.dtype)


def out_body(where, active, weights, out):
    out[...] = mul(active[...], weights[...], COLS_ON_COLS).astype(out.dtype)


def weight_grad_body(n_source, part, where, *refs):
    sources = refs[:n_source]
    kept, sent, *outs, column, total = refs[n_source:]
    half, size = kept.shape[0], sources[0].shape[0]
    for k, source in enumerate(sources):
        column[k * size : (k + 1) * size, :] = source[...]
    product = mul(column[:half], kept[...], ROWS_ON_ROWS)
    total[...] = (product + mul(column[half:], sent[...], ROWS_ON_ROWS)).astype(LOW)
    for z in range(total.shape[0] // (2 * part)):
        for k in range(2):
            if len(outs) == 2:
                at = pl.multiple_of((2 * z + ((where[0] & 1) ^ k)) * part, part)
                outs[k][z] = total[pl.ds(at, part), :]
            else:
                at = (2 * z + k) * part
                outs[0][z, k] = total[at : at + part, :]


def middle_back_body(where, *refs):
    kept, got, middle, grad, gain, grad_middle, low, gain_part = refs
    total = kept[...] + got[...].astype(FULL)
    m = middle[...]
    scale = lax.rsqrt(jnp.mean(m * m, axis=1, keepdims=True) + EPS)
    gain_part[...] = jnp.broadcast_to(
        jnp.sum(total * m * scale, axis=0, keepdims=True), gain_part.shape
    )
    weighted = total * gain[1:2, :]
    inner = jnp.mean(weighted * m, axis=1, keepdims=True)
    back = grad[...].astype(FULL) + (scale * weighted - m * (scale * scale * scale) * inner)
    grad_middle[...] = back
    low[...] = back.astype(LOW)


def attend_back_body(n_piece, q_cols, k_cols, rows, part, order, orders, where, *refs):
    pieces = refs[:n_piece]
    mixed, qkv_in, doc_row, doc_col, cosine, sine, hidden, weights = refs[n_piece : n_piece + 8]
    kept, sent, first_kept, first_sent, branch, natural, grad_qkv, grads = refs[n_piece + 8 :]
    for k in range(n_piece):
        branch[k * rows : (k + 1) * rows, :] = pieces[k][...]
    grad_mixed = mul(branch[...], weights[:, q_cols + 2 * k_cols :]).astype(LOW)
    for k, m in enumerate(order):
        at = pl.multiple_of((where[1] ^ m) * rows, rows)
        natural[pl.ds(at, rows), :q_cols] = grad_mixed[k * rows : (k + 1) * rows]
    qk = q_cols + k_cols
    total = qk + k_cols
    grads[:, total:] = mul(branch[...], mixed[...], ROWS_ON_ROWS)
    allowed = admitted(doc_row[...], doc_col[...])
    per_group = q_cols // k_cols
    query_grads, key_grads, value_grads = [], [], []
    for g in range(k_cols // HEAD_SIZE):
        key = qkv_in[:, q_cols + g * HEAD_SIZE : q_cols + (g + 1) * HEAD_SIZE]
        value = qkv_in[:, qk + g * HEAD_SIZE : qk + (g + 1) * HEAD_SIZE]
        key_grad = value_grad = None
        for h in range(g * per_group, (g + 1) * per_group):
            at = slice(h * HEAD_SIZE, (h + 1) * HEAD_SIZE)
            query = qkv_in[:, at]
            shares = softmax_of(query, key, allowed)
            grad = natural[:, at]
            grad_shares = mul(grad, value, COLS_ON_COLS)
            inner = jnp.sum(shares * grad_shares, axis=1, keepdims=True)
            grad_scores = (shares * (grad_shares - inner)).astype(LOW)
            query_grads.append(mul(grad_scores, key))
            dk = mul(grad_scores, query, ROWS_ON_ROWS)
            dv = mul(shares.astype(LOW), grad, ROWS_ON_ROWS)
            key_grad = dk if key_grad is None else key_grad + dk
            value_grad = dv if value_grad is None else value_grad + dv
        key_grads.append(key_grad)
        value_grads.append(value_grad)
    turned = jnp.concatenate(query_grads + key_grads, axis=1) * HEAD_SIZE**-0.5
    grad_qkv[:, :qk] = rotate(turned, cosine[...], -sine[...]).astype(LOW)
    grad_qkv[:, qk:] = jnp.concatenate(value_grads, axis=1).astype(LOW)
    grads[:, :total] = mul(hidden[...], grad_qkv[...], ROWS_ON_ROWS)
    for p, (even, odd) in enumerate(zip(*orders)):
        at = pl.multiple_of((where[0] ^ jnp.where(where[1] & 1 == 0, even, odd)) * part, part)
        target = kept if p < len(orders[0]) // 2 else sent
        k = p % (len(orders[0]) // 2)
        target[k * part : (k + 1) * part, :] = grads[pl.ds(at, part), :].astype(target.dtype)
    for k, m in enumerate(order):
        at = pl.multiple_of((where[1] ^ m) * rows, rows)
        natural[k * rows : (k + 1) * rows, :total] = grad_qkv[pl.ds(at, rows), :]
    product = mul(natural[:, :total], weights[:, :total], COLS_ON_COLS)
    half = first_kept.shape[0]
    first_kept[...] = product[:half]
    first_sent[...] = product[half:].astype(LOW)


def tokens_back_body(rows, where, tokens, kept, got, gain, grad_middle, moe_part, out):
    at = pl.multiple_of(where[1] * rows, rows)
    x = tokens[pl.ds(at, rows), :].astype(FULL)
    scale = lax.rsqrt(jnp.mean(x * x, axis=1, keepdims=True) + EPS)
    first = kept[...] + got[...].astype(FULL)
    attn_part = jnp.sum(first * x * scale, axis=0, keepdims=True)
    weighted = first * gain[0:1, :]
    inner = jnp.mean(weighted * x, axis=1, keepdims=True)
    out[:rows] = grad_middle[...] + (scale * weighted - x * (scale * scale * scale) * inner)
    line = lax.broadcasted_iota(jnp.int32, moe_part.shape, 0)
    out[rows:] = jnp.where(line == 0, attn_part, jnp.where(line == 1, moe_part[...], 0.0))


def unpack_body(own, hid, replicas, turn, where, source, *outs):
    part = source.shape[0] // 2
    for k in range(own * len(outs)):
        out, j = outs[k // own], k % own
        cols = slice(k * hid, (k + 1) * hid)
        pieces = [source[i * part : (i + 1) * part, cols].astype(FULL) for i in range(2)]
        pieces = [piece.T for piece in pieces] if turn else pieces
        if replicas == 1:
            out[j] = pieces[0]
            out[own + j] = pieces[1]
        else:
            first = 2 * pl.program_id(0) % replicas == 0
            out[j] = pieces[0] + pieces[1] + jnp.where(first, 0.0, out[j])


def local(
    tokens,
    cotangent,
    segments,
    routes,
    gates,
    w_query,
    key_projection,
    value_projection,
    w_out,
    gain_attn,
    gain_moe,
    w_gate,
    w_up,
    w_down,
):
    n_e, n_t = lax.axis_size("expert"), lax.axis_size("tensor")
    e, t = lax.axis_index("expert"), lax.axis_index("tensor")
    where = jnp.stack([e, t]).astype(jnp.int32)
    replicas = max(1, n_e // EXPERTS)
    own_experts = EXPERTS * replicas // n_e
    first_bit = replicas.bit_length() - 1
    length, width = tokens.shape
    part = width // n_e
    rows = length // n_t
    q_cols, k_cols = w_query.shape[1], key_projection.shape[1]
    qkv_cols = q_cols + 2 * k_cols
    hidden = w_gate.shape[2]
    wide = own_experts * hidden

    pad = 16
    all_cols = qkv_cols + q_cols
    gain_rows = jnp.pad(jnp.stack([gain_attn, gain_moe]), ((0, pad - 2), (0, all_cols - part)))
    shard = jnp.concatenate([w_query, key_projection, value_projection, w_out.T], axis=1)
    shard = jnp.concatenate([shard, gain_rows]).astype(LOW)

    e_bits, t_bits = bits_of(n_e), bits_of(n_t)
    even_bits, odd_bits = e_bits, e_bits[-1:] + e_bits[:-1]
    orders = order_of(even_bits), order_of(odd_bits)
    by_parity = [(("expert", a), ("expert", b)) for a, b in zip(even_bits, odd_bits)]

    def every(shard, ready, later):
        came, sends = [], []
        for k, (even, odd) in enumerate(by_parity):
            if k == 1:
                shard, *ready = lax.optimization_barrier((shard, *ready))
            if k == 2:
                shard = after(shard, later)
            sends.append(shard)
            came.append(swap_by_parity(shard, even, odd))
            shard = jnp.concatenate([shard, came[-1]])
        return [sends[-1], came[-1]], came, sends, ready

    pairs = n_e // 2
    turn = part % LANES == 0
    pair_experts = 2 * own_experts // replicas or 1
    at_pair = lambda dims: pl.BlockSpec(
        (pair_experts,) + dims, lambda z: (2 * z // max(2, replicas), 0, 0)
    )
    sources = [w_gate, w_up, w_down if turn else w_down.transpose(0, 2, 1)]
    sided = pl.BlockSpec((1, part, 2 * wide), lambda z: (z, 0, 0))
    packed = call(
        functools.partial(pack_body, own_experts, hidden, replicas, turn),
        [shape((pairs, 2, part, wide), LOW)] + [shape((pairs, part, 2 * wide), LOW)] * 2,
        where, *sources,
        grid=(pairs,),
        in_specs=[at_pair(w.shape[1:]) for w in sources],
        out_specs=[pl.BlockSpec((1, 2, part, wide), lambda z: (z, 0, 0, 0))] + [sided] * 2,
    )
    side = e & 1
    lines = [[z * 2 + k for z in range(n_e // 2)] for k in range(2)]

    def along(blocks):
        return lax.all_to_all(
            blocks, "expert", 0, 0, tiled=True, axis_index_groups=lines
        )

    def split_sides(blocks):
        blocks = blocks.reshape(pairs, 2, part, blocks.shape[-1])
        this = lax.dynamic_index_in_dim(blocks, side, 1, keepdims=False)
        return this, lax.dynamic_index_in_dim(blocks, 1 - side, 1, keepdims=False)

    def from_neighbour(blocks, *earlier):
        cols = blocks.shape[-1]
        blocks = along(after(blocks.reshape(pairs, 2 * part, cols), *earlier))
        this, other = split_sides(blocks)
        return this, swap(other, "expert", 1)

    def interleave(this, other):
        cols = this.shape[-1]
        block = pl.BlockSpec((1, part, cols), lambda z: (z, 0, 0))
        return call(
            functools.partial(interleave_body, part),
            [shape((pairs, 2 * part, cols), LOW)],
            where, this, other,
            grid=(pairs,),
            in_specs=[block, block],
            out_specs=[pl.BlockSpec((1, 2 * part, cols), lambda z: (z, 0, 0))],
        )[0]

    def to_neighbour(this, other, *earlier):
        return interleave(this, swap(after(other, *earlier), "expert", 1))

    e_path = [("expert", b) for b in bits_of(n_e, first_bit)]
    t_path = [("tensor", b) for b in t_bits]
    even_path, odd_path = e_path + t_path[:-1], e_path[:-1] + t_path[:-1] + e_path[-1:]
    path = list(zip(even_path, odd_path))
    last = t_path[-1]

    own = t * rows
    grad_rows = lax.dynamic_slice_in_dim(cotangent, own, rows, 0)
    gate_rows = lax.dynamic_slice_in_dim(gates, own, rows, 0)
    route_rows = lax.dynamic_slice_in_dim(routes, own, rows, 0)
    gate_high = gate_rows.astype(LOW)
    gate_rest = (gate_rows - gate_high.astype(FULL)).astype(LOW)
    extra = jnp.concatenate([route_rows.astype(LOW), gate_high, gate_rest], axis=1)
    extra = jnp.pad(extra, ((0, 0), (0, LANES - 3 * TOP)))
    grad_steps = [jnp.concatenate([grad_rows, extra], axis=1)]
    grad_first = swap_by_parity(grad_steps[0], *path[0])
    attn_arrays, attn_came, attn_sends, packed = every(shard, packed, grad_first)
    grad_steps.append(jnp.concatenate([grad_steps[0], grad_first]))
    grad_second = swap_by_parity(after(grad_steps[1], attn_sends[-1]), *path[1])
    grad_steps.append(jnp.concatenate([grad_steps[1], grad_second]))
    down_this, down_other = from_neighbour(packed[0], attn_came[-1])
    near = to_neighbour(*packed[1:], attn_came[-1])
    pitch = part + pad
    gains = jnp.zeros((pad, LANES), FULL)
    if part % LANES:
        held = jnp.concatenate(
            [a.reshape(-1, pitch, all_cols)[:, part:, :part] for a in attn_arrays]
        ).astype(FULL)
        on_even = [position_in(e ^ k, even_bits) for k in range(n_e)]
        on_odd = [position_in(e ^ k, odd_bits) for k in range(n_e)]
        gains = jnp.concatenate(
            [
                lax.dynamic_index_in_dim(held, jnp.where(t & 1 == 0, a, b), 0, keepdims=False)
                for a, b in zip(on_even, on_odd)
            ],
            axis=1,
        )

    def add_halves(kept, got):
        half = got.shape[0] // 2
        return kept[:half] + got[:half].astype(FULL), (
            kept[half:] + got[half:].astype(FULL)
        ).astype(LOW)

    def scatter_stage(kept, sent, k):
        got = swap_by_parity(sent, *path[-1 - k])
        return (kept, got) if k == len(path) - 1 else add_halves(kept, got)

    documents = segments[0]
    doc_row, doc_col = documents[None, :], documents[:, None]
    index = jnp.arange(length)
    same = (index[None, :] < index[:, None]) & (doc_row == doc_col)
    position = jnp.sum(same.astype(FULL), axis=1, keepdims=True)
    lane = jnp.arange(LANES)
    freqs = THETA ** (-2.0 * (lane % (HEAD_SIZE // 2)).astype(FULL) / HEAD_SIZE)
    angle = position * freqs[None, :]
    cosine = jnp.cos(angle)
    sine = jnp.sin(angle) * jnp.where(lane % HEAD_SIZE < HEAD_SIZE // 2, -1.0, 1.0)[None, :]
    t_masks = t_bits[::-1]
    order = order_of(t_bits)
    weights, first_hidden, qkv, mixed, gains, kept, sent = call(
        functools.partial(attend_body, orders, 2, part, pitch, q_cols, k_cols, rows, order),
        [
            shape((width, all_cols), LOW),
            shape((length, width), LOW),
            shape((length, qkv_cols), LOW),
            shape((length, q_cols), LOW),
            shape((pad, width), FULL),
            shape((length // 2, width), FULL),
            shape((length // 2, width), LOW),
        ],
        where, *attn_arrays[:-1], after(attn_arrays[-1], grad_second), tokens, gains, doc_row, doc_col, cosine, sine,
        scratch=[pltpu.VMEM((length, q_cols), LOW)],
        flops=2 * length * (width * qkv_cols + 2 * length * q_cols),
    )
    def all_rows(field):
        size = field.shape[0]
        for b in t_bits:
            field = jnp.concatenate([field, swap(field, "tensor", b)])
        at = [position_in(t ^ k, t_bits) * size for k in range(n_t)]
        return jnp.concatenate([lax.dynamic_slice_in_dim(field, a, size, 0) for a in at])

    def scatter_rows(kept, sent):
        for b in t_masks[:-1]:
            total = kept + swap(sent, "tensor", b).astype(FULL)
            half = total.shape[0] // 2
            kept, sent = total[:half], total[half:].astype(LOW)
        return kept, swap(sent, "tensor", t_masks[-1])

    grad_third = swap_by_parity(after(grad_steps[-1], attn_arrays[-1]), *path[2])
    kept, got = scatter_rows(kept, sent)
    middle, second_hidden = call(
        functools.partial(middle_body, rows),
        [shape((rows, width), FULL), shape((rows, width), LOW)],
        where, tokens, kept, after(got, grad_third, down_this), gains,
    )

    hidden_field = second_hidden
    for k, (even, odd) in enumerate(path):
        if k == 1:
            hidden_field = after(hidden_field, near)
        if k == 2:
            hidden_field = after(hidden_field, down_other, grad_got)
        hidden_got = swap_by_parity(hidden_field, even, odd)
        if k == 1:
            gate_up_rows = along(after(near, hidden_got)).reshape(width, 2 * wide)
        hidden_pieces = [hidden_field, hidden_got]
        hidden_field = jnp.concatenate(hidden_pieces)
        if k == 0:
            grad_field, grad_got = grad_steps[-1], grad_third
            for k in range(3, len(path)):
                grad_field = jnp.concatenate([grad_field, grad_got])
                grad_got = swap_by_parity(after(grad_field, second_hidden), *path[k])
            grad_pieces = [grad_field, grad_got]
    hidden_pieces = hidden_pieces + [swap(p, *last) for p in hidden_pieces]
    grad_pieces = grad_pieces + [swap(p, *last) for p in grad_pieces]
    size = 512
    total_rows = sum(p.shape[0] for p in grad_pieces)
    steps = total_rows // size
    whole = lambda a: pl.BlockSpec(a.shape, lambda i: (0,) * a.ndim)
    tile = lambda cols: pl.BlockSpec((size, cols), lambda i: (i, 0))

    def tiles_of(pieces):
        count = pieces[0].shape[0] // size
        return count, [
            pl.BlockSpec((size, p.shape[1]), lambda i, k=k: (jnp.clip(i - k * count, 0, count - 1), 0))
            for k, p in enumerate(pieces)
        ]

    tiles, specs = tiles_of(grad_pieces)
    gate_table, back, down_rows = call(
        functools.partial(owner_body, len(grad_pieces), tiles, part, own_experts, hidden, replicas),
        [
            shape((total_rows, LANES), FULL),
            shape((total_rows, wide), FULL),
            shape((width, wide), LOW),
        ],
        where, *grad_pieces, down_this, down_other,
        grid=(steps,),
        in_specs=specs + [whole(down_this), whole(down_other)],
        out_specs=[tile(LANES), tile(wide), pl.BlockSpec((width, wide), lambda i: (0, 0))],
        scratch=[pltpu.VMEM((size, width + LANES), LOW)],
        flops=2 * total_rows * width * wide,
        limit=LARGE,
    )
    half = steps // 2

    def experts(chosen, first, out_type):
        later = lambda cols: pl.BlockSpec((size, cols), lambda i: (i + first, 0))
        tiles, specs = tiles_of(chosen)
        return call(
            functools.partial(expert_body, len(chosen), tiles, own_experts, hidden),
            [
                shape((half * size, width), out_type),
                shape((half * size, wide), LOW),
                shape((half * size, 2 * wide), LOW),
            ],
            where, *chosen, gate_up_rows, gate_table, back,
            grid=(half,),
            in_specs=specs
            + [whole(gate_up_rows), later(LANES), later(wide)],
            out_specs=[tile(width), tile(wide), tile(2 * wide)],
            scratch=[pltpu.VMEM((size, width), LOW)],
            flops=2 * half * size * width * 4 * wide,
            limit=LARGE,
        )

    sent_hidden, sent_active, sent_both = experts(hidden_pieces[2:], half, LOW)
    kept_hidden, kept_active, kept_both = experts(hidden_pieces[:2], 0, FULL)

    block = 256
    column = lambda a: pl.BlockSpec((a.shape[0], block), lambda i: (0, i))

    def weight_grad(sources, kept, sent, sided):
        cols = kept.shape[1]
        dims = [(part, cols)] * 2 if sided else [(2, part, cols)]
        count = block // (2 * part)
        return call(
            functools.partial(weight_grad_body, len(sources), part),
            [shape((pairs,) + d, LOW) for d in dims],
            where, *sources, kept, sent,
            grid=(width // block,),
            in_specs=[column(a) for a in sources] + [whole(kept), whole(sent)],
            out_specs=[pl.BlockSpec((count,) + d, lambda i, n=len(d): (i,) + (0,) * n) for d in dims],
            scratch=[pltpu.VMEM((total_rows, block), LOW), pltpu.VMEM((block, cols), LOW)],
            flops=2 * total_rows * width * cols,
            limit=LARGE,
        )

    hidden_kept, hidden_sent = add_halves(kept_hidden, swap(sent_hidden, *last))
    def down(active, out_type):
        return call(
            out_body,
            [shape((half * size, width), out_type)],
            where, active, down_rows,
            grid=(half,),
            in_specs=[tile(wide), whole(down_rows)],
            out_specs=[tile(width)],
            flops=2 * half * size * width * wide,
            limit=LARGE,
        )[0]

    steps_back = len(path)
    kept, sent = scatter_stage(hidden_kept, hidden_sent, 0)
    (down_grad,) = weight_grad(grad_pieces, kept_active, after(sent_active, hidden_sent), False)
    sent_out = down(after(sent_active, down_grad), LOW)
    kept_out = down(after(kept_active, down_grad), FULL)
    kept, sent = scatter_stage(kept, after(sent, down_grad), 1)
    out_kept, out_sent = add_halves(kept_out, swap(sent_out, *last))
    both_this, both_other = weight_grad(hidden_pieces, kept_both, after(sent_both, sent_out), True)
    grad_near = to_neighbour(both_this, both_other)
    down_line = along(down_grad.reshape(pairs, 2 * part, wide))
    sent = after(sent, down_line, both_other, kept_out)
    for k in range(2, steps_back - 1):
        kept, sent = scatter_stage(kept, sent, k)
    grad_kept, grad_got = scatter_stage(kept, after(sent, out_sent), steps_back - 1)
    out_kept, out_sent = scatter_stage(out_kept, out_sent, 0)
    out_first = out_sent
    out_kept, out_sent = scatter_stage(out_kept, out_sent, 1)
    out_second = out_sent
    both_back = along(after(grad_near, grad_got)).reshape(width, 2 * wide)

    grad_middle, branch_grad, moe_part = call(
        middle_back_body,
        [shape((rows, width), FULL), shape((rows, width), LOW), shape((16, width), FULL)],
        where, grad_kept, grad_got, middle, grad_rows, gains,
    )
    branch_pieces = [branch_grad]
    for b in reversed(t_masks):
        branch_pieces = branch_pieces + [swap(p, "tensor", b) for p in branch_pieces]
    sum_orders = orders[0], orders[0]
    kept_w, sent_w, first_kept, first_sent = call(
        functools.partial(
            attend_back_body, len(branch_pieces), q_cols, k_cols, rows, part, order, sum_orders
        ),
        [
            shape((width // 2, all_cols), FULL),
            shape((width // 2, all_cols), LOW),
            shape((length // 2, width), FULL),
            shape((length // 2, width), LOW),
        ],
        where, *branch_pieces[:-1], after(branch_pieces[-1], out_first), mixed, qkv, doc_row, doc_col, cosine, sine,
        first_hidden, weights,
        scratch=[
            pltpu.VMEM((length, width), LOW),
            pltpu.VMEM((length, max(q_cols, qkv_cols)), LOW),
            pltpu.VMEM((length, qkv_cols), LOW),
            pltpu.VMEM((width, all_cols), FULL),
        ],
        flops=2 * length * width * (2 * q_cols + 2 * qkv_cols),
    )
    got_w = swap(sent_w, "expert", e_bits[-1])
    attn_grad = kept_w + got_w.astype(FULL)
    kept, got = scatter_rows(first_kept, first_sent)
    (token_rows,) = call(
        functools.partial(tokens_back_body, rows),
        [shape((rows + 16, width), FULL)],
        where, tokens, kept, after(got, got_w, out_second), gains, grad_middle, moe_part,
    )
    gathered = all_rows(token_rows.astype(LOW))
    gathered = gathered.reshape(n_t, rows + 16, width).astype(FULL)
    grad_input = gathered[:, :rows].reshape(length, width)
    gain_sum = jnp.sum(gathered[:, rows : rows + 2], axis=0)

    blocks = gain_sum.reshape(2, n_e, part).transpose(1, 0, 2)

    half_rows = attn_grad.shape[0] // 2
    kept_w, sent_w = attn_grad[:half_rows], attn_grad[half_rows:].astype(LOW)
    blocks = after(blocks, sent_w)
    gain_grads = jnp.sum(lax.all_to_all(blocks, "expert", 0, 0, tiled=True), axis=0)
    out_sent = after(out_sent, both_back)
    for k, b in enumerate(reversed(e_bits[:-1])):
        attn_grad = kept_w + swap(sent_w, "expert", b).astype(FULL)
        half_rows = attn_grad.shape[0] // 2
        kept_w, sent_w = attn_grad[:half_rows], attn_grad[half_rows:].astype(LOW)
        if k == 0:
            out_kept, out_sent = scatter_stage(out_kept, out_sent, 2)
            out_sent = after(out_sent, sent_w)
    for k in range(3, steps_back):
        out_kept, out_sent = scatter_stage(out_kept, out_sent, k)
    output_rows = (middle + (out_kept + out_sent.astype(FULL))).astype(LOW)
    output = all_rows(output_rows)

    out_dims = [(part, hidden), (part, hidden), (hidden, part) if turn else (part, hidden)]

    def unpack(source, dims, turned):
        cols = source.shape[1]
        return call(
            functools.partial(unpack_body, own_experts, hidden, replicas, turned),
            [shape((EXPERTS,) + dims, FULL)] * (cols // wide),
            where, source,
            grid=(pairs,),
            in_specs=[pl.BlockSpec((2 * part, cols), lambda z: (z, 0))],
            out_specs=[at_pair(dims)] * (cols // wide),
        )

    sides_of = lambda this, other: jnp.where(
        side == 0, jnp.stack([this, other], axis=1), jnp.stack([other, this], axis=1)
    )
    down_this, down_other = split_sides(after(down_line, got_w))
    down_back = sides_of(down_this, swap(down_other, "expert", 1)).reshape(width, wide)
    shards = unpack(both_back, out_dims[0], False) + unpack(down_back, out_dims[2], turn)
    gate_shard, up_shard, down_shard = shards
    if not turn:
        down_shard = down_shard.transpose(0, 2, 1)

    return (
        output,
        grad_input,
        attn_grad[:, :q_cols],
        attn_grad[:, q_cols : q_cols + k_cols],
        attn_grad[:, q_cols + k_cols : qkv_cols],
        attn_grad[:, qkv_cols:].T,
        gain_grads[0],
        gain_grads[1],
        gate_shard,
        up_shard,
        down_shard,
    )


def solution(mesh):
    by_rows = P("expert", None)
    by_both = P("expert", "tensor")
    in_experts = P(None, "expert", "tensor")
    down_specs = P(None, "tensor", "expert")
    return jax.shard_map(
        local,
        mesh=mesh,
        in_specs=(by_rows,) * 5
        + (by_both,) * 3
        + (P("tensor", "expert"), P("expert"), P("expert"), in_experts, in_experts, down_specs),
        out_specs=(by_rows, by_rows)
        + (by_both,) * 3
        + (P("tensor", "expert"), P("expert"), P("expert"), in_experts, in_experts, down_specs),
        check_vma=False,
    )
```

```python
import functools

import jax
import jax.numpy as jnp
from jax import lax
from jax.experimental import pallas as pl
from jax.experimental.pallas import tpu as pltpu
from jax.sharding import PartitionSpec as P

HEAD_SIZE = 64
EXPERTS = 32
TOP = 8
EPS = 1e-06
THETA = 10000.0
MASKED = -1e30
LANES = 128
LIMIT = 24 * 1024 * 1024
LARGE = 56 * 1024 * 1024

LOW = jnp.bfloat16
FULL = jnp.float32
ROWS_ON_ROWS = (((0,), (0,)), ((), ()))
COLS_ON_ROWS = (((1,), (0,)), ((), ()))
COLS_ON_COLS = (((1,), (1,)), ((), ()))


def mul(left, right, dims=COLS_ON_ROWS):
    return lax.dot_general(left, right, dims, preferred_element_type=FULL)


def shape(dims, dtype):
    return jax.ShapeDtypeStruct(dims, dtype)


def call(body, outs, *args, grid=None, in_specs=None, out_specs=None, scratch=(), flops=0, limit=LIMIT):
    size = sum(a.size * a.dtype.itemsize for a in args)
    size += sum(o.size * jnp.dtype(o.dtype).itemsize for o in outs)
    whole = pl.BlockSpec(memory_space=pltpu.VMEM)
    if in_specs is None:
        in_specs = [whole] * (len(args) - 1)
    if out_specs is None:
        out_specs = [whole] * len(outs)
    extra = {} if grid is None else {"grid": grid}
    return pl.pallas_call(
        body,
        out_shape=list(outs),
        in_specs=[pl.BlockSpec(memory_space=pltpu.SMEM)] + list(in_specs),
        out_specs=list(out_specs),
        scratch_shapes=list(scratch),
        compiler_params=pltpu.CompilerParams(vmem_limit_bytes=limit),
        cost_estimate=pl.CostEstimate(flops=flops, bytes_accessed=size, transcendentals=0),
        **extra,
    )(*args)


def swap(field, axis, mask):
    count = lax.axis_size(axis)
    return lax.ppermute(field, axis, [(i, i ^ mask) for i in range(count)])


def after(field, *earlier):
    return lax.optimization_barrier((field, *earlier))[0]


def swap_by_parity(field, even, odd):
    n_e, n_t = lax.axis_size("expert"), lax.axis_size("tensor")
    pairs = []
    for e in range(n_e):
        for t in range(n_t):
            axis, mask = odd if t & 1 else even
            to = ((e ^ mask) * n_t + t) if axis == "expert" else (e * n_t + (t ^ mask))
            pairs.append((e * n_t + t, to))
    return lax.ppermute(field, ("expert", "tensor"), pairs)


def bits_of(count, first_bit=0):
    return [1 << b for b in reversed(range(first_bit, count.bit_length() - 1))]


def position_in(mask, bits):
    return sum(jnp.where(mask & b != 0, 1 << i, 0) for i, b in enumerate(bits))


def order_of(bits):
    order = [0]
    for b in bits:
        order = order + [k ^ b for k in order]
    return order


def rotate(field, cosine, sine):
    lane = lax.broadcasted_iota(jnp.int32, (field.shape[0], LANES), 1)
    low_half = lane % HEAD_SIZE < HEAD_SIZE // 2
    turned = []
    for at in range(0, field.shape[1], LANES):
        block = field[:, at : at + LANES]
        ahead = pltpu.roll(block, LANES - HEAD_SIZE // 2, 1)
        behind = pltpu.roll(block, HEAD_SIZE // 2, 1)
        turned.append(block * cosine + jnp.where(low_half, ahead, behind) * sine)
    return jnp.concatenate(turned, axis=1)


def admitted(doc_row, doc_col):
    length = doc_row.shape[1]
    row = lax.broadcasted_iota(jnp.int32, (length, length), 0)
    col = lax.broadcasted_iota(jnp.int32, (length, length), 1)
    return (col <= row) & (doc_row == doc_col)


def softmax_of(query, key, allowed):
    scores = mul(query, key, COLS_ON_COLS) * HEAD_SIZE**-0.5
    scores = jnp.where(allowed, scores, MASKED)
    raised = jnp.exp(scores - jnp.max(scores, axis=1, keepdims=True))
    return raised / jnp.sum(raised, axis=1, keepdims=True)


def place_rows(target, sources, orders, where, part, pitch):
    count = len(orders[0]) // len(sources)
    for p, (even, odd) in enumerate(zip(*orders)):
        at = pl.multiple_of((where[0] ^ jnp.where(where[1] & 1 == 0, even, odd)) * part, part)
        k = p % count * pitch
        target[pl.ds(at, part), :] = sources[p // count][k : k + part, :]


def pack_body(own, hid, replicas, turn, where, gate, up, down, down_out, *sided):
    side = where[0] & 1
    for j in range(own):
        at = slice(j * hid, (j + 1) * hid)
        for k in range(2):
            block = down[(k * own if replicas == 1 else 0) + j]
            down_out[0, k, :, at] = (block.T if turn else block).astype(LOW)
            place = ((side ^ k) * own if replicas == 1 else 0) + j
            sided[k][0, :, at] = gate[place].astype(LOW)
            up_at = slice((own + j) * hid, (own + j + 1) * hid)
            sided[k][0, :, up_at] = up[place].astype(LOW)


def interleave_body(part, where, this, other, out):
    for k, source in enumerate((this, other)):
        at = pl.multiple_of(((where[0] & 1) ^ k) * part, part)
        out[0, pl.ds(at, part), :] = source[0]


def attend_body(orders, n, part, pitch, q_cols, k_cols, rows, order, where, *refs):
    sources = refs[:n]
    tokens, gain_in, doc_row, doc_col, cosine, sine = refs[n : n + 6]
    weights, hidden, qkv_out, mixed_out, gain, kept, sent, mixed = refs[n + 6 :]
    place_rows(weights, sources, orders, where, part, pitch)
    if part % LANES == 0:
        count = len(orders[0]) // n
        for p, (even, odd) in enumerate(zip(*orders)):
            at = pl.multiple_of((where[0] ^ jnp.where(where[1] & 1 == 0, even, odd)) * part, part)
            k = p % count * pitch + part
            gain[:, pl.ds(at, part)] = sources[p // count][k : k + gain.shape[0], :part].astype(FULL)
    else:
        gain[...] = gain_in[...]
    x = tokens[...].astype(FULL)
    scale = lax.rsqrt(jnp.mean(x * x, axis=1, keepdims=True) + EPS)
    first = (x * scale * gain[0:1, :]).astype(LOW)
    hidden[...] = first
    qkv = mul(first, weights[:, : q_cols + 2 * k_cols])
    turned = rotate(qkv[:, : q_cols + k_cols], cosine[...], sine[...]).astype(LOW)
    values = qkv[:, q_cols + k_cols :].astype(LOW)
    qkv_out[:, : q_cols + k_cols] = turned
    qkv_out[:, q_cols + k_cols :] = values
    allowed = admitted(doc_row[...], doc_col[...])
    per_group = q_cols // k_cols
    for h in range(q_cols // HEAD_SIZE):
        at, g = h * HEAD_SIZE, h // per_group * HEAD_SIZE
        shares = softmax_of(
            turned[:, at : at + HEAD_SIZE],
            turned[:, q_cols + g : q_cols + g + HEAD_SIZE],
            allowed,
        ).astype(LOW)
        mixed[:, at : at + HEAD_SIZE] = mul(shares, values[:, g : g + HEAD_SIZE]).astype(LOW)
    for k, m in enumerate(order):
        at = pl.multiple_of((where[1] ^ m) * rows, rows)
        mixed_out[k * rows : (k + 1) * rows, :] = mixed[pl.ds(at, rows), :]
    product = mul(mixed_out[...], weights[:, q_cols + 2 * k_cols :], COLS_ON_COLS)
    half = kept.shape[0]
    kept[...] = product[:half]
    sent[...] = product[half:].astype(LOW)


def middle_body(rows, where, tokens, kept, got, gain, middle, hidden):
    at = pl.multiple_of(where[1] * rows, rows)
    m = tokens[pl.ds(at, rows), :].astype(FULL) + (kept[...] + got[...].astype(FULL))
    middle[...] = m
    scale = lax.rsqrt(jnp.mean(m * m, axis=1, keepdims=True) + EPS)
    hidden[...] = (m * scale * gain[1:2, :]).astype(LOW)


def pick_tile(buffer, sources, tiles, step):
    for k, source in enumerate(sources):

        @pl.when(step // tiles == k)
        def _():
            buffer[...] = source[...]


def owner_body(n_piece, tiles, part, own, hid, replicas, where, *refs):
    grads = refs[:n_piece]
    this, other, gate_out, back_out, weights, buffer = refs[n_piece:]
    width = weights.shape[0]
    step = pl.program_id(0)

    @pl.when(step == 0)
    def _():
        for z in range(this.shape[0]):
            for k, source in enumerate((this, other)):
                at = pl.multiple_of((2 * z + ((where[0] & 1) ^ k)) * part, part)
                weights[pl.ds(at, part), :] = source[z]

    pick_tile(buffer, grads, tiles, step)
    extra = buffer[:, width:].astype(FULL)
    lane = lax.broadcasted_iota(jnp.int32, extra.shape, 1)
    gate = pltpu.roll(extra, LANES - TOP, 1) + pltpu.roll(extra, LANES - 2 * TOP, 1)
    first = where[0] // replicas * own
    back = mul(buffer[:, :width], weights[...])
    table = jnp.zeros(extra.shape, FULL)
    for j in range(own):
        hit = (lane < TOP) & (extra == (first + j).astype(FULL))
        column = jnp.sum(jnp.where(hit, gate, 0.0), axis=1, keepdims=True)
        table = jnp.where(lane == j, column, table)
        back_out[:, j * hid : (j + 1) * hid] = back[:, j * hid : (j + 1) * hid] * column
    gate_out[...] = table


def expert_body(n_piece, tiles, own, hid, where, *refs):
    rows = refs[:n_piece]
    weights, gate, back, grad_hidden, active_out, grad_both, buffer = refs[n_piece:]
    pick_tile(buffer, rows, tiles, pl.program_id(0))
    wide = own * hid
    both = mul(buffer[...], weights[...])
    for j in range(own):
        at = slice(j * hid, (j + 1) * hid)
        up_at = slice(wide + j * hid, wide + (j + 1) * hid)
        pre, up = both[:, at], both[:, up_at]
        squash = 1.0 / (1.0 + jnp.exp(-pre))
        silu = pre * squash
        active = (silu * up).astype(LOW).astype(FULL)
        active_out[:, at] = (active * gate[:, j : j + 1]).astype(LOW)
        d = back[:, at]
        grad_both[:, at] = (d * up * squash * (1.0 + pre * (1.0 - squash))).astype(LOW)
        grad_both[:, up_at] = (d * silu).astype(LOW)
    product = mul(grad_both[...], weights[...], COLS_ON_COLS)
    grad_hidden[...] = product.astype(grad_hidden.dtype)


def out_body(where, active, weights, out):
    out[...] = mul(active[...], weights[...], COLS_ON_COLS).astype(out.dtype)


def weight_grad_body(n_source, part, where, *refs):
    sources = refs[:n_source]
    kept, sent, *outs, column, total = refs[n_source:]
    half, size = kept.shape[0], sources[0].shape[0]
    for k, source in enumerate(sources):
        column[k * size : (k + 1) * size, :] = source[...]
    product = mul(column[:half], kept[...], ROWS_ON_ROWS)
    total[...] = (product + mul(column[half:], sent[...], ROWS_ON_ROWS)).astype(LOW)
    for z in range(total.shape[0] // (2 * part)):
        for k in range(2):
            if len(outs) == 2:
                at = pl.multiple_of((2 * z + ((where[0] & 1) ^ k)) * part, part)
                outs[k][z] = total[pl.ds(at, part), :]
            else:
                at = (2 * z + k) * part
                outs[0][z, k] = total[at : at + part, :]


def middle_back_body(where, *refs):
    kept, got, middle, grad, gain, grad_middle, low, gain_part = refs
    total = kept[...] + got[...].astype(FULL)
    m = middle[...]
    scale = lax.rsqrt(jnp.mean(m * m, axis=1, keepdims=True) + EPS)
    gain_part[...] = jnp.broadcast_to(
        jnp.sum(total * m * scale, axis=0, keepdims=True), gain_part.shape
    )
    weighted = total * gain[1:2, :]
    inner = jnp.mean(weighted * m, axis=1, keepdims=True)
    back = grad[...].astype(FULL) + (scale * weighted - m * (scale * scale * scale) * inner)
    grad_middle[...] = back
    low[...] = back.astype(LOW)


def attend_back_body(n_piece, q_cols, k_cols, rows, part, order, orders, where, *refs):
    pieces = refs[:n_piece]
    mixed, qkv_in, doc_row, doc_col, cosine, sine, hidden, weights = refs[n_piece : n_piece + 8]
    kept, sent, first_kept, first_sent, branch, natural, grad_qkv, grads = refs[n_piece + 8 :]
    for k in range(n_piece):
        branch[k * rows : (k + 1) * rows, :] = pieces[k][...]
    grad_mixed = mul(branch[...], weights[:, q_cols + 2 * k_cols :]).astype(LOW)
    for k, m in enumerate(order):
        at = pl.multiple_of((where[1] ^ m) * rows, rows)
        natural[pl.ds(at, rows), :q_cols] = grad_mixed[k * rows : (k + 1) * rows]
    qk = q_cols + k_cols
    total = qk + k_cols
    grads[:, total:] = mul(branch[...], mixed[...], ROWS_ON_ROWS)
    allowed = admitted(doc_row[...], doc_col[...])
    per_group = q_cols // k_cols
    query_grads, key_grads, value_grads = [], [], []
    for g in range(k_cols // HEAD_SIZE):
        key = qkv_in[:, q_cols + g * HEAD_SIZE : q_cols + (g + 1) * HEAD_SIZE]
        value = qkv_in[:, qk + g * HEAD_SIZE : qk + (g + 1) * HEAD_SIZE]
        key_grad = value_grad = None
        for h in range(g * per_group, (g + 1) * per_group):
            at = slice(h * HEAD_SIZE, (h + 1) * HEAD_SIZE)
            query = qkv_in[:, at]
            shares = softmax_of(query, key, allowed)
            grad = natural[:, at]
            grad_shares = mul(grad, value, COLS_ON_COLS)
            inner = jnp.sum(shares * grad_shares, axis=1, keepdims=True)
            grad_scores = (shares * (grad_shares - inner)).astype(LOW)
            query_grads.append(mul(grad_scores, key))
            dk = mul(grad_scores, query, ROWS_ON_ROWS)
            dv = mul(shares.astype(LOW), grad, ROWS_ON_ROWS)
            key_grad = dk if key_grad is None else key_grad + dk
            value_grad = dv if value_grad is None else value_grad + dv
        key_grads.append(key_grad)
        value_grads.append(value_grad)
    turned = jnp.concatenate(query_grads + key_grads, axis=1) * HEAD_SIZE**-0.5
    grad_qkv[:, :qk] = rotate(turned, cosine[...], -sine[...]).astype(LOW)
    grad_qkv[:, qk:] = jnp.concatenate(value_grads, axis=1).astype(LOW)
    grads[:, :total] = mul(hidden[...], grad_qkv[...], ROWS_ON_ROWS)
    for p, (even, odd) in enumerate(zip(*orders)):
        at = pl.multiple_of((where[0] ^ jnp.where(where[1] & 1 == 0, even, odd)) * part, part)
        target = kept if p < len(orders[0]) // 2 else sent
        k = p % (len(orders[0]) // 2)
        target[k * part : (k + 1) * part, :] = grads[pl.ds(at, part), :].astype(target.dtype)
    for k, m in enumerate(order):
        at = pl.multiple_of((where[1] ^ m) * rows, rows)
        natural[k * rows : (k + 1) * rows, :total] = grad_qkv[pl.ds(at, rows), :]
    product = mul(natural[:, :total], weights[:, :total], COLS_ON_COLS)
    half = first_kept.shape[0]
    first_kept[...] = product[:half]
    first_sent[...] = product[half:].astype(LOW)


def tokens_back_body(rows, where, tokens, kept, got, gain, grad_middle, moe_part, out):
    at = pl.multiple_of(where[1] * rows, rows)
    x = tokens[pl.ds(at, rows), :].astype(FULL)
    scale = lax.rsqrt(jnp.mean(x * x, axis=1, keepdims=True) + EPS)
    first = kept[...] + got[...].astype(FULL)
    attn_part = jnp.sum(first * x * scale, axis=0, keepdims=True)
    weighted = first * gain[0:1, :]
    inner = jnp.mean(weighted * x, axis=1, keepdims=True)
    out[:rows] = grad_middle[...] + (scale * weighted - x * (scale * scale * scale) * inner)
    line = lax.broadcasted_iota(jnp.int32, moe_part.shape, 0)
    out[rows:] = jnp.where(line == 0, attn_part, jnp.where(line == 1, moe_part[...], 0.0))


def unpack_body(own, hid, replicas, turn, where, source, *outs):
    part = source.shape[0] // 2
    for k in range(own * len(outs)):
        out, j = outs[k // own], k % own
        cols = slice(k * hid, (k + 1) * hid)
        pieces = [source[i * part : (i + 1) * part, cols].astype(FULL) for i in range(2)]
        pieces = [piece.T for piece in pieces] if turn else pieces
        if replicas == 1:
            out[j] = pieces[0]
            out[own + j] = pieces[1]
        else:
            first = 2 * pl.program_id(0) % replicas == 0
            out[j] = pieces[0] + pieces[1] + jnp.where(first, 0.0, out[j])


def local(
    tokens,
    cotangent,
    segments,
    routes,
    gates,
    w_query,
    key_projection,
    value_projection,
    w_out,
    gain_attn,
    gain_moe,
    w_gate,
    w_up,
    w_down,
):
    n_e, n_t = lax.axis_size("expert"), lax.axis_size("tensor")
    e, t = lax.axis_index("expert"), lax.axis_index("tensor")
    where = jnp.stack([e, t]).astype(jnp.int32)
    replicas = max(1, n_e // EXPERTS)
    own_experts = EXPERTS * replicas // n_e
    first_bit = replicas.bit_length() - 1
    length, width = tokens.shape
    part = width // n_e
    rows = length // n_t
    q_cols, k_cols = w_query.shape[1], key_projection.shape[1]
    qkv_cols = q_cols + 2 * k_cols
    hidden = w_gate.shape[2]
    wide = own_experts * hidden

    pad = 16
    all_cols = qkv_cols + q_cols
    gain_rows = jnp.pad(jnp.stack([gain_attn, gain_moe]), ((0, pad - 2), (0, all_cols - part)))
    shard = jnp.concatenate([w_query, key_projection, value_projection, w_out.T], axis=1)
    shard = jnp.concatenate([shard, gain_rows]).astype(LOW)

    e_bits, t_bits = bits_of(n_e), bits_of(n_t)
    even_bits, odd_bits = e_bits, e_bits[-1:] + e_bits[:-1]
    orders = order_of(even_bits), order_of(odd_bits)
    by_parity = [(("expert", a), ("expert", b)) for a, b in zip(even_bits, odd_bits)]

    def every(shard, ready, later):
        came, sends = [], []
        for k, (even, odd) in enumerate(by_parity):
            if k == 1:
                shard, *ready = lax.optimization_barrier((shard, *ready))
            if k == 2:
                shard = after(shard, later)
            sends.append(shard)
            came.append(swap_by_parity(shard, even, odd))
            shard = jnp.concatenate([shard, came[-1]])
        return [sends[-1], came[-1]], came, sends, ready

    pairs = n_e // 2
    turn = part % LANES == 0
    pair_experts = 2 * own_experts // replicas or 1
    at_pair = lambda dims: pl.BlockSpec(
        (pair_experts,) + dims, lambda z: (2 * z // max(2, replicas), 0, 0)
    )
    sources = [w_gate, w_up, w_down if turn else w_down.transpose(0, 2, 1)]
    sided = pl.BlockSpec((1, part, 2 * wide), lambda z: (z, 0, 0))
    packed = call(
        functools.partial(pack_body, own_experts, hidden, replicas, turn),
        [shape((pairs, 2, part, wide), LOW)] + [shape((pairs, part, 2 * wide), LOW)] * 2,
        where, *sources,
        grid=(pairs,),
        in_specs=[at_pair(w.shape[1:]) for w in sources],
        out_specs=[pl.BlockSpec((1, 2, part, wide), lambda z: (z, 0, 0, 0))] + [sided] * 2,
    )
    side = e & 1
    lines = [[z * 2 + k for z in range(n_e // 2)] for k in range(2)]

    def along(blocks):
        return lax.all_to_all(
            blocks, "expert", 0, 0, tiled=True, axis_index_groups=lines
        )

    def split_sides(blocks):
        blocks = blocks.reshape(pairs, 2, part, blocks.shape[-1])
        this = lax.dynamic_index_in_dim(blocks, side, 1, keepdims=False)
        return this, lax.dynamic_index_in_dim(blocks, 1 - side, 1, keepdims=False)

    def from_neighbour(blocks, *earlier):
        cols = blocks.shape[-1]
        blocks = along(after(blocks.reshape(pairs, 2 * part, cols), *earlier))
        this, other = split_sides(blocks)
        return this, swap(other, "expert", 1)

    def interleave(this, other):
        cols = this.shape[-1]
        block = pl.BlockSpec((1, part, cols), lambda z: (z, 0, 0))
        return call(
            functools.partial(interleave_body, part),
            [shape((pairs, 2 * part, cols), LOW)],
            where, this, other,
            grid=(pairs,),
            in_specs=[block, block],
            out_specs=[pl.BlockSpec((1, 2 * part, cols), lambda z: (z, 0, 0))],
        )[0]

    def to_neighbour(this, other, *earlier):
        return interleave(this, swap(after(other, *earlier), "expert", 1))

    e_path = [("expert", b) for b in bits_of(n_e, first_bit)]
    t_path = [("tensor", b) for b in t_bits]
    even_path, odd_path = e_path + t_path[:-1], e_path[:-1] + t_path[:-1] + e_path[-1:]
    path = list(zip(even_path, odd_path))
    last = t_path[-1]

    own = t * rows
    grad_rows = lax.dynamic_slice_in_dim(cotangent, own, rows, 0)
    gate_rows = lax.dynamic_slice_in_dim(gates, own, rows, 0)
    route_rows = lax.dynamic_slice_in_dim(routes, own, rows, 0)
    gate_high = gate_rows.astype(LOW)
    gate_rest = (gate_rows - gate_high.astype(FULL)).astype(LOW)
    extra = jnp.concatenate([route_rows.astype(LOW), gate_high, gate_rest], axis=1)
    extra = jnp.pad(extra, ((0, 0), (0, LANES - 3 * TOP)))
    grad_steps = [jnp.concatenate([grad_rows, extra], axis=1)]
    grad_first = swap_by_parity(grad_steps[0], *path[0])
    attn_arrays, attn_came, attn_sends, packed = every(shard, packed, grad_first)
    grad_steps.append(jnp.concatenate([grad_steps[0], grad_first]))
    grad_second = swap_by_parity(after(grad_steps[1], attn_sends[-1]), *path[1])
    grad_steps.append(jnp.concatenate([grad_steps[1], grad_second]))
    down_this, down_other = from_neighbour(packed[0], attn_came[-1])
    near = to_neighbour(*packed[1:], attn_came[-1])
    pitch = part + pad
    gains = jnp.zeros((pad, LANES), FULL)
    if part % LANES:
        held = jnp.concatenate(
            [a.reshape(-1, pitch, all_cols)[:, part:, :part] for a in attn_arrays]
        ).astype(FULL)
        on_even = [position_in(e ^ k, even_bits) for k in range(n_e)]
        on_odd = [position_in(e ^ k, odd_bits) for k in range(n_e)]
        gains = jnp.concatenate(
            [
                lax.dynamic_index_in_dim(held, jnp.where(t & 1 == 0, a, b), 0, keepdims=False)
                for a, b in zip(on_even, on_odd)
            ],
            axis=1,
        )

    def add_halves(kept, got):
        half = got.shape[0] // 2
        return kept[:half] + got[:half].astype(FULL), (
            kept[half:] + got[half:].astype(FULL)
        ).astype(LOW)

    def scatter_stage(kept, sent, k):
        got = swap_by_parity(sent, *path[-1 - k])
        return (kept, got) if k == len(path) - 1 else add_halves(kept, got)

    documents = segments[0]
    doc_row, doc_col = documents[None, :], documents[:, None]
    index = jnp.arange(length)
    same = (index[None, :] < index[:, None]) & (doc_row == doc_col)
    position = jnp.sum(same.astype(FULL), axis=1, keepdims=True)
    lane = jnp.arange(LANES)
    freqs = THETA ** (-2.0 * (lane % (HEAD_SIZE // 2)).astype(FULL) / HEAD_SIZE)
    angle = position * freqs[None, :]
    cosine = jnp.cos(angle)
    sine = jnp.sin(angle) * jnp.where(lane % HEAD_SIZE < HEAD_SIZE // 2, -1.0, 1.0)[None, :]
    t_masks = t_bits[::-1]
    order = order_of(t_bits)
    weights, first_hidden, qkv, mixed, gains, kept, sent = call(
        functools.partial(attend_body, orders, 2, part, pitch, q_cols, k_cols, rows, order),
        [
            shape((width, all_cols), LOW),
            shape((length, width), LOW),
            shape((length, qkv_cols), LOW),
            shape((length, q_cols), LOW),
            shape((pad, width), FULL),
            shape((length // 2, width), FULL),
            shape((length // 2, width), LOW),
        ],
        where, *attn_arrays[:-1], after(attn_arrays[-1], grad_second), tokens, gains, doc_row, doc_col, cosine, sine,
        scratch=[pltpu.VMEM((length, q_cols), LOW)],
        flops=2 * length * (width * qkv_cols + 2 * length * q_cols),
    )
    def all_rows(field):
        size = field.shape[0]
        for b in t_bits:
            field = jnp.concatenate([field, swap(field, "tensor", b)])
        at = [position_in(t ^ k, t_bits) * size for k in range(n_t)]
        return jnp.concatenate([lax.dynamic_slice_in_dim(field, a, size, 0) for a in at])

    def scatter_rows(kept, sent):
        for b in t_masks[:-1]:
            total = kept + swap(sent, "tensor", b).astype(FULL)
            half = total.shape[0] // 2
            kept, sent = total[:half], total[half:].astype(LOW)
        return kept, swap(sent, "tensor", t_masks[-1])

    grad_third = swap_by_parity(grad_steps[-1], *path[2])
    kept, got = scatter_rows(kept, sent)
    middle, second_hidden = call(
        functools.partial(middle_body, rows),
        [shape((rows, width), FULL), shape((rows, width), LOW)],
        where, tokens, kept, after(got, grad_third, down_this), gains,
    )

    hidden_field = second_hidden
    for k, (even, odd) in enumerate(path):
        if k == 1:
            hidden_field = after(hidden_field, near)
        if k == 2:
            hidden_field = after(hidden_field, down_other, grad_got)
        hidden_got = swap_by_parity(hidden_field, even, odd)
        if k == 1:
            gate_up_rows = along(after(near, hidden_got)).reshape(width, 2 * wide)
        hidden_pieces = [hidden_field, hidden_got]
        hidden_field = jnp.concatenate(hidden_pieces)
        if k == 0:
            grad_field, grad_got = grad_steps[-1], grad_third
            for k in range(3, len(path)):
                grad_field = jnp.concatenate([grad_field, grad_got])
                grad_got = swap_by_parity(grad_field, *path[k])
            grad_pieces = [grad_field, grad_got]
    hidden_pieces = hidden_pieces + [swap(p, *last) for p in hidden_pieces]
    grad_pieces = grad_pieces + [swap(p, *last) for p in grad_pieces]
    size = 512
    total_rows = sum(p.shape[0] for p in grad_pieces)
    steps = total_rows // size
    whole = lambda a: pl.BlockSpec(a.shape, lambda i: (0,) * a.ndim)
    tile = lambda cols: pl.BlockSpec((size, cols), lambda i: (i, 0))

    def tiles_of(pieces):
        count = pieces[0].shape[0] // size
        return count, [
            pl.BlockSpec((size, p.shape[1]), lambda i, k=k: (jnp.clip(i - k * count, 0, count - 1), 0))
            for k, p in enumerate(pieces)
        ]

    tiles, specs = tiles_of(grad_pieces)
    gate_table, back, down_rows = call(
        functools.partial(owner_body, len(grad_pieces), tiles, part, own_experts, hidden, replicas),
        [
            shape((total_rows, LANES), FULL),
            shape((total_rows, wide), FULL),
            shape((width, wide), LOW),
        ],
        where, *grad_pieces, down_this, down_other,
        grid=(steps,),
        in_specs=specs + [whole(down_this), whole(down_other)],
        out_specs=[tile(LANES), tile(wide), pl.BlockSpec((width, wide), lambda i: (0, 0))],
        scratch=[pltpu.VMEM((size, width + LANES), LOW)],
        flops=2 * total_rows * width * wide,
        limit=LARGE,
    )
    half = steps // 2

    def experts(chosen, first, out_type):
        later = lambda cols: pl.BlockSpec((size, cols), lambda i: (i + first, 0))
        tiles, specs = tiles_of(chosen)
        return call(
            functools.partial(expert_body, len(chosen), tiles, own_experts, hidden),
            [
                shape((half * size, width), out_type),
                shape((half * size, wide), LOW),
                shape((half * size, 2 * wide), LOW),
            ],
            where, *chosen, gate_up_rows, gate_table, back,
            grid=(half,),
            in_specs=specs
            + [whole(gate_up_rows), later(LANES), later(wide)],
            out_specs=[tile(width), tile(wide), tile(2 * wide)],
            scratch=[pltpu.VMEM((size, width), LOW)],
            flops=2 * half * size * width * 4 * wide,
            limit=LARGE,
        )

    sent_hidden, sent_active, sent_both = experts(hidden_pieces[2:], half, LOW)
    kept_hidden, kept_active, kept_both = experts(hidden_pieces[:2], 0, FULL)

    block = 256
    column = lambda a: pl.BlockSpec((a.shape[0], block), lambda i: (0, i))

    def weight_grad(sources, kept, sent, sided):
        cols = kept.shape[1]
        dims = [(part, cols)] * 2 if sided else [(2, part, cols)]
        count = block // (2 * part)
        return call(
            functools.partial(weight_grad_body, len(sources), part),
            [shape((pairs,) + d, LOW) for d in dims],
            where, *sources, kept, sent,
            grid=(width // block,),
            in_specs=[column(a) for a in sources] + [whole(kept), whole(sent)],
            out_specs=[pl.BlockSpec((count,) + d, lambda i, n=len(d): (i,) + (0,) * n) for d in dims],
            scratch=[pltpu.VMEM((total_rows, block), LOW), pltpu.VMEM((block, cols), LOW)],
            flops=2 * total_rows * width * cols,
            limit=LARGE,
        )

    hidden_kept, hidden_sent = add_halves(kept_hidden, swap(sent_hidden, *last))
    def down(active, out_type):
        return call(
            out_body,
            [shape((half * size, width), out_type)],
            where, active, down_rows,
            grid=(half,),
            in_specs=[tile(wide), whole(down_rows)],
            out_specs=[tile(width)],
            flops=2 * half * size * width * wide,
            limit=LARGE,
        )[0]

    steps_back = len(path)
    kept, sent = scatter_stage(hidden_kept, hidden_sent, 0)
    (down_grad,) = weight_grad(grad_pieces, kept_active, after(sent_active, hidden_sent), False)
    sent_out = down(after(sent_active, down_grad), LOW)
    kept_out = down(after(kept_active, down_grad), FULL)
    kept, sent = scatter_stage(kept, after(sent, down_grad), 1)
    out_kept, out_sent = add_halves(kept_out, swap(sent_out, *last))
    both_this, both_other = weight_grad(hidden_pieces, kept_both, after(sent_both, sent_out), True)
    grad_near = to_neighbour(both_this, both_other)
    down_line = along(down_grad.reshape(pairs, 2 * part, wide))
    sent = after(sent, down_line, both_other)
    for k in range(2, steps_back - 1):
        kept, sent = scatter_stage(kept, sent, k)
    grad_kept, grad_got = scatter_stage(kept, after(sent, out_sent), steps_back - 1)
    out_kept, out_sent = scatter_stage(out_kept, out_sent, 0)
    out_first = out_sent
    out_kept, out_sent = scatter_stage(out_kept, out_sent, 1)
    out_second = out_sent
    both_back = along(after(grad_near, grad_got)).reshape(width, 2 * wide)

    grad_middle, branch_grad, moe_part = call(
        middle_back_body,
        [shape((rows, width), FULL), shape((rows, width), LOW), shape((16, width), FULL)],
        where, grad_kept, grad_got, middle, grad_rows, gains,
    )
    branch_pieces = [branch_grad]
    for b in reversed(t_masks):
        branch_pieces = branch_pieces + [swap(p, "tensor", b) for p in branch_pieces]
    sum_orders = orders[0], orders[0]
    kept_w, sent_w, first_kept, first_sent = call(
        functools.partial(
            attend_back_body, len(branch_pieces), q_cols, k_cols, rows, part, order, sum_orders
        ),
        [
            shape((width // 2, all_cols), FULL),
            shape((width // 2, all_cols), LOW),
            shape((length // 2, width), FULL),
            shape((length // 2, width), LOW),
        ],
        where, *branch_pieces[:-1], after(branch_pieces[-1], out_first), mixed, qkv, doc_row, doc_col, cosine, sine,
        first_hidden, weights,
        scratch=[
            pltpu.VMEM((length, width), LOW),
            pltpu.VMEM((length, max(q_cols, qkv_cols)), LOW),
            pltpu.VMEM((length, qkv_cols), LOW),
            pltpu.VMEM((width, all_cols), FULL),
        ],
        flops=2 * length * width * (2 * q_cols + 2 * qkv_cols),
    )
    got_w = swap(sent_w, "expert", e_bits[-1])
    attn_grad = kept_w + got_w.astype(FULL)
    kept, got = scatter_rows(first_kept, first_sent)
    (token_rows,) = call(
        functools.partial(tokens_back_body, rows),
        [shape((rows + 16, width), FULL)],
        where, tokens, kept, after(got, got_w, out_second), gains, grad_middle, moe_part,
    )
    gathered = all_rows(token_rows.astype(LOW))
    gathered = gathered.reshape(n_t, rows + 16, width).astype(FULL)
    grad_input = gathered[:, :rows].reshape(length, width)
    gain_sum = jnp.sum(gathered[:, rows : rows + 2], axis=0)

    blocks = gain_sum.reshape(2, n_e, part).transpose(1, 0, 2)

    half_rows = attn_grad.shape[0] // 2
    kept_w, sent_w = attn_grad[:half_rows], attn_grad[half_rows:].astype(LOW)
    blocks = after(blocks, sent_w)
    gain_grads = jnp.sum(lax.all_to_all(blocks, "expert", 0, 0, tiled=True), axis=0)
    out_sent = after(out_sent, both_back)
    for k, b in enumerate(reversed(e_bits[:-1])):
        attn_grad = kept_w + swap(sent_w, "expert", b).astype(FULL)
        half_rows = attn_grad.shape[0] // 2
        kept_w, sent_w = attn_grad[:half_rows], attn_grad[half_rows:].astype(LOW)
        if k == 0:
            out_kept, out_sent = scatter_stage(out_kept, out_sent, 2)
            out_sent = after(out_sent, sent_w)
    for k in range(3, steps_back):
        out_kept, out_sent = scatter_stage(out_kept, out_sent, k)
    output_rows = (middle + (out_kept + out_sent.astype(FULL))).astype(LOW)
    output = all_rows(output_rows)

    out_dims = [(part, hidden), (part, hidden), (hidden, part) if turn else (part, hidden)]

    def unpack(source, dims, turned):
        cols = source.shape[1]
        return call(
            functools.partial(unpack_body, own_experts, hidden, replicas, turned),
            [shape((EXPERTS,) + dims, FULL)] * (cols // wide),
            where, source,
            grid=(pairs,),
            in_specs=[pl.BlockSpec((2 * part, cols), lambda z: (z, 0))],
            out_specs=[at_pair(dims)] * (cols // wide),
        )

    sides_of = lambda this, other: jnp.where(
        side == 0, jnp.stack([this, other], axis=1), jnp.stack([other, this], axis=1)
    )
    down_this, down_other = split_sides(after(down_line, got_w))
    down_back = sides_of(down_this, swap(down_other, "expert", 1)).reshape(width, wide)
    shards = unpack(both_back, out_dims[0], False) + unpack(down_back, out_dims[2], turn)
    gate_shard, up_shard, down_shard = shards
    if not turn:
        down_shard = down_shard.transpose(0, 2, 1)

    return (
        output,
        grad_input,
        attn_grad[:, :q_cols],
        attn_grad[:, q_cols : q_cols + k_cols],
        attn_grad[:, q_cols + k_cols : qkv_cols],
        attn_grad[:, qkv_cols:].T,
        gain_grads[0],
        gain_grads[1],
        gate_shard,
        up_shard,
        down_shard,
    )


def solution(mesh):
    by_rows = P("expert", None)
    by_both = P("expert", "tensor")
    in_experts = P(None, "expert", "tensor")
    down_specs = P(None, "tensor", "expert")
    return jax.shard_map(
        local,
        mesh=mesh,
        in_specs=(by_rows,) * 5
        + (by_both,) * 3
        + (P("tensor", "expert"), P("expert"), P("expert"), in_experts, in_experts, down_specs),
        out_specs=(by_rows, by_rows)
        + (by_both,) * 3
        + (P("tensor", "expert"), P("expert"), P("expert"), in_experts, in_experts, down_specs),
        check_vma=False,
    )
```

```python
import functools

import jax
import jax.numpy as jnp
from jax import lax
from jax.experimental import pallas as pl
from jax.experimental.pallas import tpu as pltpu
from jax.sharding import PartitionSpec as P

HEAD_SIZE = 64
EXPERTS = 32
TOP = 8
EPS = 1e-06
THETA = 10000.0
MASKED = -1e30
LANES = 128
LIMIT = 24 * 1024 * 1024
LARGE = 56 * 1024 * 1024

LOW = jnp.bfloat16
FULL = jnp.float32
ROWS_ON_ROWS = (((0,), (0,)), ((), ()))
COLS_ON_ROWS = (((1,), (0,)), ((), ()))
COLS_ON_COLS = (((1,), (1,)), ((), ()))


def mul(left, right, dims=COLS_ON_ROWS):
    return lax.dot_general(left, right, dims, preferred_element_type=FULL)


def shape(dims, dtype):
    return jax.ShapeDtypeStruct(dims, dtype)


def call(body, outs, *args, grid=None, in_specs=None, out_specs=None, scratch=(), flops=0, limit=LIMIT):
    size = sum(a.size * a.dtype.itemsize for a in args)
    size += sum(o.size * jnp.dtype(o.dtype).itemsize for o in outs)
    whole = pl.BlockSpec(memory_space=pltpu.VMEM)
    if in_specs is None:
        in_specs = [whole] * (len(args) - 1)
    if out_specs is None:
        out_specs = [whole] * len(outs)
    extra = {} if grid is None else {"grid": grid}
    return pl.pallas_call(
        body,
        out_shape=list(outs),
        in_specs=[pl.BlockSpec(memory_space=pltpu.SMEM)] + list(in_specs),
        out_specs=list(out_specs),
        scratch_shapes=list(scratch),
        compiler_params=pltpu.CompilerParams(vmem_limit_bytes=limit),
        cost_estimate=pl.CostEstimate(flops=flops, bytes_accessed=size, transcendentals=0),
        **extra,
    )(*args)


def swap(field, axis, mask):
    count = lax.axis_size(axis)
    return lax.ppermute(field, axis, [(i, i ^ mask) for i in range(count)])


def after(field, *earlier):
    return lax.optimization_barrier((field, *earlier))[0]


def swap_by_parity(field, even, odd):
    n_e, n_t = lax.axis_size("expert"), lax.axis_size("tensor")
    pairs = []
    for e in range(n_e):
        for t in range(n_t):
            axis, mask = odd if t & 1 else even
            to = ((e ^ mask) * n_t + t) if axis == "expert" else (e * n_t + (t ^ mask))
            pairs.append((e * n_t + t, to))
    return lax.ppermute(field, ("expert", "tensor"), pairs)


def bits_of(count, first_bit=0):
    return [1 << b for b in reversed(range(first_bit, count.bit_length() - 1))]


def position_in(mask, bits):
    return sum(jnp.where(mask & b != 0, 1 << i, 0) for i, b in enumerate(bits))


def order_of(bits):
    order = [0]
    for b in bits:
        order = order + [k ^ b for k in order]
    return order


def rotate(field, cosine, sine):
    lane = lax.broadcasted_iota(jnp.int32, (field.shape[0], LANES), 1)
    low_half = lane % HEAD_SIZE < HEAD_SIZE // 2
    turned = []
    for at in range(0, field.shape[1], LANES):
        block = field[:, at : at + LANES]
        ahead = pltpu.roll(block, LANES - HEAD_SIZE // 2, 1)
        behind = pltpu.roll(block, HEAD_SIZE // 2, 1)
        turned.append(block * cosine + jnp.where(low_half, ahead, behind) * sine)
    return jnp.concatenate(turned, axis=1)


def admitted(doc_row, doc_col):
    length = doc_row.shape[1]
    row = lax.broadcasted_iota(jnp.int32, (length, length), 0)
    col = lax.broadcasted_iota(jnp.int32, (length, length), 1)
    return (col <= row) & (doc_row == doc_col)


def softmax_of(query, key, allowed):
    scores = mul(query, key, COLS_ON_COLS) * HEAD_SIZE**-0.5
    scores = jnp.where(allowed, scores, MASKED)
    raised = jnp.exp(scores - jnp.max(scores, axis=1, keepdims=True))
    return raised / jnp.sum(raised, axis=1, keepdims=True)


def place_rows(target, sources, orders, where, part, pitch):
    count = len(orders[0]) // len(sources)
    for p, (even, odd) in enumerate(zip(*orders)):
        at = pl.multiple_of((where[0] ^ jnp.where(where[1] & 1 == 0, even, odd)) * part, part)
        k = p % count * pitch
        target[pl.ds(at, part), :] = sources[p // count][k : k + part, :]


def pack_body(own, hid, replicas, turn, where, gate, up, down, down_out, *sided):
    side = where[0] & 1
    for j in range(own):
        at = slice(j * hid, (j + 1) * hid)
        for k in range(2):
            block = down[(k * own if replicas == 1 else 0) + j]
            down_out[0, k, :, at] = (block.T if turn else block).astype(LOW)
            place = ((side ^ k) * own if replicas == 1 else 0) + j
            sided[k][0, :, at] = gate[place].astype(LOW)
            up_at = slice((own + j) * hid, (own + j + 1) * hid)
            sided[k][0, :, up_at] = up[place].astype(LOW)


def interleave_body(part, where, this, other, out):
    for k, source in enumerate((this, other)):
        at = pl.multiple_of(((where[0] & 1) ^ k) * part, part)
        out[0, pl.ds(at, part), :] = source[0]


def attend_body(orders, n, part, pitch, q_cols, k_cols, rows, order, where, *refs):
    sources = refs[:n]
    tokens, gain_in, doc_row, doc_col, cosine, sine = refs[n : n + 6]
    weights, hidden, qkv_out, mixed_out, gain, kept, sent, mixed = refs[n + 6 :]
    place_rows(weights, sources, orders, where, part, pitch)
    if part % LANES == 0:
        count = len(orders[0]) // n
        for p, (even, odd) in enumerate(zip(*orders)):
            at = pl.multiple_of((where[0] ^ jnp.where(where[1] & 1 == 0, even, odd)) * part, part)
            k = p % count * pitch + part
            gain[:, pl.ds(at, part)] = sources[p // count][k : k + gain.shape[0], :part].astype(FULL)
    else:
        gain[...] = gain_in[...]
    x = tokens[...].astype(FULL)
    scale = lax.rsqrt(jnp.mean(x * x, axis=1, keepdims=True) + EPS)
    first = (x * scale * gain[0:1, :]).astype(LOW)
    hidden[...] = first
    qkv = mul(first, weights[:, : q_cols + 2 * k_cols])
    turned = rotate(qkv[:, : q_cols + k_cols], cosine[...], sine[...]).astype(LOW)
    values = qkv[:, q_cols + k_cols :].astype(LOW)
    qkv_out[:, : q_cols + k_cols] = turned
    qkv_out[:, q_cols + k_cols :] = values
    allowed = admitted(doc_row[...], doc_col[...])
    per_group = q_cols // k_cols
    for h in range(q_cols // HEAD_SIZE):
        at, g = h * HEAD_SIZE, h // per_group * HEAD_SIZE
        shares = softmax_of(
            turned[:, at : at + HEAD_SIZE],
            turned[:, q_cols + g : q_cols + g + HEAD_SIZE],
            allowed,
        ).astype(LOW)
        mixed[:, at : at + HEAD_SIZE] = mul(shares, values[:, g : g + HEAD_SIZE]).astype(LOW)
    for k, m in enumerate(order):
        at = pl.multiple_of((where[1] ^ m) * rows, rows)
        mixed_out[k * rows : (k + 1) * rows, :] = mixed[pl.ds(at, rows), :]
    product = mul(mixed_out[...], weights[:, q_cols + 2 * k_cols :], COLS_ON_COLS)
    half = kept.shape[0]
    kept[...] = product[:half]
    sent[...] = product[half:].astype(LOW)


def middle_body(rows, where, tokens, kept, got, gain, middle, hidden):
    at = pl.multiple_of(where[1] * rows, rows)
    m = tokens[pl.ds(at, rows), :].astype(FULL) + (kept[...] + got[...].astype(FULL))
    middle[...] = m
    scale = lax.rsqrt(jnp.mean(m * m, axis=1, keepdims=True) + EPS)
    hidden[...] = (m * scale * gain[1:2, :]).astype(LOW)


def pick_tile(buffer, sources, tiles, step):
    for k, source in enumerate(sources):

        @pl.when(step // tiles == k)
        def _():
            buffer[...] = source[...]


def owner_body(n_piece, tiles, part, own, hid, replicas, where, *refs):
    grads = refs[:n_piece]
    this, other, gate_out, back_out, weights, buffer = refs[n_piece:]
    width = weights.shape[0]
    step = pl.program_id(0)

    @pl.when(step == 0)
    def _():
        for z in range(this.shape[0]):
            for k, source in enumerate((this, other)):
                at = pl.multiple_of((2 * z + ((where[0] & 1) ^ k)) * part, part)
                weights[pl.ds(at, part), :] = source[z]

    pick_tile(buffer, grads, tiles, step)
    extra = buffer[:, width:].astype(FULL)
    lane = lax.broadcasted_iota(jnp.int32, extra.shape, 1)
    gate = pltpu.roll(extra, LANES - TOP, 1) + pltpu.roll(extra, LANES - 2 * TOP, 1)
    first = where[0] // replicas * own
    back = mul(buffer[:, :width], weights[...])
    table = jnp.zeros(extra.shape, FULL)
    for j in range(own):
        hit = (lane < TOP) & (extra == (first + j).astype(FULL))
        column = jnp.sum(jnp.where(hit, gate, 0.0), axis=1, keepdims=True)
        table = jnp.where(lane == j, column, table)
        back_out[:, j * hid : (j + 1) * hid] = back[:, j * hid : (j + 1) * hid] * column
    gate_out[...] = table


def expert_body(n_piece, tiles, own, hid, where, *refs):
    rows = refs[:n_piece]
    weights, gate, back, grad_hidden, active_out, grad_both, buffer = refs[n_piece:]
    pick_tile(buffer, rows, tiles, pl.program_id(0))
    wide = own * hid
    both = mul(buffer[...], weights[...])
    for j in range(own):
        at = slice(j * hid, (j + 1) * hid)
        up_at = slice(wide + j * hid, wide + (j + 1) * hid)
        pre, up = both[:, at], both[:, up_at]
        squash = 1.0 / (1.0 + jnp.exp(-pre))
        silu = pre * squash
        active = (silu * up).astype(LOW).astype(FULL)
        active_out[:, at] = (active * gate[:, j : j + 1]).astype(LOW)
        d = back[:, at]
        grad_both[:, at] = (d * up * squash * (1.0 + pre * (1.0 - squash))).astype(LOW)
        grad_both[:, up_at] = (d * silu).astype(LOW)
    product = mul(grad_both[...], weights[...], COLS_ON_COLS)
    grad_hidden[...] = product.astype(grad_hidden.dtype)


def out_body(where, active, weights, out):
    out[...] = mul(active[...], weights[...], COLS_ON_COLS).astype(out.dtype)


def weight_grad_body(n_source, part, where, *refs):
    sources = refs[:n_source]
    kept, sent, *outs, column, total = refs[n_source:]
    half, size = kept.shape[0], sources[0].shape[0]
    for k, source in enumerate(sources):
        column[k * size : (k + 1) * size, :] = source[...]
    product = mul(column[:half], kept[...], ROWS_ON_ROWS)
    total[...] = (product + mul(column[half:], sent[...], ROWS_ON_ROWS)).astype(LOW)
    for z in range(total.shape[0] // (2 * part)):
        for k in range(2):
            if len(outs) == 2:
                at = pl.multiple_of((2 * z + ((where[0] & 1) ^ k)) * part, part)
                outs[k][z] = total[pl.ds(at, part), :]
            else:
                at = (2 * z + k) * part
                outs[0][z, k] = total[at : at + part, :]


def middle_back_body(where, *refs):
    kept, got, middle, grad, gain, grad_middle, low, gain_part = refs
    total = kept[...] + got[...].astype(FULL)
    m = middle[...]
    scale = lax.rsqrt(jnp.mean(m * m, axis=1, keepdims=True) + EPS)
    gain_part[...] = jnp.broadcast_to(
        jnp.sum(total * m * scale, axis=0, keepdims=True), gain_part.shape
    )
    weighted = total * gain[1:2, :]
    inner = jnp.mean(weighted * m, axis=1, keepdims=True)
    back = grad[...].astype(FULL) + (scale * weighted - m * (scale * scale * scale) * inner)
    grad_middle[...] = back
    low[...] = back.astype(LOW)


def attend_back_body(n_piece, q_cols, k_cols, rows, part, order, orders, where, *refs):
    pieces = refs[:n_piece]
    mixed, qkv_in, doc_row, doc_col, cosine, sine, hidden, weights = refs[n_piece : n_piece + 8]
    kept, sent, first_kept, first_sent, branch, natural, grad_qkv, grads = refs[n_piece + 8 :]
    for k in range(n_piece):
        branch[k * rows : (k + 1) * rows, :] = pieces[k][...]
    grad_mixed = mul(branch[...], weights[:, q_cols + 2 * k_cols :]).astype(LOW)
    for k, m in enumerate(order):
        at = pl.multiple_of((where[1] ^ m) * rows, rows)
        natural[pl.ds(at, rows), :q_cols] = grad_mixed[k * rows : (k + 1) * rows]
    qk = q_cols + k_cols
    total = qk + k_cols
    grads[:, total:] = mul(branch[...], mixed[...], ROWS_ON_ROWS)
    allowed = admitted(doc_row[...], doc_col[...])
    per_group = q_cols // k_cols
    query_grads, key_grads, value_grads = [], [], []
    for g in range(k_cols // HEAD_SIZE):
        key = qkv_in[:, q_cols + g * HEAD_SIZE : q_cols + (g + 1) * HEAD_SIZE]
        value = qkv_in[:, qk + g * HEAD_SIZE : qk + (g + 1) * HEAD_SIZE]
        key_grad = value_grad = None
        for h in range(g * per_group, (g + 1) * per_group):
            at = slice(h * HEAD_SIZE, (h + 1) * HEAD_SIZE)
            query = qkv_in[:, at]
            shares = softmax_of(query, key, allowed)
            grad = natural[:, at]
            grad_shares = mul(grad, value, COLS_ON_COLS)
            inner = jnp.sum(shares * grad_shares, axis=1, keepdims=True)
            grad_scores = (shares * (grad_shares - inner)).astype(LOW)
            query_grads.append(mul(grad_scores, key))
            dk = mul(grad_scores, query, ROWS_ON_ROWS)
            dv = mul(shares.astype(LOW), grad, ROWS_ON_ROWS)
            key_grad = dk if key_grad is None else key_grad + dk
            value_grad = dv if value_grad is None else value_grad + dv
        key_grads.append(key_grad)
        value_grads.append(value_grad)
    turned = jnp.concatenate(query_grads + key_grads, axis=1) * HEAD_SIZE**-0.5
    grad_qkv[:, :qk] = rotate(turned, cosine[...], -sine[...]).astype(LOW)
    grad_qkv[:, qk:] = jnp.concatenate(value_grads, axis=1).astype(LOW)
    grads[:, :total] = mul(hidden[...], grad_qkv[...], ROWS_ON_ROWS)
    for p, (even, odd) in enumerate(zip(*orders)):
        at = pl.multiple_of((where[0] ^ jnp.where(where[1] & 1 == 0, even, odd)) * part, part)
        target = kept if p < len(orders[0]) // 2 else sent
        k = p % (len(orders[0]) // 2)
        target[k * part : (k + 1) * part, :] = grads[pl.ds(at, part), :].astype(target.dtype)
    for k, m in enumerate(order):
        at = pl.multiple_of((where[1] ^ m) * rows, rows)
        natural[k * rows : (k + 1) * rows, :total] = grad_qkv[pl.ds(at, rows), :]
    product = mul(natural[:, :total], weights[:, :total], COLS_ON_COLS)
    half = first_kept.shape[0]
    first_kept[...] = product[:half]
    first_sent[...] = product[half:].astype(LOW)


def tokens_back_body(rows, where, tokens, kept, got, gain, grad_middle, moe_part, out):
    at = pl.multiple_of(where[1] * rows, rows)
    x = tokens[pl.ds(at, rows), :].astype(FULL)
    scale = lax.rsqrt(jnp.mean(x * x, axis=1, keepdims=True) + EPS)
    first = kept[...] + got[...].astype(FULL)
    attn_part = jnp.sum(first * x * scale, axis=0, keepdims=True)
    weighted = first * gain[0:1, :]
    inner = jnp.mean(weighted * x, axis=1, keepdims=True)
    out[:rows] = grad_middle[...] + (scale * weighted - x * (scale * scale * scale) * inner)
    line = lax.broadcasted_iota(jnp.int32, moe_part.shape, 0)
    out[rows:] = jnp.where(line == 0, attn_part, jnp.where(line == 1, moe_part[...], 0.0))


def unpack_body(own, hid, replicas, turn, where, source, *outs):
    part = source.shape[0] // 2
    for k in range(own * len(outs)):
        out, j = outs[k // own], k % own
        cols = slice(k * hid, (k + 1) * hid)
        pieces = [source[i * part : (i + 1) * part, cols].astype(FULL) for i in range(2)]
        pieces = [piece.T for piece in pieces] if turn else pieces
        if replicas == 1:
            out[j] = pieces[0]
            out[own + j] = pieces[1]
        else:
            first = 2 * pl.program_id(0) % replicas == 0
            out[j] = pieces[0] + pieces[1] + jnp.where(first, 0.0, out[j])


def local(
    tokens,
    cotangent,
    segments,
    routes,
    gates,
    w_query,
    key_projection,
    value_projection,
    w_out,
    gain_attn,
    gain_moe,
    w_gate,
    w_up,
    w_down,
):
    n_e, n_t = lax.axis_size("expert"), lax.axis_size("tensor")
    e, t = lax.axis_index("expert"), lax.axis_index("tensor")
    where = jnp.stack([e, t]).astype(jnp.int32)
    replicas = max(1, n_e // EXPERTS)
    own_experts = EXPERTS * replicas // n_e
    first_bit = replicas.bit_length() - 1
    length, width = tokens.shape
    part = width // n_e
    rows = length // n_t
    q_cols, k_cols = w_query.shape[1], key_projection.shape[1]
    qkv_cols = q_cols + 2 * k_cols
    hidden = w_gate.shape[2]
    wide = own_experts * hidden

    pad = 16
    all_cols = qkv_cols + q_cols
    gain_rows = jnp.pad(jnp.stack([gain_attn, gain_moe]), ((0, pad - 2), (0, all_cols - part)))
    shard = jnp.concatenate([w_query, key_projection, value_projection, w_out.T], axis=1)
    shard = jnp.concatenate([shard, gain_rows]).astype(LOW)

    e_bits, t_bits = bits_of(n_e), bits_of(n_t)
    even_bits, odd_bits = e_bits, e_bits[-1:] + e_bits[:-1]
    orders = order_of(even_bits), order_of(odd_bits)
    by_parity = [(("expert", a), ("expert", b)) for a, b in zip(even_bits, odd_bits)]

    def every(shard, ready, later):
        came, sends = [], []
        for k, (even, odd) in enumerate(by_parity):
            if k == 1:
                shard, *ready = lax.optimization_barrier((shard, *ready))
            if k == 2:
                shard = after(shard, later)
            sends.append(shard)
            came.append(swap_by_parity(shard, even, odd))
            shard = jnp.concatenate([shard, came[-1]])
        return [sends[-1], came[-1]], came, sends, ready

    pairs = n_e // 2
    turn = part % LANES == 0
    pair_experts = 2 * own_experts // replicas or 1
    at_pair = lambda dims: pl.BlockSpec(
        (pair_experts,) + dims, lambda z: (2 * z // max(2, replicas), 0, 0)
    )
    sources = [w_gate, w_up, w_down if turn else w_down.transpose(0, 2, 1)]
    sided = pl.BlockSpec((1, part, 2 * wide), lambda z: (z, 0, 0))
    packed = call(
        functools.partial(pack_body, own_experts, hidden, replicas, turn),
        [shape((pairs, 2, part, wide), LOW)] + [shape((pairs, part, 2 * wide), LOW)] * 2,
        where, *sources,
        grid=(pairs,),
        in_specs=[at_pair(w.shape[1:]) for w in sources],
        out_specs=[pl.BlockSpec((1, 2, part, wide), lambda z: (z, 0, 0, 0))] + [sided] * 2,
    )
    side = e & 1
    lines = [[z * 2 + k for z in range(n_e // 2)] for k in range(2)]

    def along(blocks):
        return lax.all_to_all(
            blocks, "expert", 0, 0, tiled=True, axis_index_groups=lines
        )

    def split_sides(blocks):
        blocks = blocks.reshape(pairs, 2, part, blocks.shape[-1])
        this = lax.dynamic_index_in_dim(blocks, side, 1, keepdims=False)
        return this, lax.dynamic_index_in_dim(blocks, 1 - side, 1, keepdims=False)

    def from_neighbour(blocks, *earlier):
        cols = blocks.shape[-1]
        blocks = along(after(blocks.reshape(pairs, 2 * part, cols), *earlier))
        this, other = split_sides(blocks)
        return this, swap(other, "expert", 1)

    def interleave(this, other):
        cols = this.shape[-1]
        block = pl.BlockSpec((1, part, cols), lambda z: (z, 0, 0))
        return call(
            functools.partial(interleave_body, part),
            [shape((pairs, 2 * part, cols), LOW)],
            where, this, other,
            grid=(pairs,),
            in_specs=[block, block],
            out_specs=[pl.BlockSpec((1, 2 * part, cols), lambda z: (z, 0, 0))],
        )[0]

    def to_neighbour(this, other, *earlier):
        return interleave(this, swap(after(other, *earlier), "expert", 1))

    e_path = [("expert", b) for b in bits_of(n_e, first_bit)]
    t_path = [("tensor", b) for b in t_bits]
    even_path, odd_path = e_path + t_path[:-1], e_path[:-1] + t_path[:-1] + e_path[-1:]
    path = list(zip(even_path, odd_path))
    last = t_path[-1]

    own = t * rows
    grad_rows = lax.dynamic_slice_in_dim(cotangent, own, rows, 0)
    gate_rows = lax.dynamic_slice_in_dim(gates, own, rows, 0)
    route_rows = lax.dynamic_slice_in_dim(routes, own, rows, 0)
    gate_high = gate_rows.astype(LOW)
    gate_rest = (gate_rows - gate_high.astype(FULL)).astype(LOW)
    extra = jnp.concatenate([route_rows.astype(LOW), gate_high, gate_rest], axis=1)
    extra = jnp.pad(extra, ((0, 0), (0, LANES - 3 * TOP)))
    grad_steps = [jnp.concatenate([grad_rows, extra], axis=1)]
    grad_first = swap_by_parity(grad_steps[0], *path[0])
    attn_arrays, attn_came, attn_sends, packed = every(shard, packed, grad_first)
    grad_steps.append(jnp.concatenate([grad_steps[0], grad_first]))
    grad_second = swap_by_parity(after(grad_steps[1], attn_sends[-1]), *path[1])
    grad_steps.append(jnp.concatenate([grad_steps[1], grad_second]))
    down_this, down_other = from_neighbour(packed[0], attn_came[-1])
    near = to_neighbour(*packed[1:], attn_came[-1])
    pitch = part + pad
    gains = jnp.zeros((pad, LANES), FULL)
    if part % LANES:
        held = jnp.concatenate(
            [a.reshape(-1, pitch, all_cols)[:, part:, :part] for a in attn_arrays]
        ).astype(FULL)
        on_even = [position_in(e ^ k, even_bits) for k in range(n_e)]
        on_odd = [position_in(e ^ k, odd_bits) for k in range(n_e)]
        gains = jnp.concatenate(
            [
                lax.dynamic_index_in_dim(held, jnp.where(t & 1 == 0, a, b), 0, keepdims=False)
                for a, b in zip(on_even, on_odd)
            ],
            axis=1,
        )

    def add_halves(kept, got):
        half = got.shape[0] // 2
        return kept[:half] + got[:half].astype(FULL), (
            kept[half:] + got[half:].astype(FULL)
        ).astype(LOW)

    def scatter_stage(kept, sent, k):
        got = swap_by_parity(sent, *path[-1 - k])
        return (kept, got) if k == len(path) - 1 else add_halves(kept, got)

    documents = segments[0]
    doc_row, doc_col = documents[None, :], documents[:, None]
    index = jnp.arange(length)
    same = (index[None, :] < index[:, None]) & (doc_row == doc_col)
    position = jnp.sum(same.astype(FULL), axis=1, keepdims=True)
    lane = jnp.arange(LANES)
    freqs = THETA ** (-2.0 * (lane % (HEAD_SIZE // 2)).astype(FULL) / HEAD_SIZE)
    angle = position * freqs[None, :]
    cosine = jnp.cos(angle)
    sine = jnp.sin(angle) * jnp.where(lane % HEAD_SIZE < HEAD_SIZE // 2, -1.0, 1.0)[None, :]
    t_masks = t_bits[::-1]
    order = order_of(t_bits)
    weights, first_hidden, qkv, mixed, gains, kept, sent = call(
        functools.partial(attend_body, orders, 2, part, pitch, q_cols, k_cols, rows, order),
        [
            shape((width, all_cols), LOW),
            shape((length, width), LOW),
            shape((length, qkv_cols), LOW),
            shape((length, q_cols), LOW),
            shape((pad, width), FULL),
            shape((length // 2, width), FULL),
            shape((length // 2, width), LOW),
        ],
        where, *attn_arrays[:-1], after(attn_arrays[-1], grad_second), tokens, gains, doc_row, doc_col, cosine, sine,
        scratch=[pltpu.VMEM((length, q_cols), LOW)],
        flops=2 * length * (width * qkv_cols + 2 * length * q_cols),
    )
    def all_rows(field):
        size = field.shape[0]
        for b in t_bits:
            field = jnp.concatenate([field, swap(field, "tensor", b)])
        at = [position_in(t ^ k, t_bits) * size for k in range(n_t)]
        return jnp.concatenate([lax.dynamic_slice_in_dim(field, a, size, 0) for a in at])

    def scatter_rows(kept, sent):
        for b in t_masks[:-1]:
            total = kept + swap(sent, "tensor", b).astype(FULL)
            half = total.shape[0] // 2
            kept, sent = total[:half], total[half:].astype(LOW)
        return kept, swap(sent, "tensor", t_masks[-1])

    grad_third = swap_by_parity(grad_steps[-1], *path[2])
    kept, got = scatter_rows(kept, sent)
    middle, second_hidden = call(
        functools.partial(middle_body, rows),
        [shape((rows, width), FULL), shape((rows, width), LOW)],
        where, tokens, kept, after(got, grad_third, down_this), gains,
    )

    hidden_field = second_hidden
    for k, (even, odd) in enumerate(path):
        if k == 1:
            hidden_field = after(hidden_field, near)
        if k == 2:
            hidden_field = after(hidden_field, down_other, grad_got)
        hidden_got = swap_by_parity(hidden_field, even, odd)
        if k == 1:
            gate_up_rows = along(after(near, hidden_got)).reshape(width, 2 * wide)
        hidden_pieces = [hidden_field, hidden_got]
        hidden_field = jnp.concatenate(hidden_pieces)
        if k == 0:
            grad_field, grad_got = grad_steps[-1], grad_third
            for k in range(3, len(path)):
                grad_field = jnp.concatenate([grad_field, grad_got])
                grad_got = swap_by_parity(grad_field, *path[k])
            grad_pieces = [grad_field, grad_got]
    hidden_pieces = hidden_pieces + [swap(p, *last) for p in hidden_pieces]
    grad_pieces = grad_pieces + [swap(p, *last) for p in grad_pieces]
    size = 512
    total_rows = sum(p.shape[0] for p in grad_pieces)
    steps = total_rows // size
    whole = lambda a: pl.BlockSpec(a.shape, lambda i: (0,) * a.ndim)
    tile = lambda cols: pl.BlockSpec((size, cols), lambda i: (i, 0))

    def tiles_of(pieces):
        count = pieces[0].shape[0] // size
        return count, [
            pl.BlockSpec((size, p.shape[1]), lambda i, k=k: (jnp.clip(i - k * count, 0, count - 1), 0))
            for k, p in enumerate(pieces)
        ]

    tiles, specs = tiles_of(grad_pieces)
    gate_table, back, down_rows = call(
        functools.partial(owner_body, len(grad_pieces), tiles, part, own_experts, hidden, replicas),
        [
            shape((total_rows, LANES), FULL),
            shape((total_rows, wide), FULL),
            shape((width, wide), LOW),
        ],
        where, *grad_pieces, down_this, down_other,
        grid=(steps,),
        in_specs=specs + [whole(down_this), whole(down_other)],
        out_specs=[tile(LANES), tile(wide), pl.BlockSpec((width, wide), lambda i: (0, 0))],
        scratch=[pltpu.VMEM((size, width + LANES), LOW)],
        flops=2 * total_rows * width * wide,
        limit=LARGE,
    )
    half = steps // 2

    def experts(chosen, first, out_type):
        later = lambda cols: pl.BlockSpec((size, cols), lambda i: (i + first, 0))
        tiles, specs = tiles_of(chosen)
        return call(
            functools.partial(expert_body, len(chosen), tiles, own_experts, hidden),
            [
                shape((half * size, width), out_type),
                shape((half * size, wide), LOW),
                shape((half * size, 2 * wide), LOW),
            ],
            where, *chosen, gate_up_rows, gate_table, back,
            grid=(half,),
            in_specs=specs
            + [whole(gate_up_rows), later(LANES), later(wide)],
            out_specs=[tile(width), tile(wide), tile(2 * wide)],
            scratch=[pltpu.VMEM((size, width), LOW)],
            flops=2 * half * size * width * 4 * wide,
            limit=LARGE,
        )

    sent_hidden, sent_active, sent_both = experts(hidden_pieces[2:], half, LOW)
    kept_hidden, kept_active, kept_both = experts(hidden_pieces[:2], 0, FULL)

    block = 256
    column = lambda a: pl.BlockSpec((a.shape[0], block), lambda i: (0, i))

    def weight_grad(sources, kept, sent, sided):
        cols = kept.shape[1]
        dims = [(part, cols)] * 2 if sided else [(2, part, cols)]
        count = block // (2 * part)
        return call(
            functools.partial(weight_grad_body, len(sources), part),
            [shape((pairs,) + d, LOW) for d in dims],
            where, *sources, kept, sent,
            grid=(width // block,),
            in_specs=[column(a) for a in sources] + [whole(kept), whole(sent)],
            out_specs=[pl.BlockSpec((count,) + d, lambda i, n=len(d): (i,) + (0,) * n) for d in dims],
            scratch=[pltpu.VMEM((total_rows, block), LOW), pltpu.VMEM((block, cols), LOW)],
            flops=2 * total_rows * width * cols,
        )

    hidden_kept, hidden_sent = add_halves(kept_hidden, swap(sent_hidden, *last))
    def down(active, out_type):
        return call(
            out_body,
            [shape((half * size, width), out_type)],
            where, active, down_rows,
            grid=(half,),
            in_specs=[tile(wide), whole(down_rows)],
            out_specs=[tile(width)],
            flops=2 * half * size * width * wide,
        )[0]

    steps_back = len(path)
    kept, sent = scatter_stage(hidden_kept, hidden_sent, 0)
    (down_grad,) = weight_grad(grad_pieces, kept_active, after(sent_active, hidden_sent), False)
    sent_out = down(after(sent_active, down_grad), LOW)
    kept_out = down(after(kept_active, down_grad), FULL)
    kept, sent = scatter_stage(kept, after(sent, down_grad), 1)
    out_kept, out_sent = add_halves(kept_out, swap(sent_out, *last))
    both_this, both_other = weight_grad(hidden_pieces, kept_both, after(sent_both, sent_out), True)
    grad_near = to_neighbour(both_this, both_other)
    down_line = along(down_grad.reshape(pairs, 2 * part, wide))
    sent = after(sent, down_line, both_other)
    for k in range(2, steps_back - 1):
        kept, sent = scatter_stage(kept, sent, k)
    grad_kept, grad_got = scatter_stage(kept, after(sent, out_sent), steps_back - 1)
    out_kept, out_sent = scatter_stage(out_kept, out_sent, 0)
    out_first = out_sent
    out_kept, out_sent = scatter_stage(out_kept, out_sent, 1)
    out_second = out_sent
    both_back = along(after(grad_near, grad_got)).reshape(width, 2 * wide)

    grad_middle, branch_grad, moe_part = call(
        middle_back_body,
        [shape((rows, width), FULL), shape((rows, width), LOW), shape((16, width), FULL)],
        where, grad_kept, grad_got, middle, grad_rows, gains,
    )
    branch_pieces = [branch_grad]
    for b in reversed(t_masks):
        branch_pieces = branch_pieces + [swap(p, "tensor", b) for p in branch_pieces]
    sum_orders = orders[0], orders[0]
    kept_w, sent_w, first_kept, first_sent = call(
        functools.partial(
            attend_back_body, len(branch_pieces), q_cols, k_cols, rows, part, order, sum_orders
        ),
        [
            shape((width // 2, all_cols), FULL),
            shape((width // 2, all_cols), LOW),
            shape((length // 2, width), FULL),
            shape((length // 2, width), LOW),
        ],
        where, *branch_pieces[:-1], after(branch_pieces[-1], out_first), mixed, qkv, doc_row, doc_col, cosine, sine,
        first_hidden, weights,
        scratch=[
            pltpu.VMEM((length, width), LOW),
            pltpu.VMEM((length, max(q_cols, qkv_cols)), LOW),
            pltpu.VMEM((length, qkv_cols), LOW),
            pltpu.VMEM((width, all_cols), FULL),
        ],
        flops=2 * length * width * (2 * q_cols + 2 * qkv_cols),
    )
    got_w = swap(sent_w, "expert", e_bits[-1])
    attn_grad = kept_w + got_w.astype(FULL)
    kept, got = scatter_rows(first_kept, first_sent)
    (token_rows,) = call(
        functools.partial(tokens_back_body, rows),
        [shape((rows + 16, width), FULL)],
        where, tokens, kept, after(got, got_w, out_second), gains, grad_middle, moe_part,
    )
    gathered = all_rows(token_rows.astype(LOW))
    gathered = gathered.reshape(n_t, rows + 16, width).astype(FULL)
    grad_input = gathered[:, :rows].reshape(length, width)
    gain_sum = jnp.sum(gathered[:, rows : rows + 2], axis=0)

    blocks = gain_sum.reshape(2, n_e, part).transpose(1, 0, 2)

    half_rows = attn_grad.shape[0] // 2
    kept_w, sent_w = attn_grad[:half_rows], attn_grad[half_rows:].astype(LOW)
    blocks = after(blocks, sent_w)
    gain_grads = jnp.sum(lax.all_to_all(blocks, "expert", 0, 0, tiled=True), axis=0)
    out_sent = after(out_sent, both_back)
    for k, b in enumerate(reversed(e_bits[:-1])):
        attn_grad = kept_w + swap(sent_w, "expert", b).astype(FULL)
        half_rows = attn_grad.shape[0] // 2
        kept_w, sent_w = attn_grad[:half_rows], attn_grad[half_rows:].astype(LOW)
        if k == 0:
            out_kept, out_sent = scatter_stage(out_kept, out_sent, 2)
            out_sent = after(out_sent, sent_w)
    for k in range(3, steps_back):
        out_kept, out_sent = scatter_stage(out_kept, out_sent, k)
    output_rows = (middle + (out_kept + out_sent.astype(FULL))).astype(LOW)
    output = all_rows(output_rows)

    out_dims = [(part, hidden), (part, hidden), (hidden, part) if turn else (part, hidden)]

    def unpack(source, dims, turned):
        cols = source.shape[1]
        return call(
            functools.partial(unpack_body, own_experts, hidden, replicas, turned),
            [shape((EXPERTS,) + dims, FULL)] * (cols // wide),
            where, source,
            grid=(pairs,),
            in_specs=[pl.BlockSpec((2 * part, cols), lambda z: (z, 0))],
            out_specs=[at_pair(dims)] * (cols // wide),
        )

    sides_of = lambda this, other: jnp.where(
        side == 0, jnp.stack([this, other], axis=1), jnp.stack([other, this], axis=1)
    )
    down_this, down_other = split_sides(after(down_line, got_w))
    down_back = sides_of(down_this, swap(down_other, "expert", 1)).reshape(width, wide)
    shards = unpack(both_back, out_dims[0], False) + unpack(down_back, out_dims[2], turn)
    gate_shard, up_shard, down_shard = shards
    if not turn:
        down_shard = down_shard.transpose(0, 2, 1)

    return (
        output,
        grad_input,
        attn_grad[:, :q_cols],
        attn_grad[:, q_cols : q_cols + k_cols],
        attn_grad[:, q_cols + k_cols : qkv_cols],
        attn_grad[:, qkv_cols:].T,
        gain_grads[0],
        gain_grads[1],
        gate_shard,
        up_shard,
        down_shard,
    )


def solution(mesh):
    by_rows = P("expert", None)
    by_both = P("expert", "tensor")
    in_experts = P(None, "expert", "tensor")
    down_specs = P(None, "tensor", "expert")
    return jax.shard_map(
        local,
        mesh=mesh,
        in_specs=(by_rows,) * 5
        + (by_both,) * 3
        + (P("tensor", "expert"), P("expert"), P("expert"), in_experts, in_experts, down_specs),
        out_specs=(by_rows, by_rows)
        + (by_both,) * 3
        + (P("tensor", "expert"), P("expert"), P("expert"), in_experts, in_experts, down_specs),
        check_vma=False,
    )
```

```python
import functools

import jax
import jax.numpy as jnp
from jax import lax
from jax.experimental import pallas as pl
from jax.experimental.pallas import tpu as pltpu
from jax.sharding import PartitionSpec as P

HEAD_SIZE = 64
EXPERTS = 32
TOP = 8
EPS = 1e-06
THETA = 10000.0
MASKED = -1e30
LANES = 128
LIMIT = 24 * 1024 * 1024
LARGE = 56 * 1024 * 1024

LOW = jnp.bfloat16
FULL = jnp.float32
ROWS_ON_ROWS = (((0,), (0,)), ((), ()))
COLS_ON_ROWS = (((1,), (0,)), ((), ()))
COLS_ON_COLS = (((1,), (1,)), ((), ()))


def mul(left, right, dims=COLS_ON_ROWS):
    return lax.dot_general(left, right, dims, preferred_element_type=FULL)


def shape(dims, dtype):
    return jax.ShapeDtypeStruct(dims, dtype)


def call(body, outs, *args, grid=None, in_specs=None, out_specs=None, scratch=(), flops=0, limit=LIMIT):
    size = sum(a.size * a.dtype.itemsize for a in args)
    size += sum(o.size * jnp.dtype(o.dtype).itemsize for o in outs)
    whole = pl.BlockSpec(memory_space=pltpu.VMEM)
    if in_specs is None:
        in_specs = [whole] * (len(args) - 1)
    if out_specs is None:
        out_specs = [whole] * len(outs)
    extra = {} if grid is None else {"grid": grid}
    return pl.pallas_call(
        body,
        out_shape=list(outs),
        in_specs=[pl.BlockSpec(memory_space=pltpu.SMEM)] + list(in_specs),
        out_specs=list(out_specs),
        scratch_shapes=list(scratch),
        compiler_params=pltpu.CompilerParams(vmem_limit_bytes=limit),
        cost_estimate=pl.CostEstimate(flops=flops, bytes_accessed=size, transcendentals=0),
        **extra,
    )(*args)


def swap(field, axis, mask):
    count = lax.axis_size(axis)
    return lax.ppermute(field, axis, [(i, i ^ mask) for i in range(count)])


def after(field, *earlier):
    return lax.optimization_barrier((field, *earlier))[0]


def swap_by_parity(field, even, odd):
    n_e, n_t = lax.axis_size("expert"), lax.axis_size("tensor")
    pairs = []
    for e in range(n_e):
        for t in range(n_t):
            axis, mask = odd if t & 1 else even
            to = ((e ^ mask) * n_t + t) if axis == "expert" else (e * n_t + (t ^ mask))
            pairs.append((e * n_t + t, to))
    return lax.ppermute(field, ("expert", "tensor"), pairs)


def bits_of(count, first_bit=0):
    return [1 << b for b in reversed(range(first_bit, count.bit_length() - 1))]


def position_in(mask, bits):
    return sum(jnp.where(mask & b != 0, 1 << i, 0) for i, b in enumerate(bits))


def order_of(bits):
    order = [0]
    for b in bits:
        order = order + [k ^ b for k in order]
    return order


def rotate(field, cosine, sine):
    lane = lax.broadcasted_iota(jnp.int32, (field.shape[0], LANES), 1)
    low_half = lane % HEAD_SIZE < HEAD_SIZE // 2
    turned = []
    for at in range(0, field.shape[1], LANES):
        block = field[:, at : at + LANES]
        ahead = pltpu.roll(block, LANES - HEAD_SIZE // 2, 1)
        behind = pltpu.roll(block, HEAD_SIZE // 2, 1)
        turned.append(block * cosine + jnp.where(low_half, ahead, behind) * sine)
    return jnp.concatenate(turned, axis=1)


def admitted(doc_row, doc_col):
    length = doc_row.shape[1]
    row = lax.broadcasted_iota(jnp.int32, (length, length), 0)
    col = lax.broadcasted_iota(jnp.int32, (length, length), 1)
    return (col <= row) & (doc_row == doc_col)


def softmax_of(query, key, allowed):
    scores = mul(query, key, COLS_ON_COLS) * HEAD_SIZE**-0.5
    scores = jnp.where(allowed, scores, MASKED)
    raised = jnp.exp(scores - jnp.max(scores, axis=1, keepdims=True))
    return raised / jnp.sum(raised, axis=1, keepdims=True)


def place_rows(target, sources, orders, where, part, pitch):
    count = len(orders[0]) // len(sources)
    for p, (even, odd) in enumerate(zip(*orders)):
        at = pl.multiple_of((where[0] ^ jnp.where(where[1] & 1 == 0, even, odd)) * part, part)
        k = p % count * pitch
        target[pl.ds(at, part), :] = sources[p // count][k : k + part, :]


def pack_body(own, hid, replicas, turn, where, gate, up, down, down_out, *sided):
    side = where[0] & 1
    for j in range(own):
        at = slice(j * hid, (j + 1) * hid)
        for k in range(2):
            block = down[(k * own if replicas == 1 else 0) + j]
            down_out[0, k, :, at] = (block.T if turn else block).astype(LOW)
            place = ((side ^ k) * own if replicas == 1 else 0) + j
            sided[k][0, :, at] = gate[place].astype(LOW)
            up_at = slice((own + j) * hid, (own + j + 1) * hid)
            sided[k][0, :, up_at] = up[place].astype(LOW)


def interleave_body(part, where, this, other, out):
    for k, source in enumerate((this, other)):
        at = pl.multiple_of(((where[0] & 1) ^ k) * part, part)
        out[0, pl.ds(at, part), :] = source[0]


def attend_body(orders, n, part, pitch, q_cols, k_cols, rows, order, where, *refs):
    sources = refs[:n]
    tokens, gain_in, doc_row, doc_col, cosine, sine = refs[n : n + 6]
    weights, hidden, qkv_out, mixed_out, gain, kept, sent, mixed = refs[n + 6 :]
    place_rows(weights, sources, orders, where, part, pitch)
    if part % LANES == 0:
        count = len(orders[0]) // n
        for p, (even, odd) in enumerate(zip(*orders)):
            at = pl.multiple_of((where[0] ^ jnp.where(where[1] & 1 == 0, even, odd)) * part, part)
            k = p % count * pitch + part
            gain[:, pl.ds(at, part)] = sources[p // count][k : k + gain.shape[0], :part].astype(FULL)
    else:
        gain[...] = gain_in[...]
    x = tokens[...].astype(FULL)
    scale = lax.rsqrt(jnp.mean(x * x, axis=1, keepdims=True) + EPS)
    first = (x * scale * gain[0:1, :]).astype(LOW)
    hidden[...] = first
    qkv = mul(first, weights[:, : q_cols + 2 * k_cols])
    turned = rotate(qkv[:, : q_cols + k_cols], cosine[...], sine[...]).astype(LOW)
    values = qkv[:, q_cols + k_cols :].astype(LOW)
    qkv_out[:, : q_cols + k_cols] = turned
    qkv_out[:, q_cols + k_cols :] = values
    allowed = admitted(doc_row[...], doc_col[...])
    per_group = q_cols // k_cols
    for h in range(q_cols // HEAD_SIZE):
        at, g = h * HEAD_SIZE, h // per_group * HEAD_SIZE
        shares = softmax_of(
            turned[:, at : at + HEAD_SIZE],
            turned[:, q_cols + g : q_cols + g + HEAD_SIZE],
            allowed,
        ).astype(LOW)
        mixed[:, at : at + HEAD_SIZE] = mul(shares, values[:, g : g + HEAD_SIZE]).astype(LOW)
    for k, m in enumerate(order):
        at = pl.multiple_of((where[1] ^ m) * rows, rows)
        mixed_out[k * rows : (k + 1) * rows, :] = mixed[pl.ds(at, rows), :]
    product = mul(mixed_out[...], weights[:, q_cols + 2 * k_cols :], COLS_ON_COLS)
    half = kept.shape[0]
    kept[...] = product[:half]
    sent[...] = product[half:].astype(LOW)


def middle_body(rows, where, tokens, kept, got, gain, middle, hidden):
    at = pl.multiple_of(where[1] * rows, rows)
    m = tokens[pl.ds(at, rows), :].astype(FULL) + (kept[...] + got[...].astype(FULL))
    middle[...] = m
    scale = lax.rsqrt(jnp.mean(m * m, axis=1, keepdims=True) + EPS)
    hidden[...] = (m * scale * gain[1:2, :]).astype(LOW)


def pick_tile(buffer, sources, tiles, step):
    for k, source in enumerate(sources):

        @pl.when(step // tiles == k)
        def _():
            buffer[...] = source[...]


def owner_body(n_piece, tiles, part, own, hid, replicas, where, *refs):
    grads = refs[:n_piece]
    this, other, gate_out, back_out, weights, buffer = refs[n_piece:]
    width = weights.shape[0]
    step = pl.program_id(0)

    @pl.when(step == 0)
    def _():
        for z in range(this.shape[0]):
            for k, source in enumerate((this, other)):
                at = pl.multiple_of((2 * z + ((where[0] & 1) ^ k)) * part, part)
                weights[pl.ds(at, part), :] = source[z]

    pick_tile(buffer, grads, tiles, step)
    extra = buffer[:, width:].astype(FULL)
    lane = lax.broadcasted_iota(jnp.int32, extra.shape, 1)
    gate = pltpu.roll(extra, LANES - TOP, 1) + pltpu.roll(extra, LANES - 2 * TOP, 1)
    first = where[0] // replicas * own
    back = mul(buffer[:, :width], weights[...])
    table = jnp.zeros(extra.shape, FULL)
    for j in range(own):
        hit = (lane < TOP) & (extra == (first + j).astype(FULL))
        column = jnp.sum(jnp.where(hit, gate, 0.0), axis=1, keepdims=True)
        table = jnp.where(lane == j, column, table)
        back_out[:, j * hid : (j + 1) * hid] = back[:, j * hid : (j + 1) * hid] * column
    gate_out[...] = table


def expert_body(n_piece, tiles, own, hid, where, *refs):
    rows = refs[:n_piece]
    weights, gate, back, grad_hidden, active_out, grad_both, buffer = refs[n_piece:]
    pick_tile(buffer, rows, tiles, pl.program_id(0))
    wide = own * hid
    both = mul(buffer[...], weights[...])
    for j in range(own):
        at = slice(j * hid, (j + 1) * hid)
        up_at = slice(wide + j * hid, wide + (j + 1) * hid)
        pre, up = both[:, at], both[:, up_at]
        squash = 1.0 / (1.0 + jnp.exp(-pre))
        silu = pre * squash
        active = (silu * up).astype(LOW).astype(FULL)
        active_out[:, at] = (active * gate[:, j : j + 1]).astype(LOW)
        d = back[:, at]
        grad_both[:, at] = (d * up * squash * (1.0 + pre * (1.0 - squash))).astype(LOW)
        grad_both[:, up_at] = (d * silu).astype(LOW)
    product = mul(grad_both[...], weights[...], COLS_ON_COLS)
    grad_hidden[...] = product.astype(grad_hidden.dtype)


def out_body(where, active, weights, out):
    out[...] = mul(active[...], weights[...], COLS_ON_COLS).astype(out.dtype)


def weight_grad_body(n_source, part, where, *refs):
    sources = refs[:n_source]
    kept, sent, *outs, column, total = refs[n_source:]
    half, size = kept.shape[0], sources[0].shape[0]
    for k, source in enumerate(sources):
        column[k * size : (k + 1) * size, :] = source[...]
    product = mul(column[:half], kept[...], ROWS_ON_ROWS)
    total[...] = (product + mul(column[half:], sent[...], ROWS_ON_ROWS)).astype(LOW)
    for z in range(total.shape[0] // (2 * part)):
        for k in range(2):
            if len(outs) == 2:
                at = pl.multiple_of((2 * z + ((where[0] & 1) ^ k)) * part, part)
                outs[k][z] = total[pl.ds(at, part), :]
            else:
                at = (2 * z + k) * part
                outs[0][z, k] = total[at : at + part, :]


def middle_back_body(where, *refs):
    kept, got, middle, grad, gain, grad_middle, low, gain_part = refs
    total = kept[...] + got[...].astype(FULL)
    m = middle[...]
    scale = lax.rsqrt(jnp.mean(m * m, axis=1, keepdims=True) + EPS)
    gain_part[...] = jnp.broadcast_to(
        jnp.sum(total * m * scale, axis=0, keepdims=True), gain_part.shape
    )
    weighted = total * gain[1:2, :]
    inner = jnp.mean(weighted * m, axis=1, keepdims=True)
    back = grad[...].astype(FULL) + (scale * weighted - m * (scale * scale * scale) * inner)
    grad_middle[...] = back
    low[...] = back.astype(LOW)


def attend_back_body(n_piece, q_cols, k_cols, rows, part, order, orders, where, *refs):
    pieces = refs[:n_piece]
    mixed, qkv_in, doc_row, doc_col, cosine, sine, hidden, weights = refs[n_piece : n_piece + 8]
    kept, sent, first_kept, first_sent, branch, natural, grad_qkv, grads = refs[n_piece + 8 :]
    for k in range(n_piece):
        branch[k * rows : (k + 1) * rows, :] = pieces[k][...]
    grad_mixed = mul(branch[...], weights[:, q_cols + 2 * k_cols :]).astype(LOW)
    for k, m in enumerate(order):
        at = pl.multiple_of((where[1] ^ m) * rows, rows)
        natural[pl.ds(at, rows), :q_cols] = grad_mixed[k * rows : (k + 1) * rows]
    qk = q_cols + k_cols
    total = qk + k_cols
    grads[:, total:] = mul(branch[...], mixed[...], ROWS_ON_ROWS)
    allowed = admitted(doc_row[...], doc_col[...])
    per_group = q_cols // k_cols
    query_grads, key_grads, value_grads = [], [], []
    for g in range(k_cols // HEAD_SIZE):
        key = qkv_in[:, q_cols + g * HEAD_SIZE : q_cols + (g + 1) * HEAD_SIZE]
        value = qkv_in[:, qk + g * HEAD_SIZE : qk + (g + 1) * HEAD_SIZE]
        key_grad = value_grad = None
        for h in range(g * per_group, (g + 1) * per_group):
            at = slice(h * HEAD_SIZE, (h + 1) * HEAD_SIZE)
            query = qkv_in[:, at]
            shares = softmax_of(query, key, allowed)
            grad = natural[:, at]
            grad_shares = mul(grad, value, COLS_ON_COLS)
            inner = jnp.sum(shares * grad_shares, axis=1, keepdims=True)
            grad_scores = (shares * (grad_shares - inner)).astype(LOW)
            query_grads.append(mul(grad_scores, key))
            dk = mul(grad_scores, query, ROWS_ON_ROWS)
            dv = mul(shares.astype(LOW), grad, ROWS_ON_ROWS)
            key_grad = dk if key_grad is None else key_grad + dk
            value_grad = dv if value_grad is None else value_grad + dv
        key_grads.append(key_grad)
        value_grads.append(value_grad)
    turned = jnp.concatenate(query_grads + key_grads, axis=1) * HEAD_SIZE**-0.5
    grad_qkv[:, :qk] = rotate(turned, cosine[...], -sine[...]).astype(LOW)
    grad_qkv[:, qk:] = jnp.concatenate(value_grads, axis=1).astype(LOW)
    grads[:, :total] = mul(hidden[...], grad_qkv[...], ROWS_ON_ROWS)
    for p, (even, odd) in enumerate(zip(*orders)):
        at = pl.multiple_of((where[0] ^ jnp.where(where[1] & 1 == 0, even, odd)) * part, part)
        target = kept if p < len(orders[0]) // 2 else sent
        k = p % (len(orders[0]) // 2)
        target[k * part : (k + 1) * part, :] = grads[pl.ds(at, part), :].astype(target.dtype)
    for k, m in enumerate(order):
        at = pl.multiple_of((where[1] ^ m) * rows, rows)
        natural[k * rows : (k + 1) * rows, :total] = grad_qkv[pl.ds(at, rows), :]
    product = mul(natural[:, :total], weights[:, :total], COLS_ON_COLS)
    half = first_kept.shape[0]
    first_kept[...] = product[:half]
    first_sent[...] = product[half:].astype(LOW)


def tokens_back_body(rows, where, tokens, kept, got, gain, grad_middle, moe_part, out):
    at = pl.multiple_of(where[1] * rows, rows)
    x = tokens[pl.ds(at, rows), :].astype(FULL)
    scale = lax.rsqrt(jnp.mean(x * x, axis=1, keepdims=True) + EPS)
    first = kept[...] + got[...].astype(FULL)
    attn_part = jnp.sum(first * x * scale, axis=0, keepdims=True)
    weighted = first * gain[0:1, :]
    inner = jnp.mean(weighted * x, axis=1, keepdims=True)
    out[:rows] = grad_middle[...] + (scale * weighted - x * (scale * scale * scale) * inner)
    line = lax.broadcasted_iota(jnp.int32, moe_part.shape, 0)
    out[rows:] = jnp.where(line == 0, attn_part, jnp.where(line == 1, moe_part[...], 0.0))


def unpack_body(own, hid, replicas, turn, where, source, *outs):
    part = source.shape[0] // 2
    for k in range(own * len(outs)):
        out, j = outs[k // own], k % own
        cols = slice(k * hid, (k + 1) * hid)
        pieces = [source[i * part : (i + 1) * part, cols].astype(FULL) for i in range(2)]
        pieces = [piece.T for piece in pieces] if turn else pieces
        if replicas == 1:
            out[j] = pieces[0]
            out[own + j] = pieces[1]
        else:
            first = 2 * pl.program_id(0) % replicas == 0
            out[j] = pieces[0] + pieces[1] + jnp.where(first, 0.0, out[j])


def local(
    tokens,
    cotangent,
    segments,
    routes,
    gates,
    w_query,
    key_projection,
    value_projection,
    w_out,
    gain_attn,
    gain_moe,
    w_gate,
    w_up,
    w_down,
):
    n_e, n_t = lax.axis_size("expert"), lax.axis_size("tensor")
    e, t = lax.axis_index("expert"), lax.axis_index("tensor")
    where = jnp.stack([e, t]).astype(jnp.int32)
    replicas = max(1, n_e // EXPERTS)
    own_experts = EXPERTS * replicas // n_e
    first_bit = replicas.bit_length() - 1
    length, width = tokens.shape
    part = width // n_e
    rows = length // n_t
    q_cols, k_cols = w_query.shape[1], key_projection.shape[1]
    qkv_cols = q_cols + 2 * k_cols
    hidden = w_gate.shape[2]
    wide = own_experts * hidden

    pad = 16
    all_cols = qkv_cols + q_cols
    gain_rows = jnp.pad(jnp.stack([gain_attn, gain_moe]), ((0, pad - 2), (0, all_cols - part)))
    shard = jnp.concatenate([w_query, key_projection, value_projection, w_out.T], axis=1)
    shard = jnp.concatenate([shard, gain_rows]).astype(LOW)

    e_bits, t_bits = bits_of(n_e), bits_of(n_t)
    even_bits, odd_bits = e_bits, e_bits[-1:] + e_bits[:-1]
    orders = order_of(even_bits), order_of(odd_bits)
    by_parity = [(("expert", a), ("expert", b)) for a, b in zip(even_bits, odd_bits)]

    def every(shard, ready, later):
        came, sends = [], []
        for k, (even, odd) in enumerate(by_parity):
            if k == 1:
                shard, *ready = lax.optimization_barrier((shard, *ready))
            if k == 2:
                shard = after(shard, later)
            sends.append(shard)
            came.append(swap_by_parity(shard, even, odd))
            shard = jnp.concatenate([shard, came[-1]])
        return [sends[-1], came[-1]], came, sends, ready

    pairs = n_e // 2
    turn = part % LANES == 0
    pair_experts = 2 * own_experts // replicas or 1
    at_pair = lambda dims: pl.BlockSpec(
        (pair_experts,) + dims, lambda z: (2 * z // max(2, replicas), 0, 0)
    )
    sources = [w_gate, w_up, w_down if turn else w_down.transpose(0, 2, 1)]
    sided = pl.BlockSpec((1, part, 2 * wide), lambda z: (z, 0, 0))
    packed = call(
        functools.partial(pack_body, own_experts, hidden, replicas, turn),
        [shape((pairs, 2, part, wide), LOW)] + [shape((pairs, part, 2 * wide), LOW)] * 2,
        where, *sources,
        grid=(pairs,),
        in_specs=[at_pair(w.shape[1:]) for w in sources],
        out_specs=[pl.BlockSpec((1, 2, part, wide), lambda z: (z, 0, 0, 0))] + [sided] * 2,
    )
    side = e & 1
    lines = [[z * 2 + k for z in range(n_e // 2)] for k in range(2)]

    def along(blocks):
        return lax.all_to_all(
            blocks, "expert", 0, 0, tiled=True, axis_index_groups=lines
        )

    def split_sides(blocks):
        blocks = blocks.reshape(pairs, 2, part, blocks.shape[-1])
        this = lax.dynamic_index_in_dim(blocks, side, 1, keepdims=False)
        return this, lax.dynamic_index_in_dim(blocks, 1 - side, 1, keepdims=False)

    def from_neighbour(blocks, *earlier):
        cols = blocks.shape[-1]
        blocks = along(after(blocks.reshape(pairs, 2 * part, cols), *earlier))
        this, other = split_sides(blocks)
        return this, swap(other, "expert", 1)

    def interleave(this, other):
        cols = this.shape[-1]
        block = pl.BlockSpec((1, part, cols), lambda z: (z, 0, 0))
        return call(
            functools.partial(interleave_body, part),
            [shape((pairs, 2 * part, cols), LOW)],
            where, this, other,
            grid=(pairs,),
            in_specs=[block, block],
            out_specs=[pl.BlockSpec((1, 2 * part, cols), lambda z: (z, 0, 0))],
        )[0]

    def to_neighbour(this, other, *earlier):
        return interleave(this, swap(after(other, *earlier), "expert", 1))

    e_path = [("expert", b) for b in bits_of(n_e, first_bit)]
    t_path = [("tensor", b) for b in t_bits]
    even_path, odd_path = e_path + t_path[:-1], e_path[:-1] + t_path[:-1] + e_path[-1:]
    path = list(zip(even_path, odd_path))
    last = t_path[-1]

    own = t * rows
    grad_rows = lax.dynamic_slice_in_dim(cotangent, own, rows, 0)
    gate_rows = lax.dynamic_slice_in_dim(gates, own, rows, 0)
    route_rows = lax.dynamic_slice_in_dim(routes, own, rows, 0)
    gate_high = gate_rows.astype(LOW)
    gate_rest = (gate_rows - gate_high.astype(FULL)).astype(LOW)
    extra = jnp.concatenate([route_rows.astype(LOW), gate_high, gate_rest], axis=1)
    extra = jnp.pad(extra, ((0, 0), (0, LANES - 3 * TOP)))
    grad_steps = [jnp.concatenate([grad_rows, extra], axis=1)]
    grad_first = swap_by_parity(grad_steps[0], *path[0])
    attn_arrays, attn_came, attn_sends, packed = every(shard, packed, grad_first)
    grad_steps.append(jnp.concatenate([grad_steps[0], grad_first]))
    grad_second = swap_by_parity(after(grad_steps[1], attn_sends[-1]), *path[1])
    grad_steps.append(jnp.concatenate([grad_steps[1], grad_second]))
    down_this, down_other = from_neighbour(packed[0], attn_came[-1])
    near = to_neighbour(*packed[1:], attn_came[-1])
    pitch = part + pad
    gains = jnp.zeros((pad, LANES), FULL)
    if part % LANES:
        held = jnp.concatenate(
            [a.reshape(-1, pitch, all_cols)[:, part:, :part] for a in attn_arrays]
        ).astype(FULL)
        on_even = [position_in(e ^ k, even_bits) for k in range(n_e)]
        on_odd = [position_in(e ^ k, odd_bits) for k in range(n_e)]
        gains = jnp.concatenate(
            [
                lax.dynamic_index_in_dim(held, jnp.where(t & 1 == 0, a, b), 0, keepdims=False)
                for a, b in zip(on_even, on_odd)
            ],
            axis=1,
        )

    def add_halves(kept, got):
        half = got.shape[0] // 2
        return kept[:half] + got[:half].astype(FULL), (
            kept[half:] + got[half:].astype(FULL)
        ).astype(LOW)

    def scatter_stage(kept, sent, k):
        got = swap_by_parity(sent, *path[-1 - k])
        return (kept, got) if k == len(path) - 1 else add_halves(kept, got)

    documents = segments[0]
    doc_row, doc_col = documents[None, :], documents[:, None]
    index = jnp.arange(length)
    same = (index[None, :] < index[:, None]) & (doc_row == doc_col)
    position = jnp.sum(same.astype(FULL), axis=1, keepdims=True)
    lane = jnp.arange(LANES)
    freqs = THETA ** (-2.0 * (lane % (HEAD_SIZE // 2)).astype(FULL) / HEAD_SIZE)
    angle = position * freqs[None, :]
    cosine = jnp.cos(angle)
    sine = jnp.sin(angle) * jnp.where(lane % HEAD_SIZE < HEAD_SIZE // 2, -1.0, 1.0)[None, :]
    t_masks = t_bits[::-1]
    order = order_of(t_bits)
    weights, first_hidden, qkv, mixed, gains, kept, sent = call(
        functools.partial(attend_body, orders, 2, part, pitch, q_cols, k_cols, rows, order),
        [
            shape((width, all_cols), LOW),
            shape((length, width), LOW),
            shape((length, qkv_cols), LOW),
            shape((length, q_cols), LOW),
            shape((pad, width), FULL),
            shape((length // 2, width), FULL),
            shape((length // 2, width), LOW),
        ],
        where, *attn_arrays[:-1], after(attn_arrays[-1], grad_second), tokens, gains, doc_row, doc_col, cosine, sine,
        scratch=[pltpu.VMEM((length, q_cols), LOW)],
        flops=2 * length * (width * qkv_cols + 2 * length * q_cols),
    )
    def all_rows(field):
        size = field.shape[0]
        for b in t_bits:
            field = jnp.concatenate([field, swap(field, "tensor", b)])
        at = [position_in(t ^ k, t_bits) * size for k in range(n_t)]
        return jnp.concatenate([lax.dynamic_slice_in_dim(field, a, size, 0) for a in at])

    def scatter_rows(kept, sent):
        for b in t_masks[:-1]:
            total = kept + swap(sent, "tensor", b).astype(FULL)
            half = total.shape[0] // 2
            kept, sent = total[:half], total[half:].astype(LOW)
        return kept, swap(sent, "tensor", t_masks[-1])

    grad_third = swap_by_parity(grad_steps[-1], *path[2])
    kept, got = scatter_rows(kept, sent)
    middle, second_hidden = call(
        functools.partial(middle_body, rows),
        [shape((rows, width), FULL), shape((rows, width), LOW)],
        where, tokens, kept, after(got, grad_third, down_this), gains,
    )

    hidden_field = second_hidden
    for k, (even, odd) in enumerate(path):
        if k == 1:
            hidden_field = after(hidden_field, near)
        if k == 2:
            hidden_field = after(hidden_field, down_other, grad_got)
        hidden_got = swap_by_parity(hidden_field, even, odd)
        if k == 1:
            gate_up_rows = along(after(near, hidden_got)).reshape(width, 2 * wide)
        hidden_pieces = [hidden_field, hidden_got]
        hidden_field = jnp.concatenate(hidden_pieces)
        if k == 0:
            grad_field, grad_got = grad_steps[-1], grad_third
            for k in range(3, len(path)):
                grad_field = jnp.concatenate([grad_field, grad_got])
                grad_got = swap_by_parity(grad_field, *path[k])
            grad_pieces = [grad_field, grad_got]
    hidden_pieces = hidden_pieces + [swap(p, *last) for p in hidden_pieces]
    grad_pieces = grad_pieces + [swap(p, *last) for p in grad_pieces]
    size = 512
    total_rows = sum(p.shape[0] for p in grad_pieces)
    steps = total_rows // size
    whole = lambda a: pl.BlockSpec(a.shape, lambda i: (0,) * a.ndim)
    tile = lambda cols: pl.BlockSpec((size, cols), lambda i: (i, 0))

    def tiles_of(pieces):
        count = pieces[0].shape[0] // size
        return count, [
            pl.BlockSpec((size, p.shape[1]), lambda i, k=k: (jnp.clip(i - k * count, 0, count - 1), 0))
            for k, p in enumerate(pieces)
        ]

    tiles, specs = tiles_of(grad_pieces)
    gate_table, back, down_rows = call(
        functools.partial(owner_body, len(grad_pieces), tiles, part, own_experts, hidden, replicas),
        [
            shape((total_rows, LANES), FULL),
            shape((total_rows, wide), FULL),
            shape((width, wide), LOW),
        ],
        where, *grad_pieces, down_this, down_other,
        grid=(steps,),
        in_specs=specs + [whole(down_this), whole(down_other)],
        out_specs=[tile(LANES), tile(wide), pl.BlockSpec((width, wide), lambda i: (0, 0))],
        scratch=[pltpu.VMEM((size, width + LANES), LOW)],
        flops=2 * total_rows * width * wide,
        limit=LARGE,
    )
    half = steps // 2

    def experts(chosen, first, out_type):
        later = lambda cols: pl.BlockSpec((size, cols), lambda i: (i + first, 0))
        tiles, specs = tiles_of(chosen)
        return call(
            functools.partial(expert_body, len(chosen), tiles, own_experts, hidden),
            [
                shape((half * size, width), out_type),
                shape((half * size, wide), LOW),
                shape((half * size, 2 * wide), LOW),
            ],
            where, *chosen, gate_up_rows, gate_table, back,
            grid=(half,),
            in_specs=specs
            + [whole(gate_up_rows), later(LANES), later(wide)],
            out_specs=[tile(width), tile(wide), tile(2 * wide)],
            scratch=[pltpu.VMEM((size, width), LOW)],
            flops=2 * half * size * width * 4 * wide,
            limit=LARGE,
        )

    sent_hidden, sent_active, sent_both = experts(hidden_pieces[2:], half, LOW)
    kept_hidden, kept_active, kept_both = experts(hidden_pieces[:2], 0, FULL)

    block = 256
    column = lambda a: pl.BlockSpec((a.shape[0], block), lambda i: (0, i))

    def weight_grad(sources, kept, sent, sided):
        cols = kept.shape[1]
        dims = [(part, cols)] * 2 if sided else [(2, part, cols)]
        count = block // (2 * part)
        return call(
            functools.partial(weight_grad_body, len(sources), part),
            [shape((pairs,) + d, LOW) for d in dims],
            where, *sources, kept, sent,
            grid=(width // block,),
            in_specs=[column(a) for a in sources] + [whole(kept), whole(sent)],
            out_specs=[pl.BlockSpec((count,) + d, lambda i, n=len(d): (i,) + (0,) * n) for d in dims],
            scratch=[pltpu.VMEM((total_rows, block), LOW), pltpu.VMEM((block, cols), LOW)],
            flops=2 * total_rows * width * cols,
        )

    hidden_kept, hidden_sent = add_halves(kept_hidden, swap(sent_hidden, *last))
    def down(active, out_type):
        return call(
            out_body,
            [shape((half * size, width), out_type)],
            where, active, down_rows,
            grid=(half,),
            in_specs=[tile(wide), whole(down_rows)],
            out_specs=[tile(width)],
            flops=2 * half * size * width * wide,
        )[0]

    steps_back = len(path)
    kept, sent = scatter_stage(hidden_kept, hidden_sent, 0)
    (down_grad,) = weight_grad(grad_pieces, kept_active, after(sent_active, hidden_sent), False)
    sent_out = down(after(sent_active, down_grad), LOW)
    kept_out = down(after(kept_active, down_grad), FULL)
    kept, sent = scatter_stage(kept, after(sent, down_grad), 1)
    out_kept, out_sent = add_halves(kept_out, swap(sent_out, *last))
    both_this, both_other = weight_grad(hidden_pieces, kept_both, after(sent_both, sent_out), True)
    grad_near = to_neighbour(both_this, both_other)
    down_line = along(down_grad.reshape(pairs, 2 * part, wide))
    sent = after(sent, down_line)
    for k in range(2, steps_back - 1):
        kept, sent = scatter_stage(kept, sent, k)
    grad_kept, grad_got = scatter_stage(kept, after(sent, out_sent), steps_back - 1)
    out_kept, out_sent = scatter_stage(out_kept, out_sent, 0)
    out_first = out_sent
    out_kept, out_sent = scatter_stage(out_kept, out_sent, 1)
    out_second = out_sent
    both_back = along(after(grad_near, grad_got)).reshape(width, 2 * wide)

    grad_middle, branch_grad, moe_part = call(
        middle_back_body,
        [shape((rows, width), FULL), shape((rows, width), LOW), shape((16, width), FULL)],
        where, grad_kept, grad_got, middle, grad_rows, gains,
    )
    branch_pieces = [branch_grad]
    for b in reversed(t_masks):
        branch_pieces = branch_pieces + [swap(p, "tensor", b) for p in branch_pieces]
    sum_orders = orders[0], orders[0]
    kept_w, sent_w, first_kept, first_sent = call(
        functools.partial(
            attend_back_body, len(branch_pieces), q_cols, k_cols, rows, part, order, sum_orders
        ),
        [
            shape((width // 2, all_cols), FULL),
            shape((width // 2, all_cols), LOW),
            shape((length // 2, width), FULL),
            shape((length // 2, width), LOW),
        ],
        where, *branch_pieces[:-1], after(branch_pieces[-1], out_first), mixed, qkv, doc_row, doc_col, cosine, sine,
        first_hidden, weights,
        scratch=[
            pltpu.VMEM((length, width), LOW),
            pltpu.VMEM((length, max(q_cols, qkv_cols)), LOW),
            pltpu.VMEM((length, qkv_cols), LOW),
            pltpu.VMEM((width, all_cols), FULL),
        ],
        flops=2 * length * width * (2 * q_cols + 2 * qkv_cols),
    )
    got_w = swap(sent_w, "expert", e_bits[-1])
    attn_grad = kept_w + got_w.astype(FULL)
    kept, got = scatter_rows(first_kept, first_sent)
    (token_rows,) = call(
        functools.partial(tokens_back_body, rows),
        [shape((rows + 16, width), FULL)],
        where, tokens, kept, after(got, got_w, out_second), gains, grad_middle, moe_part,
    )
    gathered = all_rows(token_rows.astype(LOW))
    gathered = gathered.reshape(n_t, rows + 16, width).astype(FULL)
    grad_input = gathered[:, :rows].reshape(length, width)
    gain_sum = jnp.sum(gathered[:, rows : rows + 2], axis=0)

    blocks = gain_sum.reshape(2, n_e, part).transpose(1, 0, 2)

    half_rows = attn_grad.shape[0] // 2
    kept_w, sent_w = attn_grad[:half_rows], attn_grad[half_rows:].astype(LOW)
    blocks = after(blocks, sent_w)
    gain_grads = jnp.sum(lax.all_to_all(blocks, "expert", 0, 0, tiled=True), axis=0)
    out_sent = after(out_sent, both_back)
    for k, b in enumerate(reversed(e_bits[:-1])):
        attn_grad = kept_w + swap(sent_w, "expert", b).astype(FULL)
        half_rows = attn_grad.shape[0] // 2
        kept_w, sent_w = attn_grad[:half_rows], attn_grad[half_rows:].astype(LOW)
        if k == 0:
            out_kept, out_sent = scatter_stage(out_kept, out_sent, 2)
            out_sent = after(out_sent, sent_w)
    for k in range(3, steps_back):
        out_kept, out_sent = scatter_stage(out_kept, out_sent, k)
    output_rows = (middle + (out_kept + out_sent.astype(FULL))).astype(LOW)
    output = all_rows(output_rows)

    out_dims = [(part, hidden), (part, hidden), (hidden, part) if turn else (part, hidden)]

    def unpack(source, dims, turned):
        cols = source.shape[1]
        return call(
            functools.partial(unpack_body, own_experts, hidden, replicas, turned),
            [shape((EXPERTS,) + dims, FULL)] * (cols // wide),
            where, source,
            grid=(pairs,),
            in_specs=[pl.BlockSpec((2 * part, cols), lambda z: (z, 0))],
            out_specs=[at_pair(dims)] * (cols // wide),
        )

    sides_of = lambda this, other: jnp.where(
        side == 0, jnp.stack([this, other], axis=1), jnp.stack([other, this], axis=1)
    )
    down_this, down_other = split_sides(after(down_line, got_w))
    down_back = sides_of(down_this, swap(down_other, "expert", 1)).reshape(width, wide)
    shards = unpack(both_back, out_dims[0], False) + unpack(down_back, out_dims[2], turn)
    gate_shard, up_shard, down_shard = shards
    if not turn:
        down_shard = down_shard.transpose(0, 2, 1)

    return (
        output,
        grad_input,
        attn_grad[:, :q_cols],
        attn_grad[:, q_cols : q_cols + k_cols],
        attn_grad[:, q_cols + k_cols : qkv_cols],
        attn_grad[:, qkv_cols:].T,
        gain_grads[0],
        gain_grads[1],
        gate_shard,
        up_shard,
        down_shard,
    )


def solution(mesh):
    by_rows = P("expert", None)
    by_both = P("expert", "tensor")
    in_experts = P(None, "expert", "tensor")
    down_specs = P(None, "tensor", "expert")
    return jax.shard_map(
        local,
        mesh=mesh,
        in_specs=(by_rows,) * 5
        + (by_both,) * 3
        + (P("tensor", "expert"), P("expert"), P("expert"), in_experts, in_experts, down_specs),
        out_specs=(by_rows, by_rows)
        + (by_both,) * 3
        + (P("tensor", "expert"), P("expert"), P("expert"), in_experts, in_experts, down_specs),
        check_vma=False,
    )
```
